32 devices in a mesh: rep: 2 (over core), shard: 16 (over z, y, x).
Axes of the slice: x: 2, y: 2, z: 4, core: 2. Of those that a mesh axis runs over, the one named last changes fastest.
Arguments:
- tokens: bfloat16 [16384, 768], P(('rep', 'shard')), may hold values from -6 to 6
- lengths: int32 [32], P(('rep', 'shard')), may hold values from 128 to 512, as said below
- routes: int32 [16384, 2], P(('rep', 'shard')), may hold values from 0 to 15, as said below
- slots: int32 [16384, 2], P(('rep', 'shard')), may hold values from 0 to 64, as said below
- norm_one: bfloat16 [768], P('shard'), may hold values from 0.5 to 1.5
- w_query: bfloat16 [768, 768], P('shard'), may hold values from -0.21875 to 0.21875
- w_key: bfloat16 [768, 768], P('shard'), may hold values from -0.21875 to 0.21875
- w_value: bfloat16 [768, 768], P('shard'), may hold values from -0.21875 to 0.21875
- w_output: bfloat16 [768, 768], P('shard'), may hold values from -1.75 to 1.75
- bias_table: bfloat16 [32, 12], P('shard'), may hold values from -3 to 3
- norm_two: bfloat16 [768], P('shard'), may hold values from 0.5 to 1.5
- router: bfloat16 [768, 16], P('shard'), may hold values from -0.15625 to 0.15625
- expert_in: bfloat16 [16, 768, 3072], P('shard'), may hold values from -0.21875 to 0.21875
- expert_out: bfloat16 [16, 768, 3072], P('shard'), may hold values from -0.21875 to 0.21875
- cotangent: bfloat16 [16384, 768], P(('rep', 'shard')), may hold values from -6 to 6
Outputs:
- output: bfloat16 [16384, 768], P(('rep', 'shard'))
- grad_tokens: float32 [16384, 768], P(('rep', 'shard'))
- grad_norm_one: float32 [768], P('shard')
- grad_w_query: float32 [768, 768], P('shard')
- grad_w_key: float32 [768, 768], P('shard')
- grad_w_value: float32 [768, 768], P('shard')
- grad_w_output: float32 [768, 768], P('shard')
- grad_bias_table: float32 [32, 12], P('shard')
- grad_norm_two: float32 [768], P('shard')
- grad_router: float32 [768, 16], P('shard')
- grad_expert_in: float32 [16, 768, 3072], P('shard', None, 'rep')
- grad_expert_out: float32 [16, 768, 3072], P('shard', None, 'rep')
The draws below stay inside these ranges and needn't reach their ends.
Inputs may be any that keep to these rules, and one draw needn't show every extreme that they name: `lengths`: one sequence has length 512 and one has 128. `routes`: the two experts of a token differ. For each sequence and expert, the choices of valid tokens that name the expert, in order of token and then choice, hold slots 0, 1, 2, and so on; a slot of 64 marks a dropped choice: every choice of a token past its sequence's length, and choices past the capacity.
All inputs are finite; a program needn't handle non-finite values.
Results may differ from the reference program's by a relative error of at most 0.023.
Values may be sent and summed in bfloat16 or wider, within the bound.
A program may use at most 192 MiB of HBM per device.

```python
import jax
import jax.numpy as jnp
from jax import lax

D = 768
HEADS = 12
HEAD_DIM = 64
FF = 3072
BUCKETS = 32
SEQ = 512
SEQS = 32
TOKENS = 16384
EXPERTS = 16
CAP = 64


def routing_draw(key):
    length_key, marked_key, first_key, label_key, second_key = jax.random.split(key, 5)
    seq_lengths = jax.random.randint(length_key, (SEQS,), SEQ // 4, SEQ + 1, dtype=jnp.int32)
    marked = jax.random.permutation(marked_key, SEQS)
    seq_lengths = seq_lengths.at[marked[0]].set(SEQ).at[marked[1]].set(SEQ // 4)
    favored = jnp.min(jax.random.randint(first_key, (3, TOKENS), 0, EXPERTS, dtype=jnp.int32), axis=0)
    labels = jax.random.permutation(label_key, EXPERTS).astype(jnp.int32)
    first_pick = labels[favored]
    second = (first_pick + 1 + jax.random.randint(second_key, (TOKENS,), 0, EXPERTS - 1, dtype=jnp.int32)) % EXPERTS
    route_pairs = jnp.stack([first_pick, second], axis=1).astype(jnp.int32)
    live_mask = jnp.arange(SEQ, dtype=jnp.int32)[None, :] < seq_lengths[:, None]
    live_mask = jnp.repeat(live_mask, 2, axis=1)
    pick_rows = route_pairs.reshape(SEQS, 2 * SEQ)
    onehot = ((pick_rows[:, :, None] == jnp.arange(EXPERTS, dtype=jnp.int32)[None, None, :]) & live_mask[:, :, None]).astype(jnp.int32)
    earlier = jnp.cumsum(onehot, axis=1) - onehot
    rank_in = jnp.sum(earlier * onehot, axis=2)
    slot_ids = jnp.where(live_mask, jnp.minimum(rank_in, CAP), CAP).reshape(TOKENS, 2).astype(jnp.int32)
    return (seq_lengths.astype(jnp.int32), route_pairs, slot_ids)


def draw_lengths(key, part):
    return routing_draw(key)[0]


def draw_routes(key, part):
    return routing_draw(key)[1]


def draw_slots(key, part):
    return routing_draw(key)[2]


def block_scale(stream_key, dims, shards, least, largest):
    loudness, own = 1.0, jax.random.fold_in(stream_key, 6)
    for position, parts in shards:
        steps = jnp.exp(jax.random.uniform(jax.random.fold_in(own, position), (parts,), jnp.float32, least / len(shards), largest / len(shards)))
        loudness = loudness * jnp.repeat(steps, dims[position] // parts).reshape([-1 if axis == position else 1 for axis in range(len(dims))])
    return loudness


def scatter_about(rng, shape, deviation, bound, cuts=(), kind=jnp.bfloat16):
    values = jax.random.normal(rng, shape, jnp.float32) * deviation
    if len(cuts) > 0:
        values = block_scale(rng, shape, cuts, -0.22, 0.18) * values
    return jnp.clip(values, min=-bound, max=bound).astype(kind)


def setup_inputs(seed: int = 0) -> dict:
    key_list = jax.random.split(jax.random.key(seed), 16)
    tokens = scatter_about(key_list[0], (TOKENS, D), 1.0, 6.0, ((0, 32),))
    lengths = draw_lengths(jax.random.fold_in(key_list[15], 71), 0)
    routes = draw_routes(jax.random.fold_in(key_list[15], 71), 0)
    slots = draw_slots(jax.random.fold_in(key_list[15], 71), 0)
    norm_one = jnp.clip(1.0 + 0.1 * jax.random.normal(key_list[4], (D,), jnp.float32), 0.5, 1.5).astype(jnp.bfloat16)
    w_query = scatter_about(key_list[5], (D, D), D ** -0.5, 0.21875, ((0, 16),))
    w_key = scatter_about(key_list[6], (D, D), D ** -0.5, 0.21875, ((0, 16),))
    w_value = scatter_about(key_list[7], (D, D), D ** -0.5, 0.21875, ((0, 16),))
    w_output = scatter_about(key_list[8], (D, D), (D // 64) ** -0.5, 1.75, ((0, 16),))
    bias_table = scatter_about(key_list[9], (BUCKETS, HEADS), 0.5, 3.0, ((0, 16),))
    norm_two = jnp.clip(1.0 + 0.1 * jax.random.normal(key_list[10], (D,), jnp.float32), 0.5, 1.5).astype(jnp.bfloat16)
    router = scatter_about(key_list[11], (D, EXPERTS), (2 * D) ** -0.5, 0.15625, ((0, 16),))
    expert_in = scatter_about(key_list[12], (EXPERTS, D, FF), D ** -0.5, 0.21875, ((0, 16),))
    expert_out = scatter_about(key_list[13], (EXPERTS, D, FF), (FF // 4) ** -0.5, 0.21875, ((0, 16),))
    cotangent = scatter_about(key_list[14], (TOKENS, D), 1.0, 6.0, ((0, 32),))
    return {"tokens": tokens, "lengths": lengths, "routes": routes, "slots": slots, "norm_one": norm_one, "w_query": w_query, "w_key": w_key, "w_value": w_value, "w_output": w_output, "bias_table": bias_table, "norm_two": norm_two, "router": router, "expert_in": expert_in, "expert_out": expert_out, "cotangent": cotangent}


@jax.custom_vjp
def low(v):
    return lax.optimization_barrier(v.astype(jnp.bfloat16)).astype(jnp.float32)

@jax.custom_vjp
def low_back(v):
    return v

def low_keep(v):
    return (low(v), None)

def low_pass(kept, grad):
    return (grad,)

def back_keep(v):
    return (v, None)

def back_low(kept, grad):
    return (low(grad),)
low.defvjp(low_keep, low_pass)
low_back.defvjp(back_keep, back_low)
norm_eps = 1e-06
score_scale = 0.125
cutoffs = (19, 21, 24, 27, 31, 35, 40, 46, 52, 59, 67, 77, 87, 99, 113)
highest = lax.Precision.HIGHEST

def matmul(left, right):
    return jnp.dot(left, right, precision=highest)

def rms_scale(values, gain_vec):
    return values * lax.rsqrt(lax.optimization_barrier(jnp.mean(values * values, axis=-1, keepdims=True)) + norm_eps) * gain_vec

def bucket_onehot():
    positions = jnp.arange(SEQ, dtype=jnp.int32)
    distance = jnp.maximum(positions[:, None] - positions[None, :], 0)
    far_count = jnp.zeros_like(distance)
    for cutoff in cutoffs:
        far_count = far_count + (distance >= cutoff).astype(jnp.int32)
    bucket = jnp.where(distance < 16, distance, 16 + far_count)
    return (bucket[:, :, None] == jnp.arange(BUCKETS, dtype=jnp.int32)[None, None, :]).astype(jnp.float32)

def gate_weights(logits, chosen, kept_mask):
    peak_logit = lax.optimization_barrier(jnp.max(logits, axis=-1, keepdims=True))
    raised = jnp.exp(logits - peak_logit)
    soft_probs = raised / lax.optimization_barrier(jnp.sum(raised, axis=-1, keepdims=True))
    picked = lax.optimization_barrier(jnp.sum(chosen * soft_probs[:, None, :], axis=-1))
    return picked / lax.optimization_barrier(jnp.sum(picked, axis=-1, keepdims=True)) * kept_mask

def expert_block(pieces):
    block_rows, weight_in, weight_out = pieces
    pre_act = low_back(matmul(block_rows, weight_in))
    hidden = low(jax.nn.gelu(pre_act, approximate=False))
    return low(low_back(matmul(hidden, weight_out.T)))

def reference(tokens, lengths, routes, slots, norm_one, w_query, w_key, w_value, w_output, bias_table, norm_two, router, expert_in, expert_out, cotangent):
    positions = jnp.arange(SEQ, dtype=jnp.int32)
    valid = (positions[None, :] < lengths[:, None]).astype(jnp.float32).reshape(TOKENS, 1)
    onehot = bucket_onehot()
    causal = positions[:, None] >= positions[None, :]
    device_ids = jnp.arange(TOKENS, dtype=jnp.int32) // SEQ
    row_total = EXPERTS * SEQS * CAP
    target = jnp.where(slots < CAP, routes * (SEQS * CAP) + device_ids[:, None] * CAP + slots, row_total).astype(jnp.int32)
    chosen = (routes[:, :, None] == jnp.arange(EXPERTS, dtype=jnp.int32)[None, None, :]).astype(jnp.float32)
    kept_mask = (slots < CAP).astype(jnp.float32)

    def forward(inputs, gain_one, query_w, key_w, value_w, output_w, table, gain_two, router_w, in_w, out_w):
        normed_one = low(rms_scale(inputs, gain_one))
        queries = low(low_back(matmul(normed_one, query_w)))
        key_proj = low(low_back(matmul(normed_one, key_w)))
        value_proj = low(low_back(matmul(normed_one, value_w)))
        pos_bias = jnp.einsum('qkb,bh->hqk', onehot, table, precision=highest)

        def attend(pieces):
            query_seq, key_seq, value_seq, length = pieces
            query_heads = query_seq.reshape(SEQ, HEADS, HEAD_DIM)
            key_heads = key_seq.reshape(SEQ, HEADS, HEAD_DIM)
            value_heads = value_seq.reshape(SEQ, HEADS, HEAD_DIM)
            raw_scores = low_back(jnp.einsum('qhd,khd->hqk', query_heads, key_heads, precision=highest))
            allowed = causal & (positions[None, :] < length)
            scores = jnp.where(allowed[None], raw_scores * score_scale + pos_bias, -1e+30)
            peak_score = lax.optimization_barrier(jnp.max(scores, axis=-1, keepdims=True))
            raised = jnp.exp(scores - peak_score)
            soft_probs = low(raised / lax.optimization_barrier(jnp.sum(raised, axis=-1, keepdims=True)))
            mixed_heads = jnp.einsum('hqk,khd->qhd', soft_probs, value_heads, precision=highest)
            return low(low_back(mixed_heads.reshape(SEQ, D)))
        attended = lax.map(jax.checkpoint(attend), (queries.reshape(SEQS, SEQ, D), key_proj.reshape(SEQS, SEQ, D), value_proj.reshape(SEQS, SEQ, D), lengths)).reshape(TOKENS, D)
        resid = inputs + low_back(matmul(attended, output_w))
        normed_two = low(rms_scale(resid, gain_two))
        logits = low_back(matmul(normed_two, router_w))
        combine = gate_weights(logits, chosen, kept_mask)
        buffer_rows = jnp.zeros((row_total, D), jnp.float32).at[target.reshape(-1)].set(jnp.repeat(normed_two, 2, axis=0), mode='drop')
        buffer_rows = low_back(buffer_rows)
        results = lax.map(jax.checkpoint(expert_block), (buffer_rows.reshape(EXPERTS, SEQS * CAP, D), in_w, out_w)).reshape(row_total, D)
        padded = jnp.concatenate([results, jnp.zeros((1, D), jnp.float32)], axis=0)
        picked_rows = padded[target]
        return (resid + lax.optimization_barrier(jnp.sum(combine[:, :, None] * picked_rows, axis=1))) * valid
    floats = tuple((item.astype(jnp.float32) for item in (tokens, norm_one, w_query, w_key, w_value, w_output, bias_table, norm_two, router, expert_in, expert_out)))
    layer_out, pull_back = jax.vjp(forward, *floats)
    grads = pull_back(cotangent.astype(jnp.float32))
    return (layer_out.astype(jnp.bfloat16), grads[0], grads[1], grads[2], grads[3], grads[4], grads[5], grads[6], grads[7], grads[8], grads[9], grads[10])
```

```python
import functools

import jax
import jax.numpy as jnp
from jax import lax
from jax.experimental import pallas as pl
from jax.experimental.pallas import tpu as pltpu
from jax.sharding import PartitionSpec as P

MESH = pl.DeviceIdType.MESH
norm_eps = 1e-06
score_scale = 0.125
cutoffs = (19, 21, 24, 27, 31, 35, 40, 46, 52, 59, 67, 77, 87, 99, 113)
f32 = jnp.float32
bf16 = jnp.bfloat16
GAIN_ONE, GAIN_TWO, TABLE = 64, 65, 80
BLK = 128
VMEM_LIMIT = 60 * 2**20
NEG = -1e30


def dot_nn(a, b):
    return lax.dot_general(a, b, (((1,), (0,)), ((), ())), preferred_element_type=f32)


def dot_nt(a, b):
    return lax.dot_general(a, b, (((1,), (1,)), ((), ())), preferred_element_type=f32)


def dot_tn(a, b):
    return lax.dot_general(a, b, (((0,), (0,)), ((), ())), preferred_element_type=f32)


def iota(shape, dim):
    return lax.broadcasted_iota(jnp.int32, shape, dim)


class Sizes:
    def __init__(self, reps, group, seq, width, heads, experts, ff, rows, buckets):
        self.reps, self.group, self.seq, self.width = reps, group, seq, width
        self.heads, self.experts, self.ff, self.rows = heads, experts, ff, rows
        self.buckets = buckets
        self.cap = 2 * seq // experts
        self.slots = experts * self.cap
        self.line = group // 4
        self.half = width // 2
        self.small = -(-rows // 16) * 16
        self.share = self.small // 16
        self.piece = 4 * rows + 16
        self.pairs = heads // 2
        split = 16 + 3 * rows
        self.chunks = ((0, self.piece),) if split % 16 else ((0, split), (split, self.piece))

    def relative(self, half, place):
        first, second = (1, 2) if half == 0 else (2, 1)
        line = place % self.line
        return line * 4 + (place // self.line % 2) * first + (place // (2 * self.line)) * second


def peers(sz):
    rep = lax.axis_index("rep")
    me = lax.axis_index("shard")
    return rep, me, lax.rem(rep, 2), rep + 1 - 2 * lax.rem(rep, 2)


def xor(a, b):
    return jnp.bitwise_xor(a, b)


def greet(sz, rep, me, sibling):
    barrier = pltpu.get_barrier_semaphore()

    def signal(k, carry):
        pl.semaphore_signal(barrier, inc=1, device_id=(rep, xor(me, k)), device_id_type=MESH)
        return carry

    lax.fori_loop(1, sz.group, signal, 0)
    pl.semaphore_signal(barrier, inc=1, device_id=(sibling, me), device_id_type=MESH)
    pl.semaphore_wait(barrier, sz.group)


def remote(src, dst, send, recv, device):
    return pltpu.make_async_remote_copy(
        src_ref=src, dst_ref=dst, send_sem=send, recv_sem=recv, device_id=device, device_id_type=MESH
    )


def send_order(group):
    order = list(range(group // 2, group)) + list(range(1, group // 2))
    return order


def row_block(index, size):
    return pl.ds(pl.multiple_of(index * size, size), size)


def target_slots(sz, routes, slots):
    return jnp.where(slots < sz.cap, routes * sz.cap + slots, -1)


def bias_tiles(sz, small_t, vector, tiles):
    lane = iota((1, 3 * BLK), 1)
    distance = jnp.where(lane <= BLK, BLK - lane, 4 * BLK - lane)
    bucket = jnp.where(distance < 16, distance, 16)
    for cutoff in cutoffs:
        bucket = bucket + (distance >= cutoff).astype(jnp.int32)
    per = sz.buckets // sz.group
    shape = (sz.group, sz.rows, 3 * BLK)
    inner = iota(shape, 1)
    named = jnp.where(inner < per, iota(shape, 0) * per + inner, -1)
    onehot = (named == bucket[None]).astype(f32).reshape(sz.width, 3 * BLK).astype(bf16)
    table = small_t[TABLE : TABLE + 16].astype(bf16)
    values = dot_nn(table, onehot)
    values = values - values[:, 0:1]
    vector[...] = jnp.where((lane > BLK) & (lane < 2 * BLK), NEG, values)

    def tile(h, carry):
        row = jnp.broadcast_to(vector[pl.ds(h, 1), :], (BLK, 3 * BLK))
        tiles[h] = pltpu.roll(row, 0, 1, stride=1, stride_axis=0)[:, : 2 * BLK]
        return carry

    lax.fori_loop(0, sz.heads, tile, 0)


def forward_kernel(
    sz,
    len_ref,
    tok_ref,
    routes_ref,
    slots_ref,
    small_ref,
    wq_ref,
    wk_ref,
    wv_ref,
    wo_ref,
    cot_ref,
    w_out,
    qkv_out,
    probs_out,
    att_out,
    resid_out,
    n2_out,
    rows_out,
    cs_out,
    garr_out,
    gate_out,
    small_out,
    pick_out,
    pieces,
    gsend,
    vector,
    tiles,
    probs,
    wide,
    send_z,
    recv_z,
    send_b,
    recv_b,
    send_c,
    recv_c,
    send_s,
    recv_s,
    send_g,
    recv_g,
    send_p,
):
    rep, me, core, sibling = peers(sz)
    seq, width, half, line = sz.seq, sz.width, sz.half, sz.line
    place_a = me // 4
    near = jnp.where(core == 0, 1, 2)
    last = jnp.where(core == 0, 2, 1)

    small_in = small_ref[...]
    for h in range(2):
        cols = slice(h * half, (h + 1) * half)
        for i in range(sz.share):
            pieces[h, 0, 0:16, i * BLK : (i + 1) * BLK] = small_in[16 * i : 16 * (i + 1)]
        if sz.rows % 16 == 0:
            for m, ref in enumerate((wq_ref, wk_ref, wv_ref, wo_ref)):
                pieces[h, 0, 16 + m * sz.rows : 16 + (m + 1) * sz.rows, :] = ref[:, cols]
        else:
            stacked = [ref[:, cols].astype(f32) for ref in (wq_ref, wk_ref, wv_ref, wo_ref)]
            pieces[h, 0, 16 : sz.piece, :] = jnp.concatenate(stacked, axis=0).astype(bf16)

    greet(sz, rep, me, sibling)

    chunks = sz.chunks

    def block(ch, slot):
        lo, hi = chunks[ch]
        return pieces.at[core, slot, pl.ds(lo, hi - lo)]

    def copy_z(ch, up, source, to):
        slot = xor(source, to)
        return remote(
            block(ch, xor(source, place_a)),
            block(ch, slot),
            send_z.at[ch, up, xor(source, place_a)],
            recv_z.at[ch, slot],
            (rep, me + (to - place_a) * 4),
        )

    def copy_b(ch, i):
        return remote(
            block(ch, i),
            block(ch, line + i),
            send_b.at[ch, i],
            recv_b.at[ch, i],
            (rep, xor(me, near)),
        )

    def copy_c(ch, i):
        return remote(
            block(ch, i),
            block(ch, 2 * line + i),
            send_c.at[ch, i],
            recv_c.at[ch, i],
            (rep, xor(me, last)),
        )

    def copy_s(ch, i):
        return remote(
            block(ch, i), block(ch, i), send_s.at[ch, i], recv_s.at[ch, i], (sibling, me)
        )

    def forward_z(ch, t):
        for up, step in ((1, 1), (0, -1)):
            source = place_a - step * t
            to = place_a + step
            there = (source >= 0) & (source < line)
            onward = there & (to >= 0) & (to < line)

            @pl.when(there)
            def _(up=up, source=source, to=to, onward=onward):
                slot = xor(source, place_a)
                if t > 0:
                    remote(
                        block(ch, slot), block(ch, slot), send_z.at[ch, up, slot],
                        recv_z.at[ch, slot], (rep, me),
                    ).wait_recv()

                @pl.when(onward)
                def _():
                    copy_z(ch, up, source, to).start()

                if t > 0:
                    copy_b(ch, slot).start()
                    copy_c(ch, slot).start()
                    copy_s(ch, slot).start()

    def wait_sent_z(ch):
        for t in range(line - 1):
            for up, step in ((1, 1), (0, -1)):
                source = place_a - step * t
                to = place_a + step
                onward = (source >= 0) & (source < line) & (to >= 0) & (to < line)

                @pl.when(onward)
                def _(up=up, source=source, to=to):
                    copy_z(ch, up, source, to).wait_send()

    def start_own(ch):
        forward_z(ch, 0)
        copy_b(ch, 0).start()
        copy_c(ch, 0).start()

    def gather(ch):
        def from_b(i, carry):
            copy_b(ch, i).wait_recv()
            copy_c(ch, line + i).start()
            copy_s(ch, line + i).start()
            return carry

        def from_c(i, carry):
            copy_c(ch, i).wait_recv()
            copy_s(ch, 2 * line + i).start()
            return carry

        from_b(0, 0)
        for t in range(1, line):
            forward_z(ch, t)
        lax.fori_loop(1, line, from_b, 0)
        lax.fori_loop(0, 2 * line, from_c, 0)

    def finish(ch):
        def sent_b(i, carry):
            copy_b(ch, i).wait_send()
            return carry

        def sent_c(i, carry):
            copy_c(ch, i).wait_send()
            return carry

        def sent_s(i, carry):
            copy_s(ch, i).wait_send()
            return carry

        wait_sent_z(ch)
        lax.fori_loop(0, line, sent_b, 0)
        lax.fori_loop(0, 2 * line, sent_c, 0)
        lax.fori_loop(1, sz.group, sent_s, 0)

    def from_sibling(ch):
        def wait(i, carry):
            lo, hi = chunks[ch]
            other = pieces.at[1 - core, i, pl.ds(lo, hi - lo)]
            remote(other, other, send_s.at[ch, i], recv_s.at[ch, i], (sibling, me)).wait_recv()
            return carry

        lax.fori_loop(1, sz.group, wait, 0)

    for ch in range(len(chunks)):
        start_own(ch)

    target = target_slots(sz, routes_ref[...], slots_ref[...])
    first, second = target[:, 0:1], target[:, 1:2]
    wide_lane = iota((1, 256), 1)
    for j in range(sz.slots // 256):
        lane = wide_lane + j * 256
        pick = ((first == lane) | (second == lane)).astype(f32).astype(bf16)
        pick_out[:, j * 256 : (j + 1) * 256] = pick
        gsend[j * 256 : (j + 1) * 256, :] = dot_tn(pick, cot_ref[...]).astype(bf16)

    def copy_g(k):
        to = xor(me, k)
        return remote(
            gsend.at[row_block(to, sz.cap)],
            garr_out.at[row_block(k, sz.cap)],
            send_g.at[k],
            recv_g.at[k],
            (rep, to),
        )

    def start_g(k, carry):
        copy_g(k).start()
        return carry

    lax.fori_loop(sz.group // 2, sz.group, start_g, 0)
    garr_out[0 : sz.cap, :] = gsend[row_block(me, sz.cap), :]

    for ch in range(len(chunks)):
        gather(ch)
    lax.fori_loop(1, sz.group // 2, start_g, 0)
    for ch in range(len(chunks)):
        from_sibling(ch)

    for place in range(sz.group):
        for h in range(2):
            source = xor(me, sz.relative(h, place))
            cols = slice(h * half, (h + 1) * half)
            if sz.rows % 16 == 0:
                for m in range(4):
                    w_out[m, row_block(source, sz.rows), cols] = pieces[
                        h, place, 16 + m * sz.rows : 16 + (m + 1) * sz.rows, :
                    ]
            else:
                tall = pieces[h, place, :, :].astype(f32)
                for m in range(4):
                    wide[m, row_block(source, sz.rows), cols] = tall[
                        16 + m * sz.rows : 16 + (m + 1) * sz.rows
                    ]
        source = xor(me, sz.relative(0, place))
        for i in range(sz.share):
            small_out[pl.ds(pl.multiple_of(source * sz.small, 16) + 16 * i, 16), :] = pieces[
                0, place, 0:16, i * BLK : (i + 1) * BLK
            ]
    if sz.rows % 16 != 0:
        for m in range(4):
            w_out[m] = wide[m].astype(bf16)

    small = small_out[...].astype(f32).reshape(sz.group, sz.small, BLK)[:, : sz.rows]
    small = small.reshape(width, BLK)
    small_t = small.T
    gain_one = small_t[GAIN_ONE : GAIN_ONE + 1]
    gain_two = small_t[GAIN_TWO : GAIN_TWO + 1]
    bias_tiles(sz, small_t, vector, tiles)

    for i in range(seq // BLK):
        rows = slice(i * BLK, (i + 1) * BLK)
        x = tok_ref[rows, :].astype(f32)
        scale = lax.rsqrt(jnp.mean(x * x, axis=-1, keepdims=True) + norm_eps)
        n2_out[rows, :] = (x * scale * gain_one).astype(bf16)
    for m in range(3):
        qkv_out[m] = dot_nn(n2_out[...], w_out[m]).astype(bf16)

    length = len_ref[0]
    key_mask = jnp.where(iota((1, seq), 1) < length, 0.0, NEG)
    low = iota((1, BLK), 1) < width // sz.heads
    halves = [jnp.where(low, 1.0, 0.0).astype(bf16), jnp.where(low, 0.0, 1.0).astype(bf16)]

    def copy_p(pair, i):
        part = (pl.ds(2 * pair, 2), pl.ds(i * BLK, BLK), pl.ds(0, (i + 1) * BLK))
        return pltpu.make_async_copy(probs.at[part], probs_out.at[part], send_p.at[pair, i])

    def attend(pair, carry):
        cols = row_block(pair, BLK)
        query = qkv_out[0, :, cols]
        key = qkv_out[1, :, cols]
        value = qkv_out[2, :, cols]
        query = query * jnp.asarray(score_scale, bf16)
        for i in range(seq // BLK):
            rows = slice(i * BLK, (i + 1) * BLK)
            keys = (i + 1) * BLK
            mixed = []
            for b in range(2):
                head = 2 * pair + b
                part = query[rows] * halves[b]
                scores = dot_nt(part, key[:keys])
                tile = tiles[head]
                if i == 0:
                    scores = scores + tile[:, BLK:]
                elif i == 1:
                    scores = scores + tile
                else:
                    scores = jnp.concatenate(
                        [scores[:, : keys - 2 * BLK], scores[:, keys - 2 * BLK :] + tile], axis=1
                    )
                scores = scores + key_mask[:, :keys]
                raised = jnp.exp(scores - jnp.max(scores, axis=-1, keepdims=True))
                soft = raised * (1.0 / jnp.sum(raised, axis=-1, keepdims=True))
                soft = soft.astype(bf16)
                probs[head, rows, :keys] = soft
                mixed.append(dot_nn(soft, value[:keys]))
            att_out[rows, cols] = jnp.where(low, mixed[0], mixed[1]).astype(bf16)
            copy_p(pair, i).start()
        return carry

    lax.fori_loop(0, sz.pairs, attend, 0)

    router = small.astype(bf16)
    for i in range(seq // BLK):
        rows = slice(i * BLK, (i + 1) * BLK)
        resid = tok_ref[rows, :].astype(f32) + dot_nn(att_out[rows, :], w_out[3])
        resid_out[rows, :] = resid
        scale = lax.rsqrt(jnp.mean(resid * resid, axis=-1, keepdims=True) + norm_eps)
        normed = (resid * scale * gain_two).astype(bf16)
        n2_out[rows, :] = normed
        logits = dot_nn(normed, router)
        lane = iota((1, BLK), 1)
        route = routes_ref[rows, :]
        slot = slots_ref[rows, :]
        logit = [
            jnp.sum(jnp.where(lane == route[:, c : c + 1], logits, 0.0), axis=-1, keepdims=True)
            for c in range(2)
        ]
        share_one = 1.0 / (1.0 + jnp.exp(logit[1] - logit[0]))
        share_two = 1.0 / (1.0 + jnp.exp(logit[0] - logit[1]))
        kept = (slot < sz.cap).astype(f32)
        gate_out[rows, :] = jnp.where(
            lane == 0, share_one, jnp.where(lane == 1, share_two, 0.0)
        )

    cs_out[...] = jnp.zeros_like(cs_out)
    normed = n2_out[...]
    combine_one = gate_out[:, 0:1]
    combine_two = gate_out[:, 1:2]
    per = 256 // sz.cap
    for j in range(sz.slots // 256):
        lane = wide_lane + j * 256
        pick = pick_out[:, j * 256 : (j + 1) * 256]
        rows_out[j * 256 : (j + 1) * 256, :] = dot_tn(pick, normed).astype(bf16)
        weight = jnp.where(first == lane, combine_one, jnp.where(second == lane, combine_two, 0.0))
        weight = jnp.sum(weight, axis=0, keepdims=True)
        for e in range(per):
            cs_out[j * per + e, 0:1, 0 : sz.cap] = weight[:, e * sz.cap : (e + 1) * sz.cap]

    def wait_g(k, carry):
        copy_g(k).wait()
        return carry

    lax.fori_loop(1, sz.group, wait_g, 0)
    for ch in range(len(chunks)):
        finish(ch)

    def wait_p(pair, carry):
        for i in range(seq // BLK):
            copy_p(pair, i).wait()
        return carry

    lax.fori_loop(0, sz.pairs, wait_p, 0)


def vmem():
    return pl.BlockSpec(memory_space=pltpu.VMEM)


def forward_call(sz, lengths, tokens, routes, slots, small, weights, cotangent):
    seq, width, group = sz.seq, sz.width, sz.group
    shape = jax.ShapeDtypeStruct
    dma = pltpu.SemaphoreType.DMA
    wide = (4, width, width) if sz.rows % 16 else (4, 8, BLK)
    parts = len(sz.chunks)
    return pl.pallas_call(
        functools.partial(forward_kernel, sz),
        out_shape=[
            shape((4, width, width), bf16),
            shape((3, seq, width), bf16),
            shape((sz.heads, seq, seq), bf16),
            shape((seq, width), bf16),
            shape((seq, width), f32),
            shape((seq, width), bf16),
            shape((sz.slots, width), bf16),
            shape((sz.experts, 8, BLK), f32),
            shape((sz.slots, width), bf16),
            shape((seq, BLK), f32),
            shape((group * sz.small, BLK), bf16),
            shape((seq, sz.slots), bf16),
        ],
        in_specs=[pl.BlockSpec(memory_space=pltpu.SMEM)] + [vmem()] * 9,
        out_specs=[vmem(), vmem(), pl.BlockSpec(memory_space=pl.ANY)] + [vmem()] * 9,
        scratch_shapes=[
            pltpu.VMEM((2, group, sz.piece, sz.half), bf16),
            pltpu.VMEM((sz.slots, width), bf16),
            pltpu.VMEM((16, 3 * BLK), f32),
            pltpu.VMEM((sz.heads, BLK, 2 * BLK), f32),
            pltpu.VMEM((sz.heads, seq, seq), bf16),
            pltpu.VMEM(wide, f32),
            dma((parts, 2, sz.line)),
            dma((parts, sz.line)),
            dma((parts, sz.line)),
            dma((parts, sz.line)),
            dma((parts, 2 * sz.line)),
            dma((parts, 2 * sz.line)),
            dma((parts, group)),
            dma((parts, group)),
            dma((group,)),
            dma((group,)),
            dma((sz.pairs, seq // BLK)),
        ],
        compiler_params=pltpu.CompilerParams(
            collective_id=0, has_side_effects=True, vmem_limit_bytes=VMEM_LIMIT
        ),
    )(lengths, tokens, routes, slots, small, *weights, cotangent)


def gelu_parts(v):
    bell = jnp.exp(-0.5 * v * v)
    t = 1.0 / (1.0 + 0.23164189 * jnp.abs(v))
    poly = t * (
        0.254829592 + t * (-0.284496736 + t * (1.421413741 + t * (-1.453152027 + t * 1.061405429)))
    )
    tail = poly * bell
    twice = jnp.where(v < 0.0, tail, 2.0 - tail)
    return 0.5 * v * twice, 0.5 * twice + v * bell * 0.3989422804014327


def column_of(row):
    return jnp.broadcast_to(row, (BLK, BLK)).T


def expert_kernel(
    sz,
    rows_ref,
    cs_ref,
    grads_ref,
    win_ref,
    wout_ref,
    results_out,
    back_out,
    dots_out,
    own_out,
    other_out,
    win,
    wout,
    arrived,
    scales,
    arrived_t,
    scaled,
    scaled_t,
    hidden,
    pre_grad,
    back_send,
    dots_send,
    sums,
    load,
    send_r,
    recv_r,
    send_c,
    recv_c,
    send_b,
    recv_b,
    send_d,
    recv_d,
    send_w,
    recv_w,
    keep_w,
):
    rep, me, core, sibling = peers(sz)
    group, cap, width = sz.group, sz.cap, sz.width
    loads = [
        pltpu.make_async_copy(win_ref.at[0], win, load.at[0]),
        pltpu.make_async_copy(wout_ref.at[0], wout, load.at[1]),
    ]
    for copy in loads:
        copy.start()
    greet(sz, rep, me, sibling)

    def copy_r(k):
        to = xor(me, k)
        return remote(
            rows_ref.at[row_block(to, cap)], arrived.at[row_block(k, cap)],
            send_r.at[k], recv_r.at[k], (rep, to),
        )

    def copy_c(k):
        to = xor(me, k)
        return remote(cs_ref.at[to], scales.at[k], send_c.at[k], recv_c.at[k], (rep, to))

    def copy_b(k):
        return remote(
            back_send.at[row_block(k, cap)], back_out.at[row_block(me, cap)],
            send_b.at[k], recv_b.at[k], (rep, xor(me, k)),
        )

    def copy_d(k):
        return remote(
            dots_send.at[k], dots_out.at[me], send_d.at[k], recv_d.at[k], (rep, xor(me, k))
        )

    def start_r(k, carry):
        copy_c(k).start()
        copy_r(k).start()
        return carry

    lax.fori_loop(group // 2, group, start_r, 0)
    lax.fori_loop(1, group // 2, start_r, 0)
    arrived[0:cap, :] = rows_ref[row_block(me, cap), :]
    scales[0] = cs_ref[me]
    dots_send[...] = jnp.zeros_like(dots_send)
    for copy in loads:
        copy.wait()

    per = 256 // cap
    step = 512

    def rows_of(g):
        start = g * per

        def arrive(k, carry):
            copy_c(k).wait_recv()
            copy_r(k).wait_recv()
            return carry

        lax.fori_loop(max(start, 1), start + per, arrive, 0)
        span = slice(g * 256, (g + 1) * 256)
        x = arrived[span, :]
        arrived_t[:, span] = x.T
        columns = [column_of(scales[start + i, 0:1, :])[:cap, 0:1] for i in range(per)]
        column = jnp.concatenate(columns, axis=0)
        raw = grads_ref[span, :].astype(f32)
        scaled[span, :] = (raw * column).astype(bf16)
        scaled_t[:, span] = scaled[span, :].T

        def part(j, carry):
            cols = row_block(j, step)
            pre = dot_nn(arrived[span, :], win[:, cols])
            grad_hidden = dot_nn(scaled[span, :], wout[:, cols])
            act, slope = gelu_parts(pre)
            hidden[span, cols] = act.astype(bf16)
            pre_grad[span, cols] = (grad_hidden * slope).astype(bf16)
            return carry

        lax.fori_loop(0, sz.ff // step, part, 0)
        back_send[span, :] = dot_nt(pre_grad[span, :], win[...]).astype(bf16)

        def send_back(k, carry):
            copy_b(k).start()
            return carry

        lax.fori_loop(max(start, 1), start + per, send_back, 0)
        results = dot_nt(hidden[span, :], wout[...])
        results_out[span, :] = (results * column).astype(bf16)
        dots = jnp.sum(results * raw, axis=-1, keepdims=True)
        for i in range(per):
            tall = jnp.broadcast_to(dots[i * cap : (i + 1) * cap], (cap, BLK))
            if cap < BLK:
                tall = jnp.concatenate([tall, jnp.zeros((BLK - cap, BLK), f32)], axis=0)
            dots_send[start + i, 0:1, :] = tall.T[0:1, :]

        def send_dots(k, carry):
            copy_d(k).start()
            return carry

        lax.fori_loop(max(start, 1), start + per, send_dots, 0)

    groups = sz.slots // 256
    for g in range(groups):
        rows_of(g)
    back_out[row_block(me, cap), :] = back_send[0:cap, :]
    dots_out[me] = dots_send[0]

    size = sz.ff // sz.reps
    cut = 512 if size > 512 else size
    subs = size // cut
    pieces = sz.reps // 2 * subs

    def columns_of(parity, i):
        return pl.ds(pl.multiple_of((2 * (i // subs) + parity) * size + (i % subs) * cut, BLK), cut)

    def copy_w(m, i):
        return remote(
            sums.at[m, i], other_out.at[m, :, pl.ds(i * cut, cut)],
            send_w.at[m, i], recv_w.at[m, i], (sibling, me),
        )

    def copy_k(m, i):
        return pltpu.make_async_copy(
            sums.at[m, pieces + i], own_out.at[m, :, pl.ds(i * cut, cut)], keep_w.at[m, i]
        )

    for i in range(pieces):
        cols = columns_of(1 - core, i)
        sums[0, i] = dot_nn(arrived_t[...], pre_grad[:, cols]).astype(bf16)
        copy_w(0, i).start()
        sums[1, i] = dot_nn(scaled_t[...], hidden[:, cols]).astype(bf16)
        copy_w(1, i).start()
    for i in range(pieces):
        cols = columns_of(core, i)
        sums[0, pieces + i] = dot_nn(arrived_t[...], pre_grad[:, cols]).astype(bf16)
        copy_k(0, i).start()
        sums[1, pieces + i] = dot_nn(scaled_t[...], hidden[:, cols]).astype(bf16)
        copy_k(1, i).start()

    def finish(k, carry):
        copy_c(k).wait_send()
        copy_r(k).wait_send()
        copy_b(k).wait_send()
        copy_d(k).wait_send()
        from_back = remote(
            back_send.at[row_block(k, cap)], back_out.at[row_block(xor(me, k), cap)],
            send_b.at[k], recv_b.at[k], (rep, xor(me, k)),
        )
        from_back.wait_recv()
        from_dots = remote(
            dots_send.at[k], dots_out.at[xor(me, k)], send_d.at[k], recv_d.at[k], (rep, xor(me, k))
        )
        from_dots.wait_recv()
        return carry

    lax.fori_loop(1, group, finish, 0)
    for i in range(pieces):
        for m in range(2):
            copy_w(m, i).wait()
            copy_k(m, i).wait()


def expert_call(sz, rows, scales, grads, weight_in, weight_out):
    group, width, ff, slots = sz.group, sz.width, sz.ff, sz.slots
    shape = jax.ShapeDtypeStruct
    dma = pltpu.SemaphoreType.DMA
    size = ff // sz.reps
    cut = 512 if size > 512 else size
    pieces = sz.reps // 2 * (size // cut)
    anywhere = pl.BlockSpec(memory_space=pl.ANY)
    return pl.pallas_call(
        functools.partial(expert_kernel, sz),
        out_shape=[
            shape((slots, width), bf16),
            shape((slots, width), bf16),
            shape((sz.experts, 8, BLK), f32),
            shape((2, width, ff // 2), bf16),
            shape((2, width, ff // 2), bf16),
        ],
        in_specs=[vmem(), vmem(), vmem(), anywhere, anywhere],
        out_specs=[vmem(), vmem(), vmem(), anywhere, anywhere],
        scratch_shapes=[
            pltpu.VMEM((width, ff), bf16),
            pltpu.VMEM((width, ff), bf16),
            pltpu.VMEM((slots, width), bf16),
            pltpu.VMEM((group, 8, BLK), f32),
            pltpu.VMEM((width, slots), bf16),
            pltpu.VMEM((slots, width), bf16),
            pltpu.VMEM((width, slots), bf16),
            pltpu.VMEM((slots, ff), bf16),
            pltpu.VMEM((slots, ff), bf16),
            pltpu.VMEM((slots, width), bf16),
            pltpu.VMEM((group, 8, BLK), f32),
            pltpu.VMEM((2, 2 * pieces, width, cut), bf16),
            dma((2,)),
        ]
        + [dma((group,))] * 8
        + [dma((2, pieces))] * 3,
        compiler_params=pltpu.CompilerParams(
            collective_id=1, has_side_effects=True, vmem_limit_bytes=VMEM_LIMIT
        ),
    )(rows, scales, grads, weight_in, weight_out)


def near_onehot(sz):
    lane = iota((1, 3 * BLK), 1)
    distance = jnp.where(lane <= BLK, BLK - lane, 4 * BLK - lane)
    bucket = jnp.where(distance < 16, distance, 16)
    for cutoff in cutoffs:
        bucket = bucket + (distance >= cutoff).astype(jnp.int32)
    per = sz.buckets // sz.group
    shape = (sz.group, sz.rows, 3 * BLK)
    inner = iota(shape, 1)
    named = jnp.where(inner < per, iota(shape, 0) * per + inner, -1)
    return (named == bucket[None]).astype(f32).reshape(sz.width, 3 * BLK)


def unit_shapes(sz):
    up = lambda n: -(-n // 16) * 16
    return [(up(sz.rows), sz.half)] + [(up(3 * sz.rows), BLK)] * (sz.half // BLK) + [(16, sz.half)]


def backward_kernel(
    sz,
    len_ref,
    tok_ref,
    cot_ref,
    routes_ref,
    slots_ref,
    w_ref,
    qkv_ref,
    probs_ref,
    att_ref,
    resid_ref,
    n2_ref,
    gate_ref,
    small_ref,
    pick_ref,
    results_ref,
    back_ref,
    dots_ref,
    out_ref,
    gtok_ref,
    gq_ref,
    gk_ref,
    gv_ref,
    go_ref,
    gsmall_ref,
    *scratch,
):
    units = unit_shapes(sz)
    count = len(units)
    (
        probs, returned, gn2, gres, gatt, dqkv, dscore, normed, normed_t, near_sum, far_sum, sums,
        wide, packed, load, send_r, recv_r, send_x, recv_x,
    ) = scratch[:19]
    buffers = scratch[19:]
    mine = buffers[0::6]
    theirs = buffers[1::6]
    from_sib = buffers[2::6]
    from_one = buffers[3::6]
    from_two = buffers[4::6]
    final = buffers[5::6]
    rep, me, core, sibling = peers(sz)
    seq, width, half, line, group = sz.seq, sz.width, sz.half, sz.line, sz.group
    near = jnp.where(core == 0, 1, 2)
    last = jnp.where(core == 0, 2, 1)
    cap = sz.cap
    blocks = seq // BLK

    def copy_p(pair, i):
        part = (pl.ds(2 * pair, 2), pl.ds(i * BLK, BLK), pl.ds(0, (i + 1) * BLK))
        return pltpu.make_async_copy(probs_ref.at[part], probs.at[part], load.at[pair, i])

    def load_p(pair, carry):
        for i in range(blocks):
            copy_p(pair, i).start()
        return carry

    lax.fori_loop(0, sz.pairs, load_p, 0)
    greet(sz, rep, me, sibling)

    def copy_r(k, owner):
        return remote(
            results_ref.at[row_block(k, cap)], returned.at[row_block(owner, cap)],
            send_r.at[k], recv_r.at[k], (rep, xor(me, k)),
        )

    def start_r(k, carry):
        copy_r(k, me).start()
        return carry

    lax.fori_loop(group // 2, group, start_r, 0)
    lax.fori_loop(1, group // 2, start_r, 0)
    returned[row_block(me, cap), :] = results_ref[0:cap, :]

    def copy_x(u, stage):
        if stage == 0:
            src, dst, to = theirs[u], from_sib[u], (sibling, me)
        elif stage == 1:
            src, dst, to = mine[u].at[pl.ds(group // 2, group // 2)], from_one[u], (rep, xor(me, last))
        elif stage == 2:
            src, dst, to = mine[u].at[pl.ds(line, line)], from_two[u].at[pl.ds(0, line)], (rep, xor(me, near))
        elif stage == 3:
            src, dst, to = final[u].at[core], final[u].at[core], (sibling, me)
        else:
            z = stage - 3
            src, dst, to = mine[u].at[z], from_two[u].at[line + z], (rep, xor(me, 4 * z))
        return remote(src, dst, send_x.at[u, stage], recv_x.at[u, stage], to)

    def add_into(ref, start, stop, other, skip=0):
        def add(p, carry):
            ref[p] = (ref[p].astype(f32) + other[p + skip].astype(f32)).astype(bf16)
            return carry

        lax.fori_loop(start, stop, add, 0)

    def step(u, number):
        if number == 0:
            copy_x(u, 0).start()
        elif number == 1:
            copy_x(u, 0).wait_recv()
            add_into(mine[u], group // 2, group, from_sib[u])
            copy_x(u, 1).start()
            add_into(mine[u], 0, group // 2, from_sib[u])
        elif number == 2:
            copy_x(u, 1).wait_recv()
            add_into(mine[u], line, 2 * line, from_one[u])
            copy_x(u, 2).start()
            add_into(mine[u], 0, line, from_one[u])
        elif number == 3:
            copy_x(u, 2).wait_recv()
            add_into(mine[u], 0, line, from_two[u])
            for z in range(1, line):
                copy_x(u, 3 + z).start()
        elif number == 4:
            total = mine[u][0].astype(f32)
            for z in range(1, line):
                copy_x(u, 3 + z).wait_recv()
                total = total + from_two[u][line + z].astype(f32)
            final[u][core] = total
            copy_x(u, 3).start()
        else:
            remote(
                final[u].at[1 - core], final[u].at[1 - core], send_x.at[u, 3], recv_x.at[u, 3],
                (sibling, me),
            ).wait_recv()
            for stage in range(3 + line):
                copy_x(u, stage).wait_send()

    def owner_of(p, swap):
        one, two = (last, near) if swap else (near, last)
        rel = lax.rem(p, line) * 4 + lax.rem(lax.div(p, line), 2) * one + lax.div(p, 2 * line) * two
        return xor(me, rel)

    def fill(u, read):
        def put(p, carry):
            mine[u][p] = read(core, owner_of(p, False)).astype(bf16)
            theirs[u][p] = read(1 - core, owner_of(p, True)).astype(bf16)
            return carry

        lax.fori_loop(0, group, put, 0)

    def padded(value, u):
        short = units[u][0] - value.shape[0]
        if short:
            value = jnp.concatenate([value, jnp.zeros((short, value.shape[1]), f32)], axis=0)
        return value

    small = small_ref[...].astype(f32).reshape(group, sz.small, BLK)[:, : sz.rows]
    small = small.reshape(width, BLK)
    small_t = small.T
    gain_one = small_t[GAIN_ONE : GAIN_ONE + 1]
    gain_two = small_t[GAIN_TWO : GAIN_TWO + 1]
    router = small.astype(bf16)
    length = len_ref[0]

    route = routes_ref[...]
    slot = slots_ref[...]
    target = jnp.where(slot < cap, route * cap + slot, -1)
    first, second = target[:, 0:1], target[:, 1:2]
    dot_one = jnp.zeros((seq, BLK), f32)
    dot_two = jnp.zeros((seq, BLK), f32)
    lanes = iota((1, BLK), 1)
    per = BLK // cap
    for j in range(sz.slots // BLK):
        row = jnp.concatenate([dots_ref[j * per + e, 0:1, 0:cap] for e in range(per)], axis=1)
        lane = lanes + j * BLK
        dot_one = dot_one + jnp.where(first == lane, row, 0.0)
        dot_two = dot_two + jnp.where(second == lane, row, 0.0)
    dot_one = jnp.sum(dot_one, axis=-1, keepdims=True)
    dot_two = jnp.sum(dot_two, axis=-1, keepdims=True)
    share = gate_ref[:, 0:1] * gate_ref[:, 1:2] * (dot_one - dot_two)
    grad_logits = share * (
        (lanes == route[:, 0:1]).astype(f32) - (lanes == route[:, 1:2]).astype(f32)
    )
    grad_logits = grad_logits.astype(bf16)
    packed[...] = dot_tn(n2_ref[...], grad_logits)

    gain_two_grad = jnp.zeros((1, width), f32)
    for i in range(blocks):
        rows = slice(i * BLK, (i + 1) * BLK)
        grad = dot_nn(pick_ref[rows, :], back_ref[...]) + dot_nt(grad_logits[rows], router)
        resid = resid_ref[rows, :]
        scale = lax.rsqrt(jnp.mean(resid * resid, axis=-1, keepdims=True) + norm_eps)
        gain_two_grad = gain_two_grad + jnp.sum(grad * resid * scale, axis=0, keepdims=True)
        valid = (iota((BLK, 1), 0) + i * BLK < length).astype(f32)
        grad_out = cot_ref[rows, :].astype(f32) * valid
        moved = grad * gain_two
        mean = jnp.mean(moved * resid, axis=-1, keepdims=True)
        total = grad_out + scale * moved - resid * (scale * scale * scale * mean)
        gres[rows, :] = total
        gn2[rows, :] = total.astype(bf16)
    gatt[...] = dot_nt(gn2[...], w_ref[3]).astype(bf16)
    wide[...] = dot_tn(att_ref[...], gn2[...])

    def read_o(h, s):
        cols = pl.ds(pl.multiple_of(h * half, BLK), half)
        return padded(wide[row_block8(s, sz.rows), cols], 0)

    fill(0, read_o)
    step(0, 0)

    for i in range(blocks):
        rows = slice(i * BLK, (i + 1) * BLK)
        x = tok_ref[rows, :].astype(f32)
        scale = lax.rsqrt(jnp.mean(x * x, axis=-1, keepdims=True) + norm_eps)
        normed[rows, :] = (x * scale * gain_one).astype(bf16)
    normed_t[...] = normed[...].T
    step(0, 1)

    low = iota((1, BLK), 1) < width // sz.heads
    halves = [jnp.where(low, 1.0, 0.0).astype(bf16), jnp.where(low, 0.0, 1.0).astype(bf16)]

    def back_pair(pair):
        cols = row_block(pair, BLK)
        query = qkv_ref[0, :, cols]
        key = qkv_ref[1, :, cols]
        value = qkv_ref[2, :, cols]
        grads = gatt[:, cols]
        for i in range(blocks):
            copy_p(pair, i).wait()
        for i in range(blocks):
            rows = slice(i * BLK, (i + 1) * BLK)
            keys = (i + 1) * BLK
            moved = []
            for b in range(2):
                head = 2 * pair + b
                soft = probs[head, rows, :keys].astype(f32)
                grad_soft = dot_nt(grads[rows] * halves[b], value[:keys])
                both = soft * grad_soft
                grad_score = both - soft * jnp.sum(both, axis=-1, keepdims=True)
                if i == 0:
                    near_sum[head, :, :BLK] = jnp.zeros((BLK, BLK), f32)
                    near_sum[head, :, BLK:] = grad_score
                    far_sum[head] = jnp.zeros((BLK, BLK), f32)
                else:
                    near_sum[head] += grad_score[:, keys - 2 * BLK :]
                    if i >= 2:
                        far = grad_score[:, :BLK]
                        for n in range(1, i - 1):
                            far = far + grad_score[:, n * BLK : (n + 1) * BLK]
                        far_sum[head] += far
                low_score = grad_score.astype(bf16)
                dscore[b, rows, :keys] = low_score
                moved.append(dot_nn(low_score, key[:keys]))
            dqkv[0, rows, cols] = (jnp.where(low, moved[0], moved[1]) * score_scale).astype(bf16)
        for i in range(blocks):
            rows = slice(i * BLK, (i + 1) * BLK)
            below = slice(i * BLK, seq)
            gk = [dot_tn(dscore[b, below, rows], query[below]) for b in range(2)]
            gv = [dot_tn(probs[2 * pair + b, below, rows], grads[below]) for b in range(2)]
            dqkv[1, rows, cols] = (jnp.where(low, gk[0], gk[1]) * score_scale).astype(bf16)
            dqkv[2, rows, cols] = jnp.where(low, gv[0], gv[1]).astype(bf16)

    parts = half // BLK
    for j in range(parts):

        def one(h, carry, j=j):
            pair = h * parts + j
            back_pair(pair)
            cols = row_block(pair, BLK)
            for m in range(3):
                sums[h, m] = dot_nn(normed_t[...], dqkv[m, :, cols])
            return carry

        lax.fori_loop(0, 2, one, 0)

        def read_j(h, s):
            rows = row_block8(s, sz.rows)
            return padded(jnp.concatenate([sums[h, m, rows, :] for m in range(3)], axis=0), 1)

        fill(1 + j, read_j)
        step(1 + j, 0)
        step(0, 2 + j)
        if j >= 1:
            step(j, 1)
        if j >= 2:
            step(j - 1, 2)

    step(parts, 1)
    step(parts - 1, 2)

    gain_one_grad = jnp.zeros((1, width), f32)
    for i in range(blocks):
        rows = slice(i * BLK, (i + 1) * BLK)
        grad = dot_nt(dqkv[0, rows, :], w_ref[0]) + dot_nt(dqkv[1, rows, :], w_ref[1])
        grad = grad + dot_nt(dqkv[2, rows, :], w_ref[2])
        x = tok_ref[rows, :].astype(f32)
        scale = lax.rsqrt(jnp.mean(x * x, axis=-1, keepdims=True) + norm_eps)
        gain_one_grad = gain_one_grad + jnp.sum(grad * x * scale, axis=0, keepdims=True)
        moved = grad * gain_one
        mean = jnp.mean(moved * x, axis=-1, keepdims=True)
        gtok_ref[rows, :] = gres[rows, :] + scale * moved - x * (scale * scale * scale * mean)

    flip = (iota((BLK, BLK), 0) + iota((BLK, BLK), 1) == BLK - 1).astype(f32)
    ones = jnp.ones((8, BLK), f32)
    highest = lax.Precision.HIGHEST

    def bucket_sums(h, carry):
        tall = jnp.concatenate([near_sum[h], jnp.zeros((BLK, BLK), f32)], axis=1)
        turned = lax.dot_general(
            flip, tall, (((1,), (0,)), ((), ())), precision=highest, preferred_element_type=f32
        )
        rolled = pltpu.roll(turned, 2 * BLK + 1, 1, stride=1, stride_axis=0)
        packed_rows[pl.ds(h, 1), :] = jnp.sum(rolled, axis=0, keepdims=True)
        far = jnp.sum(far_sum[h], axis=0, keepdims=True)
        packed_far[pl.ds(h, 1), :] = far
        return carry

    packed_rows, packed_far = scratch[-2], scratch[-1]
    packed_rows[...] = jnp.zeros_like(packed_rows)
    packed_far[...] = jnp.zeros_like(packed_far)
    lax.fori_loop(0, sz.heads, bucket_sums, 0)
    onehot = near_onehot(sz)
    table = lax.dot_general(
        packed_rows[...], onehot, (((1,), (1,)), ((), ())), precision=highest,
        preferred_element_type=f32,
    )
    far = jnp.sum(packed_far[...], axis=-1, keepdims=True)
    farthest = lax.dot_general(
        jnp.ones((8, BLK), f32), onehot[:, :BLK] * (lanes == 0).astype(f32), (((1,), (1,)), ((), ())),
        precision=highest, preferred_element_type=f32,
    )[0:1]
    table = table + far * farthest
    tall = jnp.concatenate(
        [
            jnp.zeros((GAIN_ONE, width), f32),
            gain_one_grad,
            gain_two_grad,
            jnp.zeros((TABLE - GAIN_TWO - 1, width), f32),
            table,
            jnp.zeros((BLK - TABLE - 16, width), f32),
        ],
        axis=0,
    )
    packed[...] = packed[...] + tall.T

    def read_small(h, s):
        start = pl.multiple_of(s * sz.rows, 8)
        value = packed[pl.ds(start, sz.rows), :]
        if sz.small != sz.rows:
            value = jnp.concatenate([value, jnp.zeros((sz.small - sz.rows, BLK), f32)], axis=0)
        cuts = [value[16 * i : 16 * (i + 1)] for i in range(sz.share)]
        cuts = cuts + [jnp.zeros((16, BLK), f32)] * (half // BLK - sz.share)
        return jnp.concatenate(cuts, axis=1)

    fill(count - 1, read_small)
    step(count - 1, 0)
    step(parts, 2)
    step(parts - 1, 3)
    step(count - 1, 1)
    step(parts, 3)
    step(count - 1, 2)
    if parts >= 3:
        step(parts - 2, 3)
        step(parts - 2, 4)
    step(0, 5)
    step(parts - 1, 4)
    step(count - 1, 3)

    def wait_r(k, carry):
        copy_r(k, xor(me, k)).wait_recv()
        return carry

    lax.fori_loop(1, group, wait_r, 0)
    for i in range(blocks):
        rows = slice(i * BLK, (i + 1) * BLK)
        valid = (iota((BLK, 1), 0) + i * BLK < length).astype(f32)
        total = resid_ref[rows, :] + dot_nn(pick_ref[rows, :], returned[...])
        out_ref[rows, :] = (total * valid).astype(bf16)

    step(parts, 4)
    step(count - 1, 4)
    for u in range(1, count):
        step(u, 5)
    for h in range(2):
        cols = slice(h * half, (h + 1) * half)
        go_ref[:, cols] = final[0][h, : sz.rows]
        for j in range(parts):
            at = slice(h * half + j * BLK, h * half + (j + 1) * BLK)
            for m, ref in enumerate((gq_ref, gk_ref, gv_ref)):
                ref[:, at] = final[1 + j][h, m * sz.rows : (m + 1) * sz.rows]
    for i in range(sz.share):
        gsmall_ref[16 * i : 16 * (i + 1), :] = final[count - 1][0, :, i * BLK : (i + 1) * BLK]

    def sent_r(k, carry):
        copy_r(k, me).wait_send()
        return carry

    lax.fori_loop(1, group, sent_r, 0)


def row_block8(index, size):
    return pl.ds(pl.multiple_of(index * size, 8), size)


def backward_call(sz, lengths, tokens, cotangent, routes, slots, saved, results, back, dots):
    seq, width, group, line = sz.seq, sz.width, sz.group, sz.line
    shape = jax.ShapeDtypeStruct
    dma = pltpu.SemaphoreType.DMA
    w, qkv, probs, att, resid, n2, gate, small, pick = saved
    units = unit_shapes(sz)
    buffers = []
    for rows, cols in units:
        buffers += [
            pltpu.VMEM((group, rows, cols), bf16),
            pltpu.VMEM((group, rows, cols), bf16),
            pltpu.VMEM((group, rows, cols), bf16),
            pltpu.VMEM((group // 2, rows, cols), bf16),
            pltpu.VMEM((2 * line, rows, cols), bf16),
            pltpu.VMEM((2, rows, cols), f32),
        ]
    dense = shape((sz.rows, width), f32)
    return pl.pallas_call(
        functools.partial(backward_kernel, sz),
        out_shape=[
            shape((seq, width), bf16),
            shape((seq, width), f32),
            dense,
            dense,
            dense,
            dense,
            shape((sz.small, BLK), f32),
        ],
        in_specs=[pl.BlockSpec(memory_space=pltpu.SMEM)]
        + [vmem()] * 6
        + [pl.BlockSpec(memory_space=pl.ANY)]
        + [vmem()] * 9,
        out_specs=[vmem()] * 7,
        scratch_shapes=[
            pltpu.VMEM((sz.heads, seq, seq), bf16),
            pltpu.VMEM((sz.slots, width), bf16),
            pltpu.VMEM((seq, width), bf16),
            pltpu.VMEM((seq, width), f32),
            pltpu.VMEM((seq, width), bf16),
            pltpu.VMEM((3, seq, width), bf16),
            pltpu.VMEM((2, seq, seq), bf16),
            pltpu.VMEM((seq, width), bf16),
            pltpu.VMEM((width, seq), bf16),
            pltpu.VMEM((sz.heads, BLK, 2 * BLK), f32),
            pltpu.VMEM((sz.heads, BLK, BLK), f32),
            pltpu.VMEM((2, 3, width, BLK), f32),
            pltpu.VMEM((width, width), f32),
            pltpu.VMEM((width, BLK), f32),
            dma((sz.pairs, seq // BLK)),
            dma((group,)),
            dma((group,)),
            dma((len(units), 3 + line)),
            dma((len(units), 3 + line)),
        ]
        + buffers
        + [pltpu.VMEM((16, 3 * BLK), f32), pltpu.VMEM((16, BLK), f32)],
        compiler_params=pltpu.CompilerParams(
            collective_id=2, has_side_effects=True, vmem_limit_bytes=VMEM_LIMIT
        ),
    )(
        lengths, tokens, cotangent, routes, slots, w, qkv, probs, att, resid, n2, gate, small, pick,
        results, back, dots,
    )


def shards(
    tokens, lengths, routes, slots, norm_one, w_query, w_key, w_value, w_output, bias_table, norm_two,
    router, expert_in, expert_out, cotangent, *, reps, group,
):
    seq, width = tokens.shape
    rows = w_query.shape[0]
    heads = bias_table.shape[1]
    experts = router.shape[1]
    sz = Sizes(
        reps, group, seq, width, heads, experts, expert_in.shape[2], rows, bias_table.shape[0] * group
    )
    small = jnp.zeros((sz.small, BLK), bf16)
    small = small.at[:rows, :experts].set(router)
    small = small.at[:rows, GAIN_ONE].set(norm_one)
    small = small.at[:rows, GAIN_TWO].set(norm_two)
    small = small.at[: bias_table.shape[0], TABLE : TABLE + heads].set(bias_table)
    weights = (w_query, w_key, w_value, w_output)
    (w, qkv, probs, att, resid, n2, sent, scales, grads, gate, small_all, pick) = forward_call(
        sz, lengths, tokens, routes, slots, small, weights, cotangent
    )
    results, back, dots, own, other = expert_call(sz, sent, scales, grads, expert_in, expert_out)
    saved = (w, qkv, probs, att, resid, n2, gate, small_all, pick)
    output, grad_tokens, gq, gk, gv, go, gsmall = backward_call(
        sz, lengths, tokens, cotangent, routes, slots, saved, results, back, dots
    )
    expert_grads = own.astype(f32) + other.astype(f32)
    if reps > 2:
        same = [[r for r in range(reps) if r % 2 == c] for c in range(2)]
        expert_grads = lax.psum_scatter(
            expert_grads, "rep", scatter_dimension=2, axis_index_groups=same, tiled=True
        )
        gq, gk, gv, go, gsmall = lax.psum(
            (gq, gk, gv, go, gsmall), "rep", axis_index_groups=same
        )
    return (
        output,
        grad_tokens,
        gsmall[:rows, GAIN_ONE],
        gq,
        gk,
        gv,
        go,
        gsmall[: bias_table.shape[0], TABLE : TABLE + heads],
        gsmall[:rows, GAIN_TWO],
        gsmall[:rows, :experts],
        expert_grads[0:1],
        expert_grads[1:2],
    )


def solution(mesh):
    both = ("rep", "shard")
    return jax.shard_map(
        functools.partial(shards, reps=mesh.shape["rep"], group=mesh.shape["shard"]),
        mesh=mesh,
        in_specs=(
            P(both, None),
            P(both),
            P(both, None),
            P(both, None),
            P("shard"),
            P("shard", None),
            P("shard", None),
            P("shard", None),
            P("shard", None),
            P("shard", None),
            P("shard"),
            P("shard", None),
            P("shard", None, None),
            P("shard", None, None),
            P(both, None),
        ),
        out_specs=(
            P(both, None),
            P(both, None),
            P("shard"),
            P("shard", None),
            P("shard", None),
            P("shard", None),
            P("shard", None),
            P("shard", None),
            P("shard"),
            P("shard", None),
            P("shard", None, "rep"),
            P("shard", None, "rep"),
        ),
        check_vma=False,
    )
```

```python
import functools

import jax
import jax.numpy as jnp
from jax import lax
from jax.experimental import pallas as pl
from jax.experimental.pallas import tpu as pltpu
from jax.sharding import PartitionSpec as P

MESH = pl.DeviceIdType.MESH
norm_eps = 1e-06
score_scale = 0.125
cutoffs = (19, 21, 24, 27, 31, 35, 40, 46, 52, 59, 67, 77, 87, 99, 113)
f32 = jnp.float32
bf16 = jnp.bfloat16
GAIN_ONE, GAIN_TWO, TABLE = 64, 65, 80
BLK = 128
VMEM_LIMIT = 60 * 2**20
NEG = -1e30


def dot_nn(a, b):
    return lax.dot_general(a, b, (((1,), (0,)), ((), ())), preferred_element_type=f32)


def dot_nt(a, b):
    return lax.dot_general(a, b, (((1,), (1,)), ((), ())), preferred_element_type=f32)


def dot_tn(a, b):
    return lax.dot_general(a, b, (((0,), (0,)), ((), ())), preferred_element_type=f32)


def iota(shape, dim):
    return lax.broadcasted_iota(jnp.int32, shape, dim)


class Sizes:
    def __init__(self, reps, group, seq, width, heads, experts, ff, rows, buckets):
        self.reps, self.group, self.seq, self.width = reps, group, seq, width
        self.heads, self.experts, self.ff, self.rows = heads, experts, ff, rows
        self.buckets = buckets
        self.cap = 2 * seq // experts
        self.slots = experts * self.cap
        self.line = group // 4
        self.half = width // 2
        self.small = -(-rows // 16) * 16
        self.share = self.small // 16
        self.piece = 4 * rows
        self.pairs = heads // 2
        self.chunks = ((0, self.piece),)

    def relative(self, half, place):
        first, second = (1, 2) if half == 0 else (2, 1)
        line = place % self.line
        return line * 4 + (place // self.line % 2) * first + (place // (2 * self.line)) * second


def peers(sz):
    rep = lax.axis_index("rep")
    me = lax.axis_index("shard")
    return rep, me, lax.rem(rep, 2), rep + 1 - 2 * lax.rem(rep, 2)


def xor(a, b):
    return jnp.bitwise_xor(a, b)


def greet(sz, rep, me, sibling):
    barrier = pltpu.get_barrier_semaphore()

    def signal(k, carry):
        pl.semaphore_signal(barrier, inc=1, device_id=(rep, xor(me, k)), device_id_type=MESH)
        return carry

    lax.fori_loop(1, sz.group, signal, 0)
    pl.semaphore_signal(barrier, inc=1, device_id=(sibling, me), device_id_type=MESH)
    pl.semaphore_wait(barrier, sz.group)


def remote(src, dst, send, recv, device):
    return pltpu.make_async_remote_copy(
        src_ref=src, dst_ref=dst, send_sem=send, recv_sem=recv, device_id=device, device_id_type=MESH
    )


def send_order(group):
    order = list(range(group // 2, group)) + list(range(1, group // 2))
    return order


def row_block(index, size):
    return pl.ds(pl.multiple_of(index * size, size), size)


def row_block8(index, size):
    return pl.ds(pl.multiple_of(index * size, 8), size)


def target_slots(sz, routes, slots):
    return jnp.where(slots < sz.cap, routes * sz.cap + slots, -1)


def bias_tiles(sz, small_t, vector, tiles):
    lane = iota((1, 3 * BLK), 1)
    distance = jnp.where(lane <= BLK, BLK - lane, 4 * BLK - lane)
    bucket = jnp.where(distance < 16, distance, 16)
    for cutoff in cutoffs:
        bucket = bucket + (distance >= cutoff).astype(jnp.int32)
    per = sz.buckets // sz.group
    shape = (sz.group, sz.rows, 3 * BLK)
    inner = iota(shape, 1)
    named = jnp.where(inner < per, iota(shape, 0) * per + inner, -1)
    onehot = (named == bucket[None]).astype(f32).reshape(sz.width, 3 * BLK).astype(bf16)
    table = small_t[TABLE : TABLE + 16].astype(bf16)
    values = dot_nn(table, onehot)
    values = values - values[:, 0:1]
    vector[...] = jnp.where((lane > BLK) & (lane < 2 * BLK), NEG, values)

    def tile(pair, carry):
        for b in range(2):
            row = jnp.broadcast_to(vector[pl.ds(2 * pair + b, 1), :], (BLK, 3 * BLK))
            turned = pltpu.roll(row, 0, 1, stride=1, stride_axis=0)[:, : 2 * BLK]
            tiles[pair, :, b * BLK : (b + 1) * BLK] = turned.T
        return carry

    lax.fori_loop(0, sz.pairs, tile, 0)


def forward_kernel(
    sz,
    len_ref,
    tok_ref,
    routes_ref,
    slots_ref,
    small_ref,
    wq_ref,
    wk_ref,
    wv_ref,
    wo_ref,
    cot_ref,
    w_out,
    qkv_out,
    probs_out,
    att_out,
    resid_out,
    garr_out,
    pick_out,
    n2_out,
    rows_out,
    cs_out,
    gate_out,
    small_out,
    pieces,
    gsend,
    relay,
    vector,
    tiles,
    probs,
    wide,
    whole,
    qkv,
    att,
    resid_all,
    pick_all,
    mask,
    send_z,
    recv_z,
    send_b,
    recv_b,
    send_c,
    recv_c,
    send_s,
    recv_s,
    send_m,
    recv_m,
    send_g,
    recv_g,
    send_p,
    keep,
    keep_rows,
):
    rep, me, core, sibling = peers(sz)
    seq, width, half, line = sz.seq, sz.width, sz.half, sz.line
    place_a = me // 4
    near = jnp.where(core == 0, 1, 2)
    last = jnp.where(core == 0, 2, 1)

    for h in range(2):
        cols = slice(h * half, (h + 1) * half)
        if sz.rows % 16 == 0:
            for m, ref in enumerate((wq_ref, wk_ref, wv_ref, wo_ref)):
                pieces[h, 0, m * sz.rows : (m + 1) * sz.rows, :] = ref[:, cols]
        else:
            stacked = [ref[:, cols].astype(f32) for ref in (wq_ref, wk_ref, wv_ref, wo_ref)]
            pieces[h, 0] = jnp.concatenate(stacked, axis=0).astype(bf16)

    greet(sz, rep, me, sibling)

    chunks = sz.chunks

    def block(ch, slot):
        lo, hi = chunks[ch]
        return pieces.at[core, slot, pl.ds(lo, hi - lo)]

    def copy_z(ch, up, source, to):
        slot = xor(source, to)
        return remote(
            block(ch, xor(source, place_a)),
            block(ch, slot),
            send_z.at[ch, up, xor(source, place_a)],
            recv_z.at[ch, slot],
            (rep, me + (to - place_a) * 4),
        )

    def copy_b(ch, i):
        return remote(
            block(ch, i),
            block(ch, line + i),
            send_b.at[ch, i],
            recv_b.at[ch, i],
            (rep, xor(me, near)),
        )

    def copy_c(ch, i):
        return remote(
            block(ch, i),
            block(ch, 2 * line + i),
            send_c.at[ch, i],
            recv_c.at[ch, i],
            (rep, xor(me, last)),
        )

    def copy_s(ch, i):
        return remote(
            block(ch, i), block(ch, i), send_s.at[ch, i], recv_s.at[ch, i], (sibling, me)
        )

    def forward_z(ch, t):
        for up, step in ((1, 1), (0, -1)):
            source = place_a - step * t
            to = place_a + step
            there = (source >= 0) & (source < line)
            onward = there & (to >= 0) & (to < line)

            @pl.when(there)
            def _(up=up, source=source, to=to, onward=onward):
                slot = xor(source, place_a)
                if t > 0:
                    remote(
                        block(ch, slot), block(ch, slot), send_z.at[ch, up, slot],
                        recv_z.at[ch, slot], (rep, me),
                    ).wait_recv()

                @pl.when(onward)
                def _():
                    copy_z(ch, up, source, to).start()

                if t > 0:
                    copy_b(ch, slot).start()
                    copy_c(ch, slot).start()
                    copy_s(ch, slot).start()

    def wait_sent_z(ch):
        for t in range(line - 1):
            for up, step in ((1, 1), (0, -1)):
                source = place_a - step * t
                to = place_a + step
                onward = (source >= 0) & (source < line) & (to >= 0) & (to < line)

                @pl.when(onward)
                def _(up=up, source=source, to=to):
                    copy_z(ch, up, source, to).wait_send()

    def start_own(ch):
        forward_z(ch, 0)
        copy_b(ch, 0).start()
        copy_c(ch, 0).start()

    def from_b(ch, i):
        copy_b(ch, i).wait_recv()
        copy_c(ch, line + i).start()
        copy_s(ch, line + i).start()

    def from_c(ch, i):
        copy_c(ch, i).wait_recv()
        copy_s(ch, 2 * line + i).start()

    def each(ch, do, start, stop):
        def one(i, carry):
            do(ch, i)
            return carry

        lax.fori_loop(start, stop, one, 0)

    def gather_stages(ch):
        def begin():
            from_b(ch, 0)
            forward_z(ch, 1)

        def middle():
            for t in range(2, line):
                forward_z(ch, t)

        return (
            begin,
            middle,
            lambda: each(ch, from_b, 1, line),
            lambda: each(ch, from_c, 0, line),
            lambda: each(ch, from_c, line, 2 * line),
        )

    def gather(ch):
        for stage in gather_stages(ch):
            stage()

    def finish(ch):
        def sent_b(i, carry):
            copy_b(ch, i).wait_send()
            return carry

        def sent_c(i, carry):
            copy_c(ch, i).wait_send()
            return carry

        def sent_s(i, carry):
            copy_s(ch, i).wait_send()
            return carry

        wait_sent_z(ch)
        lax.fori_loop(0, line, sent_b, 0)
        lax.fori_loop(0, 2 * line, sent_c, 0)
        lax.fori_loop(1, sz.group, sent_s, 0)

    def from_sibling(ch):
        def wait(i, carry):
            lo, hi = chunks[ch]
            other = pieces.at[1 - core, i, pl.ds(lo, hi - lo)]
            remote(other, other, send_s.at[ch, i], recv_s.at[ch, i], (sibling, me)).wait_recv()
            return carry

        lax.fori_loop(1, sz.group, wait, 0)

    chunk_rest, chunk_last = 0, len(chunks) - 1
    start_own(chunk_rest)

    def copy_m(k):
        return remote(
            small_ref, small_out.at[me], send_m.at[k], recv_m.at[k], (rep, xor(me, k))
        )

    def start_m(k, carry):
        copy_m(k).start()
        return carry

    lax.fori_loop(1, sz.group, start_m, 0)
    small_out[me] = small_ref[...]

    def keep_copy(n, src, dst):
        return pltpu.make_async_copy(src, dst, keep.at[n])

    places = jnp.concatenate(
        [routes_ref[...], slots_ref[...], jnp.zeros((4, seq), jnp.int32)], axis=0
    )
    places = places.astype(f32).T.astype(jnp.int32)
    route = places[:, 0:2]
    slot = places[:, 2:4]
    target = target_slots(sz, route, slot)
    first, second = target[:, 0:1], target[:, 1:2]
    wide_lane = iota((1, 256), 1)
    for j in range(sz.slots // 256):
        lane = wide_lane + j * 256
        pick = ((first == lane) | (second == lane)).astype(f32).astype(bf16)
        pick_all[:, j * 256 : (j + 1) * 256] = pick
        gsend[j * 256 : (j + 1) * 256, :] = dot_tn(pick, cot_ref[...]).astype(bf16)
    keep_copy(0, pick_all, pick_out).start()

    low_bits = lax.rem(me, 4)

    def copy_far(z):
        return remote(
            gsend.at[row_block(xor(place_a, z), 4 * sz.cap)],
            relay.at[z],
            send_g.at[4 * z],
            recv_g.at[4 * z],
            (rep, xor(me, 4 * z)),
        )

    def copy_plane(z, k):
        if z == 0:
            src = gsend.at[row_block(xor(me, k), sz.cap)]
        else:
            src = relay.at[z, row_block(xor(low_bits, k), sz.cap)]
        return remote(
            src,
            garr_out.at[pl.ds((4 * z + k) * sz.cap, sz.cap)],
            send_g.at[4 * z + k],
            recv_g.at[4 * z + k],
            (rep, xor(me, k)),
        )

    def own_rows(z):
        if z == 0:
            src = gsend.at[row_block(me, sz.cap)]
        else:
            src = relay.at[z, row_block(low_bits, sz.cap)]
        return pltpu.make_async_copy(
            src, garr_out.at[pl.ds(4 * z * sz.cap, sz.cap)], keep_rows.at[z]
        )

    def pass_on(z):
        if z > 0:
            copy_far(z).wait_recv()
        own_rows(z).start()
        for k in range(1, 4):
            copy_plane(z, k).start()

    far_order = list(range(line // 2, line)) + list(range(1, line // 2))
    begin, middle, rest_b, low_c, high_c = gather_stages(chunk_rest)
    begin()
    middle()
    rest_b()
    for z in far_order:
        copy_far(z).start()

    def wait_m(k, carry):
        remote(
            small_ref, small_out.at[xor(me, k)], send_m.at[k], recv_m.at[k], (rep, xor(me, k))
        ).wait()
        return carry

    lax.fori_loop(1, sz.group, wait_m, 0)
    small = small_out[...].astype(f32)[:, : sz.rows].reshape(width, BLK)
    small_t = small.T
    gain_one = small_t[GAIN_ONE : GAIN_ONE + 1]
    gain_two = small_t[GAIN_TWO : GAIN_TWO + 1]
    for i in range(seq // BLK):
        rows = slice(i * BLK, (i + 1) * BLK)
        x = tok_ref[rows, :].astype(f32)
        scale = lax.rsqrt(jnp.mean(x * x, axis=-1, keepdims=True) + norm_eps)
        n2_out[rows, :] = (x * scale * gain_one).astype(bf16)
    low_c()
    bias_tiles(sz, small_t, vector, tiles)
    length = len_ref[0]
    mask[...] = jnp.broadcast_to(jnp.where(iota((seq, 1), 0) < length, 0.0, NEG), (seq, BLK))
    high_c()
    from_sibling(chunk_rest)
    pass_on(0)

    def assemble(low, high):
        for place in range(sz.group):
            for h in range(2):
                source = xor(me, sz.relative(h, place))
                cols = slice(h * half, (h + 1) * half)
                if sz.rows % 16 == 0:
                    for m in range(low, high):
                        whole[m, row_block(source, sz.rows), cols] = pieces[
                            h, place, m * sz.rows : (m + 1) * sz.rows, :
                        ]
                else:
                    tall = pieces[h, place, :, :].astype(f32)
                    for m in range(low, high):
                        wide[m, row_block8(source, sz.rows), cols] = tall[
                            m * sz.rows : (m + 1) * sz.rows
                        ]
        if sz.rows % 16 != 0:
            for m in range(low, high):
                whole[m] = wide[m].astype(bf16)

    assemble(0, 3)
    keep_copy(2, whole.at[pl.ds(0, 3)], w_out.at[pl.ds(0, 3)]).start()
    for m in range(3):
        qkv[m] = dot_nn(n2_out[...], whole[m]).astype(bf16)
    keep_copy(3, qkv, qkv_out).start()

    low = iota((1, BLK), 1) < width // sz.heads
    halves = [jnp.where(low, 1.0, 0.0).astype(bf16), jnp.where(low, 0.0, 1.0).astype(bf16)]
    size = width // sz.heads

    def copy_p(pair, i):
        part = (pair, pl.ds(0, (i + 1) * BLK), pl.ds(2 * i * BLK, 2 * BLK))
        return pltpu.make_async_copy(probs.at[part], probs_out.at[part], send_p.at[pair, i])

    def attend(pair, carry):
        cols = row_block(pair, BLK)
        query = qkv[0, :, cols] * jnp.asarray(score_scale, bf16)
        key = qkv[1, :, cols]
        value_t = qkv[2, :, cols].T
        for i in range(seq // BLK):
            rows = slice(i * BLK, (i + 1) * BLK)
            keys = (i + 1) * BLK
            both = jnp.concatenate([query[rows] * halves[0], query[rows] * halves[1]], axis=0)
            scores = dot_nt(key[:keys], both)
            tile = tiles[pair]
            if i == 0:
                scores = scores + tile[BLK:]
            elif i == 1:
                scores = scores + tile
            else:
                scores = jnp.concatenate(
                    [scores[: keys - 2 * BLK], scores[keys - 2 * BLK :] + tile], axis=0
                )
            hidden = mask[:keys, :]
            scores = scores + jnp.concatenate([hidden, hidden], axis=1)
            raised = jnp.exp(scores - jnp.max(scores, axis=0, keepdims=True))
            soft = raised * (1.0 / jnp.sum(raised, axis=0, keepdims=True))
            soft = soft.astype(bf16)
            probs[pair, :keys, 2 * i * BLK : 2 * (i + 1) * BLK] = soft
            mixed = dot_nn(value_t[:, :keys], soft)
            mixed = jnp.concatenate([mixed[:size, :BLK], mixed[size:, BLK:]], axis=0)
            att[rows, cols] = mixed.T.astype(bf16)
        for i in range(seq // BLK):
            copy_p(pair, i).start()
        return carry

    lax.fori_loop(0, sz.pairs - 2, attend, 0)
    pass_on(far_order[-1])
    lax.fori_loop(sz.pairs - 2, sz.pairs, attend, 0)
    pass_on(far_order[0])
    keep_copy(4, att, att_out).start()
    assemble(3, 4)
    keep_copy(5, whole.at[pl.ds(3, 1)], w_out.at[pl.ds(3, 1)]).start()

    router = small.astype(bf16)
    for i in range(seq // BLK):
        rows = slice(i * BLK, (i + 1) * BLK)
        resid = tok_ref[rows, :].astype(f32) + dot_nn(att[rows, :], whole[3])
        resid_all[rows, :] = resid
        scale = lax.rsqrt(jnp.mean(resid * resid, axis=-1, keepdims=True) + norm_eps)
        normed = (resid * scale * gain_two).astype(bf16)
        n2_out[rows, :] = normed
        logits = dot_nn(normed, router)
        lane = iota((1, BLK), 1)
        logit = [
            jnp.sum(jnp.where(lane == route[rows, c : c + 1], logits, 0.0), axis=-1, keepdims=True)
            for c in range(2)
        ]
        share_one = 1.0 / (1.0 + jnp.exp(logit[1] - logit[0]))
        share_two = 1.0 / (1.0 + jnp.exp(logit[0] - logit[1]))
        gate_out[rows, :] = jnp.where(
            lane == 0, share_one, jnp.where(lane == 1, share_two, 0.0)
        )
    keep_copy(6, resid_all, resid_out).start()

    cs_out[...] = jnp.zeros_like(cs_out)
    normed = n2_out[...]
    combine_one = gate_out[:, 0:1]
    combine_two = gate_out[:, 1:2]
    per = 256 // sz.cap
    for j in range(sz.slots // 256):
        lane = wide_lane + j * 256
        pick = pick_all[:, j * 256 : (j + 1) * 256]
        rows_out[j * 256 : (j + 1) * 256, :] = dot_tn(pick, normed).astype(bf16)
        weight = jnp.where(first == lane, combine_one, jnp.where(second == lane, combine_two, 0.0))
        weight = jnp.sum(weight, axis=0, keepdims=True)
        for e in range(per):
            cs_out[j * per + e, 0:1, 0 : sz.cap] = weight[:, e * sz.cap : (e + 1) * sz.cap]

    for z in far_order[1:-1]:
        pass_on(z)
    for z in range(line):
        own_rows(z).wait()
        if z > 0:
            copy_far(z).wait_send()
        for k in range(1, 4):
            copy_plane(z, k).wait()
    for ch in range(len(chunks)):
        finish(ch)

    def wait_p(pair, carry):
        for i in range(seq // BLK):
            copy_p(pair, i).wait()
        return carry

    lax.fori_loop(0, sz.pairs, wait_p, 0)
    keep_copy(0, pick_all, pick_out).wait()
    keep_copy(2, whole.at[pl.ds(0, 3)], w_out.at[pl.ds(0, 3)]).wait()
    keep_copy(3, qkv, qkv_out).wait()
    keep_copy(4, att, att_out).wait()
    keep_copy(5, whole.at[pl.ds(3, 1)], w_out.at[pl.ds(3, 1)]).wait()
    keep_copy(6, resid_all, resid_out).wait()


def vmem():
    return pl.BlockSpec(memory_space=pltpu.VMEM)


def anywhere():
    return pl.BlockSpec(memory_space=pl.ANY)


def forward_call(sz, lengths, tokens, routes, slots, small, weights, cotangent):
    seq, width, group = sz.seq, sz.width, sz.group
    shape = jax.ShapeDtypeStruct
    dma = pltpu.SemaphoreType.DMA
    wide = (4, width, width) if sz.rows % 16 else (4, 8, BLK)
    parts = len(sz.chunks)
    return pl.pallas_call(
        functools.partial(forward_kernel, sz),
        out_shape=[
            shape((4, width, width), bf16),
            shape((3, seq, width), bf16),
            shape((sz.pairs, seq, 2 * seq), bf16),
            shape((seq, width), bf16),
            shape((seq, width), f32),
            shape((sz.slots, width), bf16),
            shape((seq, sz.slots), bf16),
            shape((seq, width), bf16),
            shape((sz.slots, width), bf16),
            shape((sz.experts, 8, BLK), f32),
            shape((seq, BLK), f32),
            shape((group, sz.small, BLK), bf16),
        ],
        in_specs=[pl.BlockSpec(memory_space=pltpu.SMEM)] + [vmem()] * 9,
        out_specs=[anywhere()] * 7 + [vmem()] * 5,
        scratch_shapes=[
            pltpu.VMEM((2, group, sz.piece, sz.half), bf16),
            pltpu.VMEM((sz.slots, width), bf16),
            pltpu.VMEM((sz.line, 4 * sz.cap, width), bf16),
            pltpu.VMEM((16, 3 * BLK), f32),
            pltpu.VMEM((sz.pairs, 2 * BLK, 2 * BLK), f32),
            pltpu.VMEM((sz.pairs, seq, 2 * seq), bf16),
            pltpu.VMEM(wide, f32),
            pltpu.VMEM((4, width, width), bf16),
            pltpu.VMEM((3, seq, width), bf16),
            pltpu.VMEM((seq, width), bf16),
            pltpu.VMEM((seq, width), f32),
            pltpu.VMEM((seq, sz.slots), bf16),
            pltpu.VMEM((seq, BLK), f32),
            dma((parts, 2, sz.line)),
            dma((parts, sz.line)),
            dma((parts, sz.line)),
            dma((parts, sz.line)),
            dma((parts, 2 * sz.line)),
            dma((parts, 2 * sz.line)),
            dma((parts, group)),
            dma((parts, group)),
            dma((group,)),
            dma((group,)),
            dma((group,)),
            dma((group,)),
            dma((sz.pairs, seq // BLK)),
            dma((8,)),
            dma((sz.line,)),
        ],
        compiler_params=pltpu.CompilerParams(
            collective_id=0, has_side_effects=True, vmem_limit_bytes=VMEM_LIMIT
        ),
    )(lengths, tokens, routes, slots, small, *weights, cotangent)


def gelu_parts(v):
    bell = jnp.exp(-0.5 * v * v)
    t = 1.0 / (1.0 + 0.23164189 * jnp.abs(v))
    poly = t * (
        0.254829592 + t * (-0.284496736 + t * (1.421413741 + t * (-1.453152027 + t * 1.061405429)))
    )
    tail = poly * bell
    twice = jnp.where(v < 0.0, tail, 2.0 - tail)
    return 0.5 * v * twice, 0.5 * twice + v * bell * 0.3989422804014327


def column_of(row):
    return jnp.broadcast_to(row, (BLK, BLK)).T


def expert_kernel(
    sz,
    rows_ref,
    cs_ref,
    grads_ref,
    win_ref,
    wout_ref,
    results_out,
    back_out,
    dots_out,
    own_in,
    own_out,
    other_in,
    other_out,
    win,
    wout,
    arrived,
    scales,
    arrived_t,
    scaled,
    scaled_t,
    hidden,
    pre_grad,
    back_send,
    dots_send,
    sums,
    load,
    send_r,
    recv_r,
    send_c,
    recv_c,
    send_b,
    recv_b,
    send_d,
    recv_d,
    send_w,
    recv_w,
    keep_w,
):
    rep, me, core, sibling = peers(sz)
    group, cap, width = sz.group, sz.cap, sz.width
    loads = [
        pltpu.make_async_copy(win_ref.at[0], win, load.at[0]),
        pltpu.make_async_copy(wout_ref.at[0], wout, load.at[1]),
    ]
    for copy in loads:
        copy.start()
    greet(sz, rep, me, sibling)

    def copy_r(k):
        to = xor(me, k)
        return remote(
            rows_ref.at[row_block(to, cap)], arrived.at[row_block(k, cap)],
            send_r.at[k], recv_r.at[k], (rep, to),
        )

    def copy_c(k):
        to = xor(me, k)
        return remote(cs_ref.at[to], scales.at[k], send_c.at[k], recv_c.at[k], (rep, to))

    def copy_b(k):
        return remote(
            back_send.at[row_block(k, cap)], back_out.at[row_block(me, cap)],
            send_b.at[k], recv_b.at[k], (rep, xor(me, k)),
        )

    def copy_d(k):
        return remote(
            dots_send.at[k], dots_out.at[me], send_d.at[k], recv_d.at[k], (rep, xor(me, k))
        )

    def start_r(k, carry):
        copy_c(k).start()
        copy_r(k).start()
        return carry

    lax.fori_loop(group // 2, group, start_r, 0)
    lax.fori_loop(1, group // 2, start_r, 0)
    arrived[0:cap, :] = rows_ref[row_block(me, cap), :]
    scales[0] = cs_ref[me]
    dots_send[...] = jnp.zeros_like(dots_send)
    for copy in loads:
        copy.wait()

    per = 256 // cap
    step = 512

    def rows_of(g):
        start = g * per

        def arrive(k, carry):
            copy_c(k).wait_recv()
            copy_r(k).wait_recv()
            return carry

        lax.fori_loop(max(start, 1), start + per, arrive, 0)
        span = slice(g * 256, (g + 1) * 256)
        x = arrived[span, :]
        arrived_t[:, span] = x.T
        columns = [column_of(scales[start + i, 0:1, :])[:cap, 0:1] for i in range(per)]
        column = jnp.concatenate(columns, axis=0)
        raw = grads_ref[span, :].astype(f32)
        scaled[span, :] = (raw * column).astype(bf16)
        scaled_t[:, span] = scaled[span, :].T

        def part(j, carry):
            cols = row_block(j, step)
            pre = dot_nn(arrived[span, :], win[:, cols])
            grad_hidden = dot_nn(scaled[span, :], wout[:, cols])
            act, slope = gelu_parts(pre)
            hidden[span, cols] = act.astype(bf16)
            pre_grad[span, cols] = (grad_hidden * slope).astype(bf16)
            return carry

        lax.fori_loop(0, sz.ff // step, part, 0)
        back_send[span, :] = dot_nt(pre_grad[span, :], win[...]).astype(bf16)

        def send_back(k, carry):
            copy_b(k).start()
            return carry

        lax.fori_loop(max(start, 1), start + per, send_back, 0)
        results = dot_nt(hidden[span, :], wout[...])
        results_out[span, :] = (results * column).astype(bf16)
        dots = jnp.sum(results * raw, axis=-1, keepdims=True)
        for i in range(per):
            tall = jnp.broadcast_to(dots[i * cap : (i + 1) * cap], (cap, BLK))
            if cap < BLK:
                tall = jnp.concatenate([tall, jnp.zeros((BLK - cap, BLK), f32)], axis=0)
            dots_send[start + i, 0:1, :] = tall.T[0:1, :]

        def send_dots(k, carry):
            copy_d(k).start()
            return carry

        lax.fori_loop(max(start, 1), start + per, send_dots, 0)

    groups = sz.slots // 256
    for g in range(groups):
        rows_of(g)
    back_out[row_block(me, cap), :] = back_send[0:cap, :]
    dots_out[me] = dots_send[0]

    size = sz.ff // sz.reps
    cut = 512 if size > 512 else size
    subs = size // cut
    pieces = sz.reps // 2 * subs

    def columns_of(parity, i):
        return pl.ds(pl.multiple_of((2 * (i // subs) + parity) * size + (i % subs) * cut, BLK), cut)

    def copy_w(m, i):
        return remote(
            sums.at[m, i], (other_in, other_out)[m].at[:, pl.ds(i * cut, cut)],
            send_w.at[m, i], recv_w.at[m, i], (sibling, me),
        )

    def copy_k(m, i):
        return pltpu.make_async_copy(
            sums.at[m, pieces + i], (own_in, own_out)[m].at[:, pl.ds(i * cut, cut)], keep_w.at[m, i]
        )

    for i in range(pieces):
        cols = columns_of(1 - core, i)
        sums[0, i] = dot_nn(arrived_t[...], pre_grad[:, cols]).astype(bf16)
        copy_w(0, i).start()
        sums[1, i] = dot_nn(scaled_t[...], hidden[:, cols]).astype(bf16)
        copy_w(1, i).start()
    for i in range(pieces):
        cols = columns_of(core, i)
        sums[0, pieces + i] = dot_nn(arrived_t[...], pre_grad[:, cols]).astype(bf16)
        copy_k(0, i).start()
        sums[1, pieces + i] = dot_nn(scaled_t[...], hidden[:, cols]).astype(bf16)
        copy_k(1, i).start()

    def finish(k, carry):
        copy_c(k).wait_send()
        copy_r(k).wait_send()
        copy_b(k).wait_send()
        copy_d(k).wait_send()
        from_back = remote(
            back_send.at[row_block(k, cap)], back_out.at[row_block(xor(me, k), cap)],
            send_b.at[k], recv_b.at[k], (rep, xor(me, k)),
        )
        from_back.wait_recv()
        from_dots = remote(
            dots_send.at[k], dots_out.at[xor(me, k)], send_d.at[k], recv_d.at[k], (rep, xor(me, k))
        )
        from_dots.wait_recv()
        return carry

    lax.fori_loop(1, group, finish, 0)
    for i in range(pieces):
        for m in range(2):
            copy_w(m, i).wait()
            copy_k(m, i).wait()


def expert_call(sz, rows, scales, grads, weight_in, weight_out):
    group, width, ff, slots = sz.group, sz.width, sz.ff, sz.slots
    shape = jax.ShapeDtypeStruct
    dma = pltpu.SemaphoreType.DMA
    size = ff // sz.reps
    cut = 512 if size > 512 else size
    pieces = sz.reps // 2 * (size // cut)
    anywhere = pl.BlockSpec(memory_space=pl.ANY)
    return pl.pallas_call(
        functools.partial(expert_kernel, sz),
        out_shape=[
            shape((slots, width), bf16),
            shape((slots, width), bf16),
            shape((sz.experts, 8, BLK), f32),
            shape((width, ff // 2), bf16),
            shape((width, ff // 2), bf16),
            shape((width, ff // 2), bf16),
            shape((width, ff // 2), bf16),
        ],
        in_specs=[vmem(), vmem(), vmem(), anywhere, anywhere],
        out_specs=[vmem(), vmem(), vmem(), anywhere, anywhere, anywhere, anywhere],
        scratch_shapes=[
            pltpu.VMEM((width, ff), bf16),
            pltpu.VMEM((width, ff), bf16),
            pltpu.VMEM((slots, width), bf16),
            pltpu.VMEM((group, 8, BLK), f32),
            pltpu.VMEM((width, slots), bf16),
            pltpu.VMEM((slots, width), bf16),
            pltpu.VMEM((width, slots), bf16),
            pltpu.VMEM((slots, ff), bf16),
            pltpu.VMEM((slots, ff), bf16),
            pltpu.VMEM((slots, width), bf16),
            pltpu.VMEM((group, 8, BLK), f32),
            pltpu.VMEM((2, 2 * pieces, width, cut), bf16),
            dma((2,)),
        ]
        + [dma((group,))] * 8
        + [dma((2, pieces))] * 3,
        compiler_params=pltpu.CompilerParams(
            collective_id=1, has_side_effects=True, vmem_limit_bytes=VMEM_LIMIT
        ),
    )(rows, scales, grads, weight_in, weight_out)


def near_onehot(sz):
    lane = iota((1, 3 * BLK), 1)
    distance = jnp.where(lane <= BLK, BLK + lane, lane - 2 * BLK)
    bucket = jnp.where(distance < 16, distance, 16)
    for cutoff in cutoffs:
        bucket = bucket + (distance >= cutoff).astype(jnp.int32)
    per = sz.buckets // sz.group
    shape = (sz.group, sz.rows, 3 * BLK)
    inner = iota(shape, 1)
    named = jnp.where(inner < per, iota(shape, 0) * per + inner, -1)
    return (named == bucket[None]).astype(f32).reshape(sz.width, 3 * BLK).astype(bf16)


def unit_shapes(sz):
    up = lambda n: -(-n // 16) * 16
    return [(up(sz.rows), sz.half)] + [(up(3 * sz.rows), BLK)] * (sz.half // BLK)


def backward_kernel(
    sz,
    len_ref,
    tok_ref,
    cot_ref,
    routes_ref,
    slots_ref,
    n2_ref,
    gate_ref,
    small_ref,
    dots_ref,
    w_hbm,
    qkv_hbm,
    probs_hbm,
    att_hbm,
    resid_hbm,
    pick_hbm,
    results_hbm,
    back_hbm,
    out_ref,
    gtok_ref,
    gq_ref,
    gk_ref,
    gv_ref,
    go_ref,
    gsmall_ref,
    *scratch,
):
    units = unit_shapes(sz)
    (
        probs, w_ref, qkv_ref, att_ref, resid_ref, pick_ref, back_ref, returned, total_bf, gres, gatt,
        dqkv, dscore, stacks, normed, normed_t, near_sum, far_sum, sums, wide, packed, packed_rows,
        packed_far, small_mine, small_from, small_final,
        load, load_p, send_r, recv_r, send_x, recv_x, send_m, recv_m,
    ) = scratch[:34]
    buffers = scratch[34:]
    mine = buffers[0::6]
    theirs = buffers[1::6]
    from_sib = buffers[2::6]
    from_one = buffers[3::6]
    from_two = buffers[4::6]
    final = buffers[5::6]
    rep, me, core, sibling = peers(sz)
    seq, width, half, line, group = sz.seq, sz.width, sz.half, sz.line, sz.group
    near = jnp.where(core == 0, 1, 2)
    last = jnp.where(core == 0, 2, 1)
    cap = sz.cap
    blocks = seq // BLK

    def fetch(n, src, dst):
        return pltpu.make_async_copy(src, dst, load.at[n])

    loads = [
        fetch(0, back_hbm, back_ref),
        fetch(1, pick_hbm, pick_ref),
        fetch(2, resid_hbm, resid_ref),
        fetch(3, w_hbm.at[3], w_ref.at[3]),
        fetch(4, att_hbm, att_ref),
        fetch(5, qkv_hbm, qkv_ref),
        fetch(6, w_hbm.at[pl.ds(0, 3)], w_ref.at[pl.ds(0, 3)]),
        fetch(7, results_hbm.at[pl.ds(0, cap)], returned.at[row_block(me, cap)]),
    ]

    def copy_p(pair, i):
        part = (pair, pl.ds(0, (i + 1) * BLK), pl.ds(2 * i * BLK, 2 * BLK))
        return pltpu.make_async_copy(probs_hbm.at[part], probs.at[part], load_p.at[pair, i])

    def start_p(pair, carry):
        for i in range(blocks):
            copy_p(pair, i).start()
        return carry

    for copy in loads[:6]:
        copy.start()
    lax.fori_loop(0, sz.pairs, start_p, 0)
    for copy in loads[6:]:
        copy.start()
    greet(sz, rep, me, sibling)

    def copy_r(k, owner):
        return remote(
            results_hbm.at[row_block(k, cap)], returned.at[row_block(owner, cap)],
            send_r.at[k], recv_r.at[k], (rep, xor(me, k)),
        )

    def start_r(k, carry):
        copy_r(k, me).start()
        return carry

    lax.fori_loop(group // 2, group, start_r, 0)
    lax.fori_loop(1, group // 2, start_r, 0)

    def copy_x(u, stage):
        if stage == 0:
            src, dst, to = theirs[u], from_sib[u], (sibling, me)
        elif stage == 1:
            src, dst, to = mine[u].at[pl.ds(group // 2, group // 2)], from_one[u], (rep, xor(me, last))
        elif stage == 2:
            src, dst, to = mine[u].at[pl.ds(line, line)], from_two[u].at[pl.ds(0, line)], (rep, xor(me, near))
        elif stage == 3:
            src, dst, to = final[u].at[core], final[u].at[core], (sibling, me)
        else:
            z = stage - 3
            src, dst, to = mine[u].at[z], from_two[u].at[line + z], (rep, xor(me, 4 * z))
        return remote(src, dst, send_x.at[u, stage], recv_x.at[u, stage], to)

    def add_into(ref, start, stop, other, skip=0):
        def add(p, carry):
            ref[p] = (ref[p].astype(f32) + other[p + skip].astype(f32)).astype(bf16)
            return carry

        lax.fori_loop(start, stop, add, 0)

    def step(u, number):
        if number == 0:
            copy_x(u, 0).start()
        elif number == 1:
            copy_x(u, 0).wait_recv()
            add_into(mine[u], group // 2, group, from_sib[u])
            copy_x(u, 1).start()
            add_into(mine[u], 0, group // 2, from_sib[u])
        elif number == 2:
            copy_x(u, 1).wait_recv()
            add_into(mine[u], line, 2 * line, from_one[u])
            copy_x(u, 2).start()
            add_into(mine[u], 0, line, from_one[u])
        elif number == 3:
            copy_x(u, 2).wait_recv()
            add_into(mine[u], 0, line, from_two[u])
            for z in range(1, line):
                copy_x(u, 3 + z).start()
        elif number == 4:
            total = mine[u][0].astype(f32)
            for z in range(1, line):
                copy_x(u, 3 + z).wait_recv()
                total = total + from_two[u][line + z].astype(f32)
            final[u][core] = total
            copy_x(u, 3).start()
        else:
            remote(
                final[u].at[1 - core], final[u].at[1 - core], send_x.at[u, 3], recv_x.at[u, 3],
                (sibling, me),
            ).wait_recv()
            for stage in range(3 + line):
                copy_x(u, stage).wait_send()

    def owner_of(p, swap):
        one, two = (last, near) if swap else (near, last)
        rel = lax.rem(p, line) * 4 + lax.rem(lax.div(p, line), 2) * one + lax.div(p, 2 * line) * two
        return xor(me, rel)

    def fill(u, read):
        def put(p, carry):
            mine[u][p] = read(core, owner_of(p, False)).astype(bf16)
            theirs[u][p] = read(1 - core, owner_of(p, True)).astype(bf16)
            return carry

        lax.fori_loop(0, group, put, 0)

    def padded(value, u):
        short = units[u][0] - value.shape[0]
        if short:
            value = jnp.concatenate([value, jnp.zeros((short, value.shape[1]), f32)], axis=0)
        return value

    small = small_ref[...].astype(f32)[:, : sz.rows].reshape(width, BLK)
    small_t = small.T
    gain_one = small_t[GAIN_ONE : GAIN_ONE + 1]
    gain_two = small_t[GAIN_TWO : GAIN_TWO + 1]
    router = small.astype(bf16)
    length = len_ref[0]

    places = jnp.concatenate(
        [routes_ref[...], slots_ref[...], jnp.zeros((4, seq), jnp.int32)], axis=0
    )
    places = places.astype(f32).T.astype(jnp.int32)
    route = places[:, 0:2]
    target = target_slots(sz, route, places[:, 2:4])
    first, second = target[:, 0:1], target[:, 1:2]
    dot_one = jnp.zeros((seq, BLK), f32)
    dot_two = jnp.zeros((seq, BLK), f32)
    lanes = iota((1, BLK), 1)
    per = BLK // cap
    for j in range(sz.slots // BLK):
        row = jnp.concatenate([dots_ref[j * per + e, 0:1, 0:cap] for e in range(per)], axis=1)
        lane = lanes + j * BLK
        dot_one = dot_one + jnp.where(first == lane, row, 0.0)
        dot_two = dot_two + jnp.where(second == lane, row, 0.0)
    dot_one = jnp.sum(dot_one, axis=-1, keepdims=True)
    dot_two = jnp.sum(dot_two, axis=-1, keepdims=True)
    share = gate_ref[:, 0:1] * gate_ref[:, 1:2] * (dot_one - dot_two)
    grad_logits = share * (
        (lanes == route[:, 0:1]).astype(f32) - (lanes == route[:, 1:2]).astype(f32)
    )
    grad_logits = grad_logits.astype(bf16)
    packed[...] = dot_tn(n2_ref[...], grad_logits)

    for copy in loads[:3]:
        copy.wait()
    gain_two_grad = jnp.zeros((1, width), f32)
    for i in range(blocks):
        rows = slice(i * BLK, (i + 1) * BLK)
        grad = dot_nn(pick_ref[rows, :], back_ref[...]) + dot_nt(grad_logits[rows], router)
        resid = resid_ref[rows, :]
        scale = lax.rsqrt(jnp.mean(resid * resid, axis=-1, keepdims=True) + norm_eps)
        gain_two_grad = gain_two_grad + jnp.sum(grad * resid * scale, axis=0, keepdims=True)
        valid = (iota((BLK, 1), 0) + i * BLK < length).astype(f32)
        grad_out = cot_ref[rows, :].astype(f32) * valid
        moved = grad * gain_two
        mean = jnp.mean(moved * resid, axis=-1, keepdims=True)
        total = grad_out + scale * moved - resid * (scale * scale * scale * mean)
        gres[rows, :] = total
        total_bf[rows, :] = total.astype(bf16)
    loads[3].wait()
    loads[4].wait()
    gatt[...] = dot_nt(total_bf[...], w_ref[3]).astype(bf16)
    wide[...] = dot_tn(att_ref[...], total_bf[...])

    def read_o(h, s):
        cols = pl.ds(pl.multiple_of(h * half, BLK), half)
        return padded(wide[row_block8(s, sz.rows), cols], 0)

    fill(0, read_o)
    step(0, 0)

    for i in range(blocks):
        rows = slice(i * BLK, (i + 1) * BLK)
        x = tok_ref[rows, :].astype(f32)
        scale = lax.rsqrt(jnp.mean(x * x, axis=-1, keepdims=True) + norm_eps)
        normed[rows, :] = (x * scale * gain_one).astype(bf16)
    normed_t[...] = normed[...].T
    step(0, 1)

    low = iota((1, BLK), 1) < width // sz.heads
    halves = [jnp.where(low, 1.0, 0.0).astype(bf16), jnp.where(low, 0.0, 1.0).astype(bf16)]

    size = width // sz.heads
    loads[5].wait()

    def back_pair(pair):
        cols = row_block(pair, BLK)
        query = qkv_ref[0, :, cols]
        key = qkv_ref[1, :, cols]
        key_t = key.T
        value = qkv_ref[2, :, cols]
        grads = gatt[:, cols]
        for i in range(blocks):
            copy_p(pair, i).wait()
        for i in range(blocks):
            rows = slice(i * BLK, (i + 1) * BLK)
            keys = (i + 1) * BLK
            at = slice(2 * i * BLK, 2 * (i + 1) * BLK)
            both = jnp.concatenate([grads[rows] * halves[0], grads[rows] * halves[1]], axis=0)
            stacks[0, at, :] = jnp.concatenate(
                [query[rows] * halves[0], query[rows] * halves[1]], axis=0
            )
            stacks[1, at, :] = both
            soft = probs[pair, :keys, at].astype(f32)
            product = soft * dot_nt(value[:keys], both)
            grad_score = product - soft * jnp.sum(product, axis=0, keepdims=True)
            if i == 0:
                near_sum[pair, :BLK] = jnp.zeros((BLK, 2 * BLK), f32)
                near_sum[pair, BLK:] = grad_score
                far_sum[pair] = jnp.zeros((8, 2 * BLK), f32)
            else:
                near_sum[pair] += grad_score[keys - 2 * BLK :]
                if i >= 2:
                    far = grad_score[: keys - 2 * BLK].reshape((keys - 2 * BLK) // 8, 8, 2 * BLK)
                    far_sum[pair] += jnp.sum(far, axis=0)
            low_score = grad_score.astype(bf16)
            dscore[:keys, at] = low_score
            moved = dot_nn(key_t[:, :keys], low_score)
            moved = jnp.concatenate([moved[:size, :BLK], moved[size:, BLK:]], axis=0)
            dqkv[0, rows, cols] = (moved.T * score_scale).astype(bf16)
        for i in range(blocks):
            rows = slice(i * BLK, (i + 1) * BLK)
            below = slice(2 * i * BLK, 2 * seq)
            grad_key = dot_nn(dscore[rows, below], stacks[0, below, :])
            grad_value = dot_nn(probs[pair, rows, below], stacks[1, below, :])
            dqkv[1, rows, cols] = (grad_key * score_scale).astype(bf16)
            dqkv[2, rows, cols] = grad_value.astype(bf16)

    parts = half // BLK
    for j in range(parts):

        def one(h, carry, j=j):
            pair = h * parts + j
            back_pair(pair)
            cols = row_block(pair, BLK)
            grads = jnp.concatenate([dqkv[m, :, cols] for m in range(3)], axis=1)
            sums[h] = dot_nn(normed_t[...], grads)
            return carry

        lax.fori_loop(0, 2, one, 0)

        def read_j(h, s):
            rows = row_block8(s, sz.rows)
            value = sums[h, rows, :]
            return padded(
                jnp.concatenate([value[:, m * BLK : (m + 1) * BLK] for m in range(3)], axis=0), 1
            )

        fill(1 + j, read_j)
        step(1 + j, 0)
        if j >= 1:
            step(j, 1)
        if j >= 2:
            step(j - 1, 2)
        step(0, 2 + j)

    loads[6].wait()
    gain_one_grads = []

    def input_grad(i):
        rows = slice(i * BLK, (i + 1) * BLK)
        grad = dot_nt(dqkv[0, rows, :], w_ref[0]) + dot_nt(dqkv[1, rows, :], w_ref[1])
        grad = grad + dot_nt(dqkv[2, rows, :], w_ref[2])
        x = tok_ref[rows, :].astype(f32)
        scale = lax.rsqrt(jnp.mean(x * x, axis=-1, keepdims=True) + norm_eps)
        gain_one_grads.append(jnp.sum(grad * x * scale, axis=0, keepdims=True))
        moved = grad * gain_one
        mean = jnp.mean(moved * x, axis=-1, keepdims=True)
        gtok_ref[rows, :] = gres[rows, :] + scale * moved - x * (scale * scale * scale * mean)

    flip = (iota((2 * BLK, 2 * BLK), 0) + iota((2 * BLK, 2 * BLK), 1) == 2 * BLK - 1)
    flip = flip.astype(f32).astype(bf16)

    def bucket_sums(pair, carry):
        turned = dot_nn(flip, near_sum[pair].astype(bf16))
        far = jnp.sum(far_sum[pair], axis=0, keepdims=True)
        for b in range(2):
            tall = jnp.concatenate(
                [turned[:, b * BLK : (b + 1) * BLK], jnp.zeros((2 * BLK, 2 * BLK), f32)], axis=1
            )
            rolled = pltpu.roll(tall, BLK + 1, 1, stride=1, stride_axis=0)
            packed_rows[pl.ds(2 * pair + b, 1), :] = jnp.sum(rolled, axis=0, keepdims=True)
            packed_far[pl.ds(2 * pair + b, 1), :] = far[:, b * BLK : (b + 1) * BLK]
        return carry

    def table_grad():
        packed_rows[...] = jnp.zeros_like(packed_rows)
        packed_far[...] = jnp.zeros_like(packed_far)
        lax.fori_loop(0, sz.pairs, bucket_sums, 0)
        onehot = near_onehot(sz)
        values = packed_rows[...]
        upper = values.astype(bf16)
        lower = (values - upper.astype(f32)).astype(bf16)
        table = dot_nt(upper, onehot) + dot_nt(lower, onehot)
        far = jnp.sum(packed_far[...], axis=-1, keepdims=True)
        one_far = jnp.broadcast_to((lanes == 0).astype(f32), (8, BLK)).astype(bf16)
        farthest = dot_nt(one_far, onehot[:, :BLK])[0:1]
        return table + far * farthest

    def copy_m(k):
        return remote(
            small_mine.at[xor(me, k)], small_from.at[k], send_m.at[k], recv_m.at[k], (rep, xor(me, k))
        )

    def small_start(table):
        gain_one_grad = gain_one_grads[0]
        for grad in gain_one_grads[1:]:
            gain_one_grad = gain_one_grad + grad
        tall = jnp.concatenate(
            [
                jnp.zeros((GAIN_ONE, width), f32),
                gain_one_grad,
                gain_two_grad,
                jnp.zeros((TABLE - GAIN_TWO - 1, width), f32),
                table,
                jnp.zeros((BLK - TABLE - 16, width), f32),
            ],
            axis=0,
        )
        whole = (packed[...] + tall.T).reshape(group, sz.rows, BLK)
        if sz.small != sz.rows:
            whole = jnp.concatenate(
                [whole, jnp.zeros((group, sz.small - sz.rows, BLK), f32)], axis=1
            )
        small_mine[...] = whole.astype(bf16)

        def start_m(k, carry):
            copy_m(k).start()
            return carry

        lax.fori_loop(1, group, start_m, 0)

    def copy_f():
        return remote(
            small_final.at[core], small_final.at[core], send_m.at[0], recv_m.at[0], (sibling, me)
        )

    def small_sum():
        small_final[core] = small_mine[me].astype(f32)

        def add(k, carry):
            copy_m(k).wait()
            small_final[core] += small_from[k].astype(f32)
            return carry

        lax.fori_loop(1, group, add, 0)
        copy_f().start()

    def small_end():
        remote(
            small_final.at[1 - core], small_final.at[1 - core], send_m.at[0], recv_m.at[0],
            (sibling, me),
        ).wait_recv()
        gsmall_ref[...] = small_final[0] + small_final[1]
        copy_f().wait_send()

    def results():
        def wait_r(k, carry):
            copy_r(k, xor(me, k)).wait_recv()
            return carry

        lax.fori_loop(1, group, wait_r, 0)
        loads[7].wait()
        for i in range(blocks):
            rows = slice(i * BLK, (i + 1) * BLK)
            valid = (iota((BLK, 1), 0) + i * BLK < length).astype(f32)
            total = resid_ref[rows, :] + dot_nn(pick_ref[rows, :], returned[...])
            out_ref[rows, :] = (total * valid).astype(bf16)

    input_grad(0)
    step(parts, 1)
    step(parts - 1, 2)
    input_grad(1)
    step(parts - 2, 3)
    input_grad(2)
    step(parts, 2)
    step(parts - 1, 3)
    for i in range(3, blocks):
        input_grad(i)
    table = table_grad()
    small_start(table)
    step(parts, 3)
    step(parts - 2, 4)
    results()
    step(0, 5)
    step(parts - 1, 4)
    small_sum()
    step(parts, 4)
    small_end()
    for u in range(1, 1 + parts):
        step(u, 5)
    for h in range(2):
        cols = slice(h * half, (h + 1) * half)
        go_ref[:, cols] = final[0][h, : sz.rows]
        for j in range(parts):
            at = slice(h * half + j * BLK, h * half + (j + 1) * BLK)
            for m, ref in enumerate((gq_ref, gk_ref, gv_ref)):
                ref[:, at] = final[1 + j][h, m * sz.rows : (m + 1) * sz.rows]

    def sent_r(k, carry):
        copy_r(k, me).wait_send()
        return carry

    lax.fori_loop(1, group, sent_r, 0)


def backward_call(sz, lengths, tokens, cotangent, routes, slots, saved, results, back, dots):
    seq, width, group, line = sz.seq, sz.width, sz.group, sz.line
    shape = jax.ShapeDtypeStruct
    dma = pltpu.SemaphoreType.DMA
    w, qkv, probs, att, resid, pick, n2, gate, small = saved
    units = unit_shapes(sz)
    buffers = []
    for rows, cols in units:
        buffers += [
            pltpu.VMEM((group, rows, cols), bf16),
            pltpu.VMEM((group, rows, cols), bf16),
            pltpu.VMEM((group, rows, cols), bf16),
            pltpu.VMEM((group // 2, rows, cols), bf16),
            pltpu.VMEM((2 * line, rows, cols), bf16),
            pltpu.VMEM((2, rows, cols), f32),
        ]
    dense = shape((sz.rows, width), f32)
    return pl.pallas_call(
        functools.partial(backward_kernel, sz),
        out_shape=[
            shape((seq, width), bf16),
            shape((seq, width), f32),
            dense,
            dense,
            dense,
            dense,
            shape((sz.small, BLK), f32),
        ],
        in_specs=[pl.BlockSpec(memory_space=pltpu.SMEM)] + [vmem()] * 8 + [anywhere()] * 8,
        out_specs=[vmem()] * 7,
        scratch_shapes=[
            pltpu.VMEM((sz.pairs, seq, 2 * seq), bf16),
            pltpu.VMEM((4, width, width), bf16),
            pltpu.VMEM((3, seq, width), bf16),
            pltpu.VMEM((seq, width), bf16),
            pltpu.VMEM((seq, width), f32),
            pltpu.VMEM((seq, sz.slots), bf16),
            pltpu.VMEM((sz.slots, width), bf16),
            pltpu.VMEM((sz.slots, width), bf16),
            pltpu.VMEM((seq, width), bf16),
            pltpu.VMEM((seq, width), f32),
            pltpu.VMEM((seq, width), bf16),
            pltpu.VMEM((3, seq, width), bf16),
            pltpu.VMEM((seq, 2 * seq), bf16),
            pltpu.VMEM((2, 2 * seq, BLK), bf16),
            pltpu.VMEM((seq, width), bf16),
            pltpu.VMEM((width, seq), bf16),
            pltpu.VMEM((sz.pairs, 2 * BLK, 2 * BLK), f32),
            pltpu.VMEM((sz.pairs, 8, 2 * BLK), f32),
            pltpu.VMEM((2, width, 3 * BLK), f32),
            pltpu.VMEM((width, width), f32),
            pltpu.VMEM((width, BLK), f32),
            pltpu.VMEM((16, 3 * BLK), f32),
            pltpu.VMEM((16, BLK), f32),
            pltpu.VMEM((group, sz.small, BLK), bf16),
            pltpu.VMEM((group, sz.small, BLK), bf16),
            pltpu.VMEM((2, sz.small, BLK), f32),
            dma((8,)),
            dma((sz.pairs, seq // BLK)),
            dma((group,)),
            dma((group,)),
            dma((len(units), 3 + line)),
            dma((len(units), 3 + line)),
            dma((group,)),
            dma((group,)),
        ]
        + buffers,
        compiler_params=pltpu.CompilerParams(
            collective_id=2, has_side_effects=True, vmem_limit_bytes=VMEM_LIMIT
        ),
    )(
        lengths, tokens, cotangent, routes, slots, n2, gate, small, dots, w, qkv, probs, att, resid,
        pick, results, back,
    )


def shards(
    tokens, lengths, routes, slots, norm_one, w_query, w_key, w_value, w_output, bias_table, norm_two,
    router, expert_in, expert_out, cotangent, *, reps, group,
):
    seq, width = tokens.shape
    rows = w_query.shape[0]
    heads = bias_table.shape[1]
    experts = router.shape[1]
    sz = Sizes(
        reps, group, seq, width, heads, experts, expert_in.shape[2], rows, bias_table.shape[0] * group
    )
    fill = lambda count: jnp.zeros((rows, count), bf16)
    few = bias_table.shape[0]
    small = jnp.concatenate(
        [
            router,
            fill(GAIN_ONE - experts),
            norm_one[:, None],
            norm_two[:, None],
            fill(TABLE - GAIN_TWO - 1),
            jnp.pad(bias_table, ((0, rows - few), (0, BLK - TABLE - heads))),
        ],
        axis=1,
    )
    small = jnp.pad(small, ((0, sz.small - rows), (0, 0)))
    weights = (w_query, w_key, w_value, w_output)
    routes, slots = routes.T, slots.T
    (w, qkv, probs, att, resid, grads, pick, n2, sent, scales, gate, small_all) = forward_call(
        sz, lengths, tokens, routes, slots, small, weights, cotangent
    )
    results, back, dots, *halves = expert_call(sz, sent, scales, grads, expert_in, expert_out)
    saved = (w, qkv, probs, att, resid, pick, n2, gate, small_all)
    output, grad_tokens, gq, gk, gv, go, gsmall = backward_call(
        sz, lengths, tokens, cotangent, routes, slots, saved, results, back, dots
    )
    grad_in = (halves[0].astype(f32) + halves[2].astype(f32))[None]
    grad_out = (halves[1].astype(f32) + halves[3].astype(f32))[None]
    if reps > 2:
        same = [[r for r in range(reps) if r % 2 == c] for c in range(2)]
        grad_in, grad_out = (
            lax.psum_scatter(
                grad, "rep", scatter_dimension=2, axis_index_groups=same, tiled=True
            )
            for grad in (grad_in, grad_out)
        )
        gq, gk, gv, go, gsmall = lax.psum(
            (gq, gk, gv, go, gsmall), "rep", axis_index_groups=same
        )
    return (
        output,
        grad_tokens,
        gsmall[:rows, GAIN_ONE],
        gq,
        gk,
        gv,
        go,
        gsmall[: bias_table.shape[0], TABLE : TABLE + heads],
        gsmall[:rows, GAIN_TWO],
        gsmall[:rows, :experts],
        grad_in,
        grad_out,
    )


def solution(mesh):
    both = ("rep", "shard")
    return jax.shard_map(
        functools.partial(shards, reps=mesh.shape["rep"], group=mesh.shape["shard"]),
        mesh=mesh,
        in_specs=(
            P(both, None),
            P(both),
            P(both, None),
            P(both, None),
            P("shard"),
            P("shard", None),
            P("shard", None),
            P("shard", None),
            P("shard", None),
            P("shard", None),
            P("shard"),
            P("shard", None),
            P("shard", None, None),
            P("shard", None, None),
            P(both, None),
        ),
        out_specs=(
            P(both, None),
            P(both, None),
            P("shard"),
            P("shard", None),
            P("shard", None),
            P("shard", None),
            P("shard", None),
            P("shard", None),
            P("shard"),
            P("shard", None),
            P("shard", None, "rep"),
            P("shard", None, "rep"),
        ),
        check_vma=False,
    )
```

```python
import functools

import jax
import jax.numpy as jnp
from jax import lax
from jax.experimental import pallas as pl
from jax.experimental.pallas import tpu as pltpu
from jax.sharding import PartitionSpec as P

MESH = pl.DeviceIdType.MESH
norm_eps = 1e-06
score_scale = 0.125
cutoffs = (19, 21, 24, 27, 31, 35, 40, 46, 52, 59, 67, 77, 87, 99, 113)
f32 = jnp.float32
bf16 = jnp.bfloat16
GAIN_ONE, GAIN_TWO, TABLE = 64, 65, 80
BLK = 128
VMEM_LIMIT = 60 * 2**20
NEG = -1e30
PLAN_H = ((), ((1, 1),), ((2, 1),))
PLAN_J = (((1, 0),), ((2, 0),), ((3, 0), (1, 2), (0, 2)))
PLAN_T = (
    "T", (3, 1), (2, 2), 0, (1, 3), (0, 3), 1, (3, 2), (2, 3), 2, 3, "M", (3, 3), (1, 4), (0, 4), "R", "m", (2, 4),
    (0, 5), (3, 4), "e",
)


def dot_nn(a, b):
    return lax.dot_general(a, b, (((1,), (0,)), ((), ())), preferred_element_type=f32)


def dot_nt(a, b):
    return lax.dot_general(a, b, (((1,), (1,)), ((), ())), preferred_element_type=f32)


def dot_tn(a, b):
    return lax.dot_general(a, b, (((0,), (0,)), ((), ())), preferred_element_type=f32)


def iota(shape, dim):
    return lax.broadcasted_iota(jnp.int32, shape, dim)


class Sizes:
    def __init__(self, reps, group, seq, width, heads, experts, ff, rows, buckets):
        self.reps, self.group, self.seq, self.width = reps, group, seq, width
        self.heads, self.experts, self.ff, self.rows = heads, experts, ff, rows
        self.buckets = buckets
        self.cap = 2 * seq // experts
        self.slots = experts * self.cap
        self.line = group // 4
        self.half = width // 2
        self.small = -(-rows // 16) * 16
        self.share = self.small // 16
        self.piece = 4 * rows
        self.pairs = heads // 2
        self.chunks = ((0, self.piece),)

    def relative(self, half, place):
        first, second = (1, 2) if half == 0 else (2, 1)
        line = place % self.line
        return line * 4 + (place // self.line % 2) * first + (place // (2 * self.line)) * second


def peers(sz):
    rep = lax.axis_index("rep")
    me = lax.axis_index("shard")
    return rep, me, lax.rem(rep, 2), rep + 1 - 2 * lax.rem(rep, 2)


def xor(a, b):
    return jnp.bitwise_xor(a, b)


def greet(sz, rep, me, sibling):
    barrier = pltpu.get_barrier_semaphore()

    def signal(k, carry):
        pl.semaphore_signal(barrier, inc=1, device_id=(rep, xor(me, k)), device_id_type=MESH)
        return carry

    lax.fori_loop(1, sz.group, signal, 0)
    pl.semaphore_signal(barrier, inc=1, device_id=(sibling, me), device_id_type=MESH)
    pl.semaphore_wait(barrier, sz.group)


def remote(src, dst, send, recv, device):
    return pltpu.make_async_remote_copy(
        src_ref=src, dst_ref=dst, send_sem=send, recv_sem=recv, device_id=device, device_id_type=MESH
    )


def send_order(group):
    order = list(range(group // 2, group)) + list(range(1, group // 2))
    return order


def row_block(index, size):
    return pl.ds(pl.multiple_of(index * size, size), size)


def row_block8(index, size):
    return pl.ds(pl.multiple_of(index * size, 8), size)


def target_slots(sz, routes, slots):
    return jnp.where(slots < sz.cap, routes * sz.cap + slots, -1)


def bias_tiles(sz, small_t, vector, tiles):
    lane = iota((1, 3 * BLK), 1)
    distance = jnp.where(lane <= BLK, BLK - lane, 4 * BLK - lane)
    bucket = jnp.where(distance < 16, distance, 16)
    for cutoff in cutoffs:
        bucket = bucket + (distance >= cutoff).astype(jnp.int32)
    per = sz.buckets // sz.group
    shape = (sz.group, sz.rows, 3 * BLK)
    inner = iota(shape, 1)
    named = jnp.where(inner < per, iota(shape, 0) * per + inner, -1)
    onehot = (named == bucket[None]).astype(f32).reshape(sz.width, 3 * BLK).astype(bf16)
    table = small_t[TABLE : TABLE + 16].astype(bf16)
    values = dot_nn(table, onehot)
    values = values - values[:, 0:1]
    vector[...] = jnp.where((lane > BLK) & (lane < 2 * BLK), NEG, values)

    def tile(pair, carry):
        for b in range(2):
            row = jnp.broadcast_to(vector[pl.ds(2 * pair + b, 1), :], (BLK, 3 * BLK))
            turned = pltpu.roll(row, 0, 1, stride=1, stride_axis=0)[:, : 2 * BLK]
            tiles[pair, :, b * BLK : (b + 1) * BLK] = turned.T
        return carry

    lax.fori_loop(0, sz.pairs, tile, 0)


def forward_kernel(
    sz,
    len_ref,
    tok_ref,
    routes_ref,
    slots_ref,
    small_ref,
    wq_ref,
    wk_ref,
    wv_ref,
    wo_ref,
    cot_ref,
    w_out,
    qkv_out,
    probs_out,
    att_out,
    resid_out,
    garr_out,
    far_out,
    pick_out,
    n2_out,
    rows_out,
    cs_out,
    gate_out,
    small_out,
    pieces,
    gsend,
    relay,
    vector,
    tiles,
    probs,
    wide,
    whole,
    qkv,
    att,
    resid_all,
    pick_all,
    mask,
    send_z,
    recv_z,
    send_b,
    recv_b,
    send_c,
    recv_c,
    send_s,
    recv_s,
    send_m,
    recv_m,
    send_g,
    recv_g,
    send_p,
    keep,
    keep_rows,
):
    rep, me, core, sibling = peers(sz)
    seq, width, half, line = sz.seq, sz.width, sz.half, sz.line
    place_a = me // 4
    near = jnp.where(core == 0, 1, 2)
    last = jnp.where(core == 0, 2, 1)

    for h in range(2):
        cols = slice(h * half, (h + 1) * half)
        if sz.rows % 16 == 0:
            for m, ref in enumerate((wq_ref, wk_ref, wv_ref, wo_ref)):
                pieces[h, 0, m * sz.rows : (m + 1) * sz.rows, :] = ref[:, cols]
        else:
            stacked = [ref[:, cols].astype(f32) for ref in (wq_ref, wk_ref, wv_ref, wo_ref)]
            pieces[h, 0] = jnp.concatenate(stacked, axis=0).astype(bf16)

    greet(sz, rep, me, sibling)

    chunks = sz.chunks

    def block(ch, slot):
        lo, hi = chunks[ch]
        return pieces.at[core, slot, pl.ds(lo, hi - lo)]

    def copy_z(ch, up, source, to):
        slot = xor(source, to)
        return remote(
            block(ch, xor(source, place_a)),
            block(ch, slot),
            send_z.at[ch, up, xor(source, place_a)],
            recv_z.at[ch, slot],
            (rep, me + (to - place_a) * 4),
        )

    def copy_b(ch, i):
        return remote(
            block(ch, i),
            block(ch, line + i),
            send_b.at[ch, i],
            recv_b.at[ch, i],
            (rep, xor(me, near)),
        )

    def copy_c(ch, i):
        return remote(
            block(ch, i),
            block(ch, 2 * line + i),
            send_c.at[ch, i],
            recv_c.at[ch, i],
            (rep, xor(me, last)),
        )

    def copy_s(ch, i):
        return remote(
            block(ch, i), block(ch, i), send_s.at[ch, i], recv_s.at[ch, i], (sibling, me)
        )

    def forward_z(ch, t):
        for up, step in ((1, 1), (0, -1)):
            source = place_a - step * t
            to = place_a + step
            there = (source >= 0) & (source < line)
            onward = there & (to >= 0) & (to < line)

            @pl.when(there)
            def _(up=up, source=source, to=to, onward=onward):
                slot = xor(source, place_a)
                if t > 0:
                    remote(
                        block(ch, slot), block(ch, slot), send_z.at[ch, up, slot],
                        recv_z.at[ch, slot], (rep, me),
                    ).wait_recv()

                @pl.when(onward)
                def _():
                    copy_z(ch, up, source, to).start()

                if t > 0:
                    copy_b(ch, slot).start()
                    copy_c(ch, slot).start()
                    copy_s(ch, slot).start()

    def wait_sent_z(ch):
        for t in range(line - 1):
            for up, step in ((1, 1), (0, -1)):
                source = place_a - step * t
                to = place_a + step
                onward = (source >= 0) & (source < line) & (to >= 0) & (to < line)

                @pl.when(onward)
                def _(up=up, source=source, to=to):
                    copy_z(ch, up, source, to).wait_send()

    def start_own(ch):
        forward_z(ch, 0)
        copy_b(ch, 0).start()
        copy_c(ch, 0).start()

    def from_b(ch, i):
        copy_b(ch, i).wait_recv()
        copy_c(ch, line + i).start()
        copy_s(ch, line + i).start()

    def from_c(ch, i):
        copy_c(ch, i).wait_recv()
        copy_s(ch, 2 * line + i).start()

    def each(ch, do, start, stop):
        def one(i, carry):
            do(ch, i)
            return carry

        lax.fori_loop(start, stop, one, 0)

    def gather_stages(ch):
        def begin():
            from_b(ch, 0)
            forward_z(ch, 1)

        def middle():
            for t in range(2, line):
                forward_z(ch, t)

        return (
            begin,
            middle,
            lambda: each(ch, from_b, 1, line),
            lambda: each(ch, from_c, 0, line),
            lambda: each(ch, from_c, line, 2 * line),
        )

    def gather(ch):
        for stage in gather_stages(ch):
            stage()

    def finish(ch):
        def sent_b(i, carry):
            copy_b(ch, i).wait_send()
            return carry

        def sent_c(i, carry):
            copy_c(ch, i).wait_send()
            return carry

        def sent_s(i, carry):
            copy_s(ch, i).wait_send()
            return carry

        wait_sent_z(ch)
        lax.fori_loop(0, line, sent_b, 0)
        lax.fori_loop(0, 2 * line, sent_c, 0)
        lax.fori_loop(1, sz.group, sent_s, 0)

    def from_sibling(ch):
        def wait(i, carry):
            lo, hi = chunks[ch]
            other = pieces.at[1 - core, i, pl.ds(lo, hi - lo)]
            remote(other, other, send_s.at[ch, i], recv_s.at[ch, i], (sibling, me)).wait_recv()
            return carry

        lax.fori_loop(1, sz.group, wait, 0)

    chunk_rest, chunk_last = 0, len(chunks) - 1
    start_own(chunk_rest)

    def copy_m(k):
        return remote(
            small_ref, small_out.at[me], send_m.at[k], recv_m.at[k], (rep, xor(me, k))
        )

    def start_m(k, carry):
        copy_m(k).start()
        return carry

    lax.fori_loop(1, sz.group, start_m, 0)
    small_out[me] = small_ref[...]

    def keep_copy(n, src, dst):
        return pltpu.make_async_copy(src, dst, keep.at[n])

    places = jnp.concatenate(
        [routes_ref[...], slots_ref[...], jnp.zeros((4, seq), jnp.int32)], axis=0
    )
    places = places.astype(f32).T.astype(jnp.int32)
    route = places[:, 0:2]
    slot = places[:, 2:4]
    target = target_slots(sz, route, slot)
    first, second = target[:, 0:1], target[:, 1:2]
    wide_lane = iota((1, 256), 1)
    for j in range(sz.slots // 256):
        lane = wide_lane + j * 256
        pick = ((first == lane) | (second == lane)).astype(f32).astype(bf16)
        pick_all[:, j * 256 : (j + 1) * 256] = pick
        gsend[j * 256 : (j + 1) * 256, :] = dot_tn(pick, cot_ref[...]).astype(bf16)
    keep_copy(0, pick_all, pick_out).start()

    low_bits = lax.rem(me, 4)

    def copy_far(z):
        return remote(
            gsend.at[row_block(xor(place_a, z), 4 * sz.cap)],
            relay.at[z],
            send_g.at[4 * z],
            recv_g.at[4 * z],
            (rep, xor(me, 4 * z)),
        )

    def copy_plane(z, k):
        if z == 0:
            src = gsend.at[row_block(xor(me, k), sz.cap)]
        else:
            src = relay.at[z, row_block(xor(low_bits, k), sz.cap)]
        return remote(
            src,
            garr_out.at[pl.ds((4 * z + k) * sz.cap, sz.cap)],
            send_g.at[4 * z + k],
            recv_g.at[4 * z + k],
            (rep, xor(me, k)),
        )

    def own_rows(z):
        if z == 0:
            src = gsend.at[row_block(me, sz.cap)]
        else:
            src = relay.at[z, row_block(low_bits, sz.cap)]
        return pltpu.make_async_copy(
            src, garr_out.at[pl.ds(4 * z * sz.cap, sz.cap)], keep_rows.at[z]
        )

    def keep_far(z):
        return pltpu.make_async_copy(
            relay.at[z], far_out.at[z - line // 2], keep_rows.at[z]
        )

    def pass_on(z):
        if z > 0:
            copy_far(z).wait_recv()
        own_rows(z).start()
        for k in range(1, 4):
            copy_plane(z, k).start()

    far_order = list(range(line // 2, line)) + list(range(1, line // 2))
    begin, middle, rest_b, low_c, high_c = gather_stages(chunk_rest)
    begin()
    middle()
    rest_b()
    for z in far_order:
        copy_far(z).start()

    def wait_m(k, carry):
        remote(
            small_ref, small_out.at[xor(me, k)], send_m.at[k], recv_m.at[k], (rep, xor(me, k))
        ).wait()
        return carry

    lax.fori_loop(1, sz.group, wait_m, 0)
    small = small_out[...].astype(f32)[:, : sz.rows].reshape(width, BLK)
    small_t = small.T
    gain_one = small_t[GAIN_ONE : GAIN_ONE + 1]
    gain_two = small_t[GAIN_TWO : GAIN_TWO + 1]
    for i in range(seq // BLK):
        rows = slice(i * BLK, (i + 1) * BLK)
        x = tok_ref[rows, :].astype(f32)
        scale = lax.rsqrt(jnp.mean(x * x, axis=-1, keepdims=True) + norm_eps)
        n2_out[rows, :] = (x * scale * gain_one).astype(bf16)
    low_c()
    bias_tiles(sz, small_t, vector, tiles)
    length = len_ref[0]
    mask[...] = jnp.broadcast_to(jnp.where(iota((seq, 1), 0) < length, 0.0, NEG), (seq, BLK))
    high_c()
    from_sibling(chunk_rest)
    pass_on(0)

    def assemble(low, high):
        for place in range(sz.group):
            for h in range(2):
                source = xor(me, sz.relative(h, place))
                cols = slice(h * half, (h + 1) * half)
                if sz.rows % 16 == 0:
                    for m in range(low, high):
                        whole[m, row_block(source, sz.rows), cols] = pieces[
                            h, place, m * sz.rows : (m + 1) * sz.rows, :
                        ]
                else:
                    tall = pieces[h, place, :, :].astype(f32)
                    for m in range(low, high):
                        wide[m, row_block8(source, sz.rows), cols] = tall[
                            m * sz.rows : (m + 1) * sz.rows
                        ]
        if sz.rows % 16 != 0:
            for m in range(low, high):
                whole[m] = wide[m].astype(bf16)

    assemble(0, 3)
    keep_copy(2, whole.at[pl.ds(0, 3)], w_out.at[pl.ds(0, 3)]).start()
    for m in range(3):
        qkv[m] = dot_nn(n2_out[...], whole[m]).astype(bf16)
    keep_copy(3, qkv, qkv_out).start()

    low = iota((1, BLK), 1) < width // sz.heads
    halves = [jnp.where(low, 1.0, 0.0).astype(bf16), jnp.where(low, 0.0, 1.0).astype(bf16)]
    size = width // sz.heads

    def copy_p(pair, i):
        part = (pair, pl.ds(0, (i + 1) * BLK), pl.ds(2 * i * BLK, 2 * BLK))
        return pltpu.make_async_copy(probs.at[part], probs_out.at[part], send_p.at[pair, i])

    def attend(pair, carry):
        cols = row_block(pair, BLK)
        query = qkv[0, :, cols] * jnp.asarray(score_scale, bf16)
        key = qkv[1, :, cols]
        value_t = qkv[2, :, cols].T
        for i in range(seq // BLK):
            rows = slice(i * BLK, (i + 1) * BLK)
            keys = (i + 1) * BLK
            both = jnp.concatenate([query[rows] * halves[0], query[rows] * halves[1]], axis=0)
            scores = dot_nt(key[:keys], both)
            tile = tiles[pair]
            if i == 0:
                scores = scores + tile[BLK:]
            elif i == 1:
                scores = scores + tile
            else:
                scores = jnp.concatenate(
                    [scores[: keys - 2 * BLK], scores[keys - 2 * BLK :] + tile], axis=0
                )
            hidden = mask[:keys, :]
            scores = scores + jnp.concatenate([hidden, hidden], axis=1)
            raised = jnp.exp(scores - jnp.max(scores, axis=0, keepdims=True))
            soft = raised * (1.0 / jnp.sum(raised, axis=0, keepdims=True))
            soft = soft.astype(bf16)
            probs[pair, :keys, 2 * i * BLK : 2 * (i + 1) * BLK] = soft
            mixed = dot_nn(value_t[:, :keys], soft)
            mixed = jnp.concatenate([mixed[:size, :BLK], mixed[size:, BLK:]], axis=0)
            att[rows, cols] = mixed.T.astype(bf16)
        for i in range(seq // BLK):
            copy_p(pair, i).start()
        return carry

    lax.fori_loop(0, sz.pairs, attend, 0)
    keep_copy(4, att, att_out).start()
    assemble(3, 4)
    keep_copy(5, whole.at[pl.ds(3, 1)], w_out.at[pl.ds(3, 1)]).start()

    router = small.astype(bf16)
    for i in range(seq // BLK):
        rows = slice(i * BLK, (i + 1) * BLK)
        resid = tok_ref[rows, :].astype(f32) + dot_nn(att[rows, :], whole[3])
        resid_all[rows, :] = resid
        scale = lax.rsqrt(jnp.mean(resid * resid, axis=-1, keepdims=True) + norm_eps)
        normed = (resid * scale * gain_two).astype(bf16)
        n2_out[rows, :] = normed
        logits = dot_nn(normed, router)
        lane = iota((1, BLK), 1)
        logit = [
            jnp.sum(jnp.where(lane == route[rows, c : c + 1], logits, 0.0), axis=-1, keepdims=True)
            for c in range(2)
        ]
        share_one = 1.0 / (1.0 + jnp.exp(logit[1] - logit[0]))
        share_two = 1.0 / (1.0 + jnp.exp(logit[0] - logit[1]))
        gate_out[rows, :] = jnp.where(
            lane == 0, share_one, jnp.where(lane == 1, share_two, 0.0)
        )
    keep_copy(6, resid_all, resid_out).start()

    cs_out[...] = jnp.zeros_like(cs_out)
    normed = n2_out[...]
    combine_one = gate_out[:, 0:1]
    combine_two = gate_out[:, 1:2]
    per = 256 // sz.cap
    for j in range(sz.slots // 256):
        lane = wide_lane + j * 256
        pick = pick_all[:, j * 256 : (j + 1) * 256]
        rows_out[j * 256 : (j + 1) * 256, :] = dot_tn(pick, normed).astype(bf16)
        weight = jnp.where(first == lane, combine_one, jnp.where(second == lane, combine_two, 0.0))
        weight = jnp.sum(weight, axis=0, keepdims=True)
        for e in range(per):
            cs_out[j * per + e, 0:1, 0 : sz.cap] = weight[:, e * sz.cap : (e + 1) * sz.cap]

    for z in range(1, line // 2):
        pass_on(z)
    for z in range(line // 2, line):
        copy_far(z).wait_recv()
        keep_far(z).start()
    for z in range(line):
        if z > 0:
            copy_far(z).wait_send()
        if z < line // 2:
            own_rows(z).wait()
            for k in range(1, 4):
                copy_plane(z, k).wait()
        else:
            keep_far(z).wait()
    finish(0)

    def wait_p(pair, carry):
        for i in range(seq // BLK):
            copy_p(pair, i).wait()
        return carry

    lax.fori_loop(0, sz.pairs, wait_p, 0)
    keep_copy(0, pick_all, pick_out).wait()
    keep_copy(2, whole.at[pl.ds(0, 3)], w_out.at[pl.ds(0, 3)]).wait()
    keep_copy(3, qkv, qkv_out).wait()
    keep_copy(4, att, att_out).wait()
    keep_copy(5, whole.at[pl.ds(3, 1)], w_out.at[pl.ds(3, 1)]).wait()
    keep_copy(6, resid_all, resid_out).wait()


def vmem():
    return pl.BlockSpec(memory_space=pltpu.VMEM)


def anywhere():
    return pl.BlockSpec(memory_space=pl.ANY)


def forward_call(sz, lengths, tokens, routes, slots, small, weights, cotangent):
    seq, width, group = sz.seq, sz.width, sz.group
    shape = jax.ShapeDtypeStruct
    dma = pltpu.SemaphoreType.DMA
    wide = (4, width, width) if sz.rows % 16 else (4, 8, BLK)
    parts = len(sz.chunks)
    return pl.pallas_call(
        functools.partial(forward_kernel, sz),
        out_shape=[
            shape((4, width, width), bf16),
            shape((3, seq, width), bf16),
            shape((sz.pairs, seq, 2 * seq), bf16),
            shape((seq, width), bf16),
            shape((seq, width), f32),
            shape((sz.slots // 2, width), bf16),
            shape((sz.line // 2, 4 * sz.cap, width), bf16),
            shape((seq, sz.slots), bf16),
            shape((seq, width), bf16),
            shape((sz.slots, width), bf16),
            shape((sz.experts, 8, BLK), f32),
            shape((seq, BLK), f32),
            shape((group, sz.small, BLK), bf16),
        ],
        in_specs=[pl.BlockSpec(memory_space=pltpu.SMEM)] + [vmem()] * 9,
        out_specs=[anywhere()] * 8 + [vmem()] * 5,
        scratch_shapes=[
            pltpu.VMEM((2, group, sz.piece, sz.half), bf16),
            pltpu.VMEM((sz.slots, width), bf16),
            pltpu.VMEM((sz.line, 4 * sz.cap, width), bf16),
            pltpu.VMEM((16, 3 * BLK), f32),
            pltpu.VMEM((sz.pairs, 2 * BLK, 2 * BLK), f32),
            pltpu.VMEM((sz.pairs, seq, 2 * seq), bf16),
            pltpu.VMEM(wide, f32),
            pltpu.VMEM((4, width, width), bf16),
            pltpu.VMEM((3, seq, width), bf16),
            pltpu.VMEM((seq, width), bf16),
            pltpu.VMEM((seq, width), f32),
            pltpu.VMEM((seq, sz.slots), bf16),
            pltpu.VMEM((seq, BLK), f32),
            dma((parts, 2, sz.line)),
            dma((parts, sz.line)),
            dma((parts, sz.line)),
            dma((parts, sz.line)),
            dma((parts, 2 * sz.line)),
            dma((parts, 2 * sz.line)),
            dma((parts, group)),
            dma((parts, group)),
            dma((group,)),
            dma((group,)),
            dma((group,)),
            dma((group,)),
            dma((sz.pairs, seq // BLK)),
            dma((8,)),
            dma((sz.line,)),
        ],
        compiler_params=pltpu.CompilerParams(
            collective_id=0, has_side_effects=True, vmem_limit_bytes=VMEM_LIMIT
        ),
    )(lengths, tokens, routes, slots, small, *weights, cotangent)


def gelu_parts(v):
    density = jnp.exp2(v * v * -0.7213475204444817 - 1.3257480647361593)
    base = 1.0 + 0.23164189 * jnp.abs(v)
    t = pl.reciprocal(base, approx=True)
    t = t * (2.0 - base * t)
    poly = t * (
        0.3193815351 + t * (-0.3565637813 + t * (1.7814779373 + t * (-1.8212559795 + t * 1.3302744289)))
    )
    tail = poly * density
    below = jnp.where(v < 0.0, tail, 1.0 - tail)
    return v * below, below + v * density


def column_of(row):
    return jnp.broadcast_to(row, (BLK, BLK)).T


def expert_kernel(
    sz,
    cs_ref,
    rows_ref,
    grads_hbm,
    far_hbm,
    win_ref,
    wout_ref,
    dots_out,
    results_out,
    near_out,
    back_out,
    grad_in_out,
    grad_out_out,
    win,
    wout,
    arrived,
    scales,
    arrived_t,
    scaled,
    scaled_t,
    hidden,
    pre_grad,
    back_send,
    dots_send,
    sums,
    others,
    totals,
    grads_ref,
    results_ref,
    load,
    send_r,
    recv_r,
    send_c,
    recv_c,
    send_b,
    recv_b,
    send_d,
    recv_d,
    send_n,
    recv_n,
    send_w,
    recv_w,
    keep_w,
    keep_r,
    far_own,
    send_f,
    recv_f,
):
    rep, me, core, sibling = peers(sz)
    group, cap, width = sz.group, sz.cap, sz.width
    loads = [
        pltpu.make_async_copy(win_ref.at[0], win, load.at[0]),
        pltpu.make_async_copy(wout_ref.at[0], wout, load.at[1]),
        pltpu.make_async_copy(grads_hbm, grads_ref.at[pl.ds(0, sz.slots // 2)], load.at[2]),
        pltpu.make_async_copy(
            rows_ref.at[row_block(me, cap)], arrived.at[pl.ds(0, cap)], load.at[3]
        ),
    ]
    for copy in loads:
        copy.start()
    low_bits = lax.rem(me, 4)
    later = [
        pltpu.make_async_copy(
            far_hbm.at[n, row_block(low_bits, cap)],
            grads_ref.at[pl.ds((sz.slots // 2) + 4 * n * cap, cap)],
            far_own.at[n],
        )
        for n in range(sz.line // 2)
    ]
    for copy in later:
        copy.start()
    greet(sz, rep, me, sibling)

    def copy_f(n, k):
        return remote(
            far_hbm.at[n, row_block(xor(low_bits, k), cap)],
            grads_ref.at[pl.ds((sz.slots // 2) + (4 * n + k) * cap, cap)],
            send_f.at[n, k],
            recv_f.at[n, k],
            (rep, xor(me, k)),
        )

    def copy_r(k):
        to = xor(me, k)
        return remote(
            rows_ref.at[row_block(to, cap)], arrived.at[row_block(k, cap)],
            send_r.at[k], recv_r.at[k], (rep, to),
        )

    def copy_c(k):
        to = xor(me, k)
        return remote(cs_ref.at[to], scales.at[k], send_c.at[k], recv_c.at[k], (rep, to))

    def copy_b(k):
        return remote(
            back_send.at[row_block(k, cap)], back_out.at[row_block(me, cap)],
            send_b.at[k], recv_b.at[k], (rep, xor(me, k)),
        )

    def copy_n(k):
        return remote(
            results_ref.at[row_block(k, cap)], near_out.at[row_block(me, cap)],
            send_n.at[k], recv_n.at[k], (rep, xor(me, k)),
        )

    def copy_d(k):
        return remote(
            dots_send.at[k], dots_out.at[me], send_d.at[k], recv_d.at[k], (rep, xor(me, k))
        )

    def start_r(k, carry):
        copy_c(k).start()
        copy_r(k).start()
        return carry

    per = 256 // cap
    groups = sz.slots // 256
    early = list(range(groups // 2, groups - 1)) + list(range(0, groups // 2))
    for g in early:
        lax.fori_loop(max(g * per, 1), (g + 1) * per, start_r, 0)
    for n in range(sz.line // 2):
        for k in range(1, 4):
            copy_f(n, k).start()
    scales[0] = cs_ref[me]
    dots_send[...] = jnp.zeros_like(dots_send)
    for copy in loads:
        copy.wait()

    step = 1024

    def keep_results(g):
        span = pl.ds(g * 256, 256)
        return pltpu.make_async_copy(results_ref.at[span], results_out.at[span], keep_r.at[g])

    def rows_of(g):
        start = g * per

        def arrive(k, carry):
            copy_c(k).wait_recv()
            copy_r(k).wait_recv()
            return carry

        lax.fori_loop(max(start, 1), start + per, arrive, 0)
        for n in range(sz.line // 2):
            if (sz.slots // 2 + 4 * n * cap) // 256 == g:
                later[n].wait()
                for k in range(1, 4):
                    copy_f(n, k).wait_recv()
        span = slice(g * 256, (g + 1) * 256)
        x = arrived[span, :]
        arrived_t[:, span] = x.T
        columns = [column_of(scales[start + i, 0:1, :])[:cap, 0:1] for i in range(per)]
        column = jnp.concatenate(columns, axis=0)
        raw = grads_ref[span, :].astype(f32)
        scaled[span, :] = (raw * column).astype(bf16)
        scaled_t[:, span] = scaled[span, :].T

        def part(j, carry):
            cols = row_block(j, step)
            pre = dot_nn(arrived[span, :], win[:, cols])
            grad_hidden = dot_nn(scaled[span, :], wout[:, cols])
            act, slope = gelu_parts(pre)
            hidden[span, cols] = act.astype(bf16)
            pre_grad[span, cols] = (grad_hidden * slope).astype(bf16)
            return carry

        lax.fori_loop(0, sz.ff // step, part, 0)
        back_send[span, :] = dot_nt(pre_grad[span, :], win[...]).astype(bf16)

        def send_back(k, carry):
            copy_b(k).start()
            return carry

        lax.fori_loop(max(start, 1), start + per, send_back, 0)
        results = dot_nt(hidden[span, :], wout[...])
        results_ref[span, :] = (results * column).astype(bf16)
        if g < groups // 2:

            def send_near(k, carry):
                copy_n(k).start()
                return carry

            lax.fori_loop(max(start, 1), start + per, send_near, 0)
        else:
            keep_results(g).start()
        dots = jnp.sum(results * raw, axis=-1, keepdims=True)
        for i in range(per):
            tall = jnp.broadcast_to(dots[i * cap : (i + 1) * cap], (cap, BLK))
            if cap < BLK:
                tall = jnp.concatenate([tall, jnp.zeros((BLK - cap, BLK), f32)], axis=0)
            dots_send[start + i, 0:1, :] = tall.T[0:1, :]

        def send_dots(k, carry):
            copy_d(k).start()
            return carry

        lax.fori_loop(max(start, 1), start + per, send_dots, 0)

    def start_last():
        def sent(k, carry):
            copy_r(k).wait_send()
            return carry

        for g in early:
            lax.fori_loop(max(g * per, 1), (g + 1) * per, sent, 0)
        lax.fori_loop((groups - 1) * per, groups * per, start_r, 0)

    for g in range(groups):
        if g == 1:
            start_last()
        rows_of(g)
    own_back = pltpu.make_async_copy(
        back_send.at[pl.ds(0, cap)], back_out.at[row_block(me, cap)], load.at[4]
    )
    own_back.start()
    own_near = pltpu.make_async_copy(
        results_ref.at[pl.ds(0, cap)], near_out.at[row_block(me, cap)], load.at[5]
    )
    own_near.start()
    dots_out[me] = dots_send[0]

    size = sz.ff // sz.reps
    cut = 512 if size > 512 else size
    subs = size // cut
    pieces = sz.reps // 2 * subs

    def columns_of(parity, i):
        return pl.ds(pl.multiple_of((2 * (i // subs) + parity) * size + (i % subs) * cut, BLK), cut)

    def copy_w(m, i):
        return remote(
            sums.at[m, i], others.at[m, i], send_w.at[m, i], recv_w.at[m, i], (sibling, me)
        )

    def copy_k(m, i):
        return pltpu.make_async_copy(
            totals.at[m, i], (grad_in_out, grad_out_out)[m].at[:, pl.ds(i * cut, cut)], keep_w.at[m, i]
        )

    for i in range(pieces):
        cols = columns_of(1 - core, i)
        sums[0, i] = dot_nn(arrived_t[...], pre_grad[:, cols]).astype(bf16)
        copy_w(0, i).start()
        sums[1, i] = dot_nn(scaled_t[...], hidden[:, cols]).astype(bf16)
        copy_w(1, i).start()
    for i in range(pieces):
        cols = columns_of(core, i)
        for m, left, right in ((0, arrived_t, pre_grad), (1, scaled_t, hidden)):
            total = dot_nn(left[...], right[:, cols])
            copy_w(m, i).wait_recv()
            totals[m, i] = total + others[m, i].astype(f32)
            copy_k(m, i).start()

    def finish(k, carry):
        copy_c(k).wait_send()
        copy_b(k).wait_send()
        copy_d(k).wait_send()
        from_back = remote(
            back_send.at[row_block(k, cap)], back_out.at[row_block(xor(me, k), cap)],
            send_b.at[k], recv_b.at[k], (rep, xor(me, k)),
        )
        from_back.wait_recv()
        from_dots = remote(
            dots_send.at[k], dots_out.at[xor(me, k)], send_d.at[k], recv_d.at[k], (rep, xor(me, k))
        )
        from_dots.wait_recv()
        return carry

    lax.fori_loop(1, group, finish, 0)

    def sent_last(k, carry):
        copy_r(k).wait_send()
        return carry

    lax.fori_loop((groups - 1) * per, groups * per, sent_last, 0)

    def end_near(k, carry):
        copy_n(k).wait()
        return carry

    lax.fori_loop(1, group // 2, end_near, 0)
    for n in range(sz.line // 2):
        for k in range(1, 4):
            copy_f(n, k).wait_send()
    for g in range(groups // 2, groups):
        keep_results(g).wait()
    own_back.wait()
    own_near.wait()
    for i in range(pieces):
        for m in range(2):
            copy_w(m, i).wait_send()
            copy_k(m, i).wait()


def expert_call(sz, rows, scales, grads, far, weight_in, weight_out):
    group, width, ff, slots = sz.group, sz.width, sz.ff, sz.slots
    shape = jax.ShapeDtypeStruct
    dma = pltpu.SemaphoreType.DMA
    size = ff // sz.reps
    cut = 512 if size > 512 else size
    pieces = sz.reps // 2 * (size // cut)
    return pl.pallas_call(
        functools.partial(expert_kernel, sz),
        out_shape=[
            shape((sz.experts, 8, BLK), f32),
            shape((slots, width), bf16),
            shape((slots, width), bf16),
            shape((slots, width), bf16),
            shape((width, ff // 2), f32),
            shape((width, ff // 2), f32),
        ],
        in_specs=[vmem()] + [anywhere()] * 5,
        out_specs=[vmem()] + [anywhere()] * 5,
        scratch_shapes=[
            pltpu.VMEM((width, ff), bf16),
            pltpu.VMEM((width, ff), bf16),
            pltpu.VMEM((slots, width), bf16),
            pltpu.VMEM((group, 8, BLK), f32),
            pltpu.VMEM((width, slots), bf16),
            pltpu.VMEM((slots, width), bf16),
            pltpu.VMEM((width, slots), bf16),
            pltpu.VMEM((slots, ff), bf16),
            pltpu.VMEM((slots, ff), bf16),
            pltpu.VMEM((slots, width), bf16),
            pltpu.VMEM((group, 8, BLK), f32),
            pltpu.VMEM((2, pieces, width, cut), bf16),
            pltpu.VMEM((2, pieces, width, cut), bf16),
            pltpu.VMEM((2, pieces, width, cut), f32),
            pltpu.VMEM((slots, width), bf16),
            pltpu.VMEM((slots, width), bf16),
            dma((6,)),
        ]
        + [dma((group,))] * 10
        + [dma((2, pieces))] * 3
        + [dma((slots // 256,)), dma((sz.line // 2,)), dma((sz.line // 2, 4)), dma((sz.line // 2, 4))],
        compiler_params=pltpu.CompilerParams(
            collective_id=1, has_side_effects=True, vmem_limit_bytes=VMEM_LIMIT
        ),
    )(scales, rows, grads, far, weight_in, weight_out)


def near_onehot(sz):
    lane = iota((1, 3 * BLK), 1)
    distance = jnp.where(lane <= BLK, BLK + lane, lane - 2 * BLK)
    bucket = jnp.where(distance < 16, distance, 16)
    for cutoff in cutoffs:
        bucket = bucket + (distance >= cutoff).astype(jnp.int32)
    per = sz.buckets // sz.group
    shape = (sz.group, sz.rows, 3 * BLK)
    inner = iota(shape, 1)
    named = jnp.where(inner < per, iota(shape, 0) * per + inner, -1)
    return (named == bucket[None]).astype(f32).reshape(sz.width, 3 * BLK).astype(bf16)


def unit_shapes(sz):
    up = lambda n: -(-n // 16) * 16
    return [(up(sz.rows), sz.half)] + [(up(3 * sz.rows), BLK)] * (sz.half // BLK)


def backward_kernel(
    sz,
    len_ref,
    tok_ref,
    cot_ref,
    routes_ref,
    slots_ref,
    n2_ref,
    gate_ref,
    small_ref,
    dots_ref,
    w_hbm,
    qkv_hbm,
    probs_hbm,
    att_hbm,
    resid_hbm,
    pick_hbm,
    results_hbm,
    near_hbm,
    back_hbm,
    out_ref,
    gtok_ref,
    gq_ref,
    gk_ref,
    gv_ref,
    go_ref,
    gsmall_ref,
    *scratch,
):
    units = unit_shapes(sz)
    (
        probs, w_ref, qkv_ref, att_ref, resid_ref, pick_ref, back_ref, returned, total_bf, gres, gatt,
        dqkv, dscore, stacks, normed, normed_t, near_sum, far_sum, sums, wide, packed, packed_rows,
        packed_far, small_mine, small_from, small_final,
        load, load_p, send_r, recv_r, send_x, recv_x, send_m, recv_m,
    ) = scratch[:34]
    buffers = scratch[34:]
    mine = buffers[0::6]
    theirs = buffers[1::6]
    from_sib = buffers[2::6]
    from_one = buffers[3::6]
    from_two = buffers[4::6]
    final = buffers[5::6]
    rep, me, core, sibling = peers(sz)
    seq, width, half, line, group = sz.seq, sz.width, sz.half, sz.line, sz.group
    near = jnp.where(core == 0, 1, 2)
    last = jnp.where(core == 0, 2, 1)
    cap = sz.cap
    blocks = seq // BLK

    def fetch(n, src, dst):
        return pltpu.make_async_copy(src, dst, load.at[n])

    same_half = row_block(lax.div(me, group // 2), sz.slots // 2)
    loads = [
        fetch(0, back_hbm, back_ref),
        fetch(1, pick_hbm, pick_ref),
        fetch(2, resid_hbm, resid_ref),
        fetch(3, w_hbm.at[3], w_ref.at[3]),
        fetch(4, att_hbm, att_ref),
        fetch(5, qkv_hbm, qkv_ref),
        fetch(6, w_hbm.at[pl.ds(0, 3)], w_ref.at[pl.ds(0, 3)]),
        fetch(7, near_hbm.at[same_half], returned.at[same_half]),
    ]

    def copy_p(pair, i):
        part = (pair, pl.ds(0, (i + 1) * BLK), pl.ds(2 * i * BLK, 2 * BLK))
        return pltpu.make_async_copy(probs_hbm.at[part], probs.at[part], load_p.at[pair, i])

    def start_p(pair, carry):
        for i in range(blocks):
            copy_p(pair, i).start()
        return carry

    for copy in loads[:6]:
        copy.start()
    lax.fori_loop(0, sz.pairs, start_p, 0)
    for copy in loads[6:]:
        copy.start()
    greet(sz, rep, me, sibling)

    def copy_r(k, owner):
        return remote(
            results_hbm.at[row_block(k, cap)], returned.at[row_block(owner, cap)],
            send_r.at[k], recv_r.at[k], (rep, xor(me, k)),
        )

    def start_r(k, carry):
        copy_r(k, me).start()
        return carry

    lax.fori_loop(group // 2, group, start_r, 0)

    def copy_x(u, stage):
        if stage == 0:
            src, dst, to = theirs[u], from_sib[u], (sibling, me)
        elif stage == 1:
            src, dst, to = mine[u].at[pl.ds(group // 2, group // 2)], from_one[u], (rep, xor(me, last))
        elif stage == 2:
            src, dst, to = mine[u].at[pl.ds(line, line)], from_two[u].at[pl.ds(0, line)], (rep, xor(me, near))
        elif stage == 3:
            src, dst, to = final[u].at[core], final[u].at[core], (sibling, me)
        else:
            z = stage - 3
            src, dst, to = mine[u].at[z], from_two[u].at[line + z], (rep, xor(me, 4 * z))
        return remote(src, dst, send_x.at[u, stage], recv_x.at[u, stage], to)

    def add_into(ref, start, stop, other, skip=0):
        def add(p, carry):
            ref[p] = (ref[p].astype(f32) + other[p + skip].astype(f32)).astype(bf16)
            return carry

        lax.fori_loop(start, stop, add, 0)

    def step(u, number):
        if number == 0:
            copy_x(u, 0).start()
        elif number == 1:
            copy_x(u, 0).wait_recv()
            add_into(mine[u], group // 2, group, from_sib[u])
            copy_x(u, 1).start()
            add_into(mine[u], 0, group // 2, from_sib[u])
        elif number == 2:
            copy_x(u, 1).wait_recv()
            add_into(mine[u], line, 2 * line, from_one[u])
            copy_x(u, 2).start()
            add_into(mine[u], 0, line, from_one[u])
        elif number == 3:
            copy_x(u, 2).wait_recv()
            add_into(mine[u], 0, line, from_two[u])
            for z in range(1, line):
                copy_x(u, 3 + z).start()
        elif number == 4:
            total = mine[u][0].astype(f32)
            for z in range(1, line):
                copy_x(u, 3 + z).wait_recv()
                total = total + from_two[u][line + z].astype(f32)
            final[u][core] = total
            copy_x(u, 3).start()
        else:
            remote(
                final[u].at[1 - core], final[u].at[1 - core], send_x.at[u, 3], recv_x.at[u, 3],
                (sibling, me),
            ).wait_recv()
            for stage in range(3 + line):
                copy_x(u, stage).wait_send()

    def owner_of(p, swap):
        one, two = (last, near) if swap else (near, last)
        rel = lax.rem(p, line) * 4 + lax.rem(lax.div(p, line), 2) * one + lax.div(p, 2 * line) * two
        return xor(me, rel)

    def fill(u, read):
        def put(p, carry):
            mine[u][p] = read(core, owner_of(p, False)).astype(bf16)
            theirs[u][p] = read(1 - core, owner_of(p, True)).astype(bf16)
            return carry

        lax.fori_loop(0, group, put, 0)

    def padded(value, u):
        short = units[u][0] - value.shape[0]
        if short:
            value = jnp.concatenate([value, jnp.zeros((short, value.shape[1]), f32)], axis=0)
        return value

    small = small_ref[...].astype(f32)[:, : sz.rows].reshape(width, BLK)
    small_t = small.T
    gain_one = small_t[GAIN_ONE : GAIN_ONE + 1]
    gain_two = small_t[GAIN_TWO : GAIN_TWO + 1]
    router = small.astype(bf16)
    length = len_ref[0]

    places = jnp.concatenate(
        [routes_ref[...], slots_ref[...], jnp.zeros((4, seq), jnp.int32)], axis=0
    )
    places = places.astype(f32).T.astype(jnp.int32)
    route = places[:, 0:2]
    target = target_slots(sz, route, places[:, 2:4])
    first, second = target[:, 0:1], target[:, 1:2]
    dot_one = jnp.zeros((seq, BLK), f32)
    dot_two = jnp.zeros((seq, BLK), f32)
    lanes = iota((1, BLK), 1)
    per = BLK // cap
    for j in range(sz.slots // BLK):
        row = jnp.concatenate([dots_ref[j * per + e, 0:1, 0:cap] for e in range(per)], axis=1)
        lane = lanes + j * BLK
        dot_one = dot_one + jnp.where(first == lane, row, 0.0)
        dot_two = dot_two + jnp.where(second == lane, row, 0.0)
    dot_one = jnp.sum(dot_one, axis=-1, keepdims=True)
    dot_two = jnp.sum(dot_two, axis=-1, keepdims=True)
    share = gate_ref[:, 0:1] * gate_ref[:, 1:2] * (dot_one - dot_two)
    grad_logits = share * (
        (lanes == route[:, 0:1]).astype(f32) - (lanes == route[:, 1:2]).astype(f32)
    )
    grad_logits = grad_logits.astype(bf16)
    packed[...] = dot_tn(n2_ref[...], grad_logits)

    for copy in loads[:3]:
        copy.wait()
    gain_two_grad = jnp.zeros((1, width), f32)
    for i in range(blocks):
        rows = slice(i * BLK, (i + 1) * BLK)
        grad = dot_nn(pick_ref[rows, :], back_ref[...]) + dot_nt(grad_logits[rows], router)
        resid = resid_ref[rows, :]
        scale = lax.rsqrt(jnp.mean(resid * resid, axis=-1, keepdims=True) + norm_eps)
        gain_two_grad = gain_two_grad + jnp.sum(grad * resid * scale, axis=0, keepdims=True)
        valid = (iota((BLK, 1), 0) + i * BLK < length).astype(f32)
        grad_out = cot_ref[rows, :].astype(f32) * valid
        moved = grad * gain_two
        mean = jnp.mean(moved * resid, axis=-1, keepdims=True)
        total = grad_out + scale * moved - resid * (scale * scale * scale * mean)
        gres[rows, :] = total
        total_bf[rows, :] = total.astype(bf16)
    loads[3].wait()
    loads[4].wait()
    gatt[...] = dot_nt(total_bf[...], w_ref[3]).astype(bf16)
    wide[...] = dot_tn(att_ref[...], total_bf[...])

    def read_o(h, s):
        cols = pl.ds(pl.multiple_of(h * half, BLK), half)
        return padded(wide[row_block8(s, sz.rows), cols], 0)

    fill(0, read_o)
    step(0, 0)

    for i in range(blocks):
        rows = slice(i * BLK, (i + 1) * BLK)
        x = tok_ref[rows, :].astype(f32)
        scale = lax.rsqrt(jnp.mean(x * x, axis=-1, keepdims=True) + norm_eps)
        normed[rows, :] = (x * scale * gain_one).astype(bf16)
    normed_t[...] = normed[...].T
    step(0, 1)

    low = iota((1, BLK), 1) < width // sz.heads
    halves = [jnp.where(low, 1.0, 0.0).astype(bf16), jnp.where(low, 0.0, 1.0).astype(bf16)]

    size = width // sz.heads
    loads[5].wait()

    def back_pair(pair):
        cols = row_block(pair, BLK)
        query = qkv_ref[0, :, cols]
        key = qkv_ref[1, :, cols]
        key_t = key.T
        value = qkv_ref[2, :, cols]
        grads = gatt[:, cols]
        for i in range(blocks):
            copy_p(pair, i).wait()
        for i in range(blocks):
            rows = slice(i * BLK, (i + 1) * BLK)
            keys = (i + 1) * BLK
            at = slice(2 * i * BLK, 2 * (i + 1) * BLK)
            both = jnp.concatenate([grads[rows] * halves[0], grads[rows] * halves[1]], axis=0)
            stacks[0, at, :] = jnp.concatenate(
                [query[rows] * halves[0], query[rows] * halves[1]], axis=0
            )
            stacks[1, at, :] = both
            soft = probs[pair, :keys, at].astype(f32)
            product = soft * dot_nt(value[:keys], both)
            grad_score = product - soft * jnp.sum(product, axis=0, keepdims=True)
            if i == 0:
                near_sum[pair, :BLK] = jnp.zeros((BLK, 2 * BLK), f32)
                near_sum[pair, BLK:] = grad_score
                far_sum[pair] = jnp.zeros((8, 2 * BLK), f32)
            else:
                near_sum[pair] += grad_score[keys - 2 * BLK :]
                if i >= 2:
                    far = grad_score[: keys - 2 * BLK].reshape((keys - 2 * BLK) // 8, 8, 2 * BLK)
                    far_sum[pair] += jnp.sum(far, axis=0)
            low_score = grad_score.astype(bf16)
            dscore[:keys, at] = low_score
            moved = dot_nn(key_t[:, :keys], low_score)
            moved = jnp.concatenate([moved[:size, :BLK], moved[size:, BLK:]], axis=0)
            dqkv[0, rows, cols] = (moved.T * score_scale).astype(bf16)
        for i in range(blocks):
            rows = slice(i * BLK, (i + 1) * BLK)
            below = slice(2 * i * BLK, 2 * seq)
            grad_key = dot_nn(dscore[rows, below], stacks[0, below, :])
            grad_value = dot_nn(probs[pair, rows, below], stacks[1, below, :])
            dqkv[1, rows, cols] = (grad_key * score_scale).astype(bf16)
            dqkv[2, rows, cols] = grad_value.astype(bf16)

    parts = half // BLK
    for j in range(parts):

        def one(h, carry, j=j):
            pair = h * parts + j
            back_pair(pair)
            cols = row_block(pair, BLK)
            grads = jnp.concatenate([dqkv[m, :, cols] for m in range(3)], axis=1)
            sums[h] = dot_nn(normed_t[...], grads)
            return carry

        one(0, 0)
        for u, n in PLAN_H[j]:
            step(u, n)
        one(1, 0)

        def read_j(h, s):
            rows = row_block8(s, sz.rows)
            value = sums[h, rows, :]
            return padded(
                jnp.concatenate([value[:, m * BLK : (m + 1) * BLK] for m in range(3)], axis=0), 1
            )

        fill(1 + j, read_j)
        for u, n in PLAN_J[j]:
            step(u, n)

    loads[6].wait()
    gain_one_grads = []

    def input_grad(i):
        rows = slice(i * BLK, (i + 1) * BLK)
        grad = dot_nt(dqkv[0, rows, :], w_ref[0]) + dot_nt(dqkv[1, rows, :], w_ref[1])
        grad = grad + dot_nt(dqkv[2, rows, :], w_ref[2])
        x = tok_ref[rows, :].astype(f32)
        scale = lax.rsqrt(jnp.mean(x * x, axis=-1, keepdims=True) + norm_eps)
        gain_one_grads.append(jnp.sum(grad * x * scale, axis=0, keepdims=True))
        moved = grad * gain_one
        mean = jnp.mean(moved * x, axis=-1, keepdims=True)
        gtok_ref[rows, :] = gres[rows, :] + scale * moved - x * (scale * scale * scale * mean)

    flip = (iota((2 * BLK, 2 * BLK), 0) + iota((2 * BLK, 2 * BLK), 1) == 2 * BLK - 1)
    flip = flip.astype(f32).astype(bf16)

    def bucket_sums(pair, carry):
        turned = dot_nn(flip, near_sum[pair].astype(bf16))
        far = jnp.sum(far_sum[pair], axis=0, keepdims=True)
        for b in range(2):
            tall = jnp.concatenate(
                [turned[:, b * BLK : (b + 1) * BLK], jnp.zeros((2 * BLK, 2 * BLK), f32)], axis=1
            )
            rolled = pltpu.roll(tall, BLK + 1, 1, stride=1, stride_axis=0)
            packed_rows[pl.ds(2 * pair + b, 1), :] = jnp.sum(rolled, axis=0, keepdims=True)
            packed_far[pl.ds(2 * pair + b, 1), :] = far[:, b * BLK : (b + 1) * BLK]
        return carry

    def table_grad():
        packed_rows[...] = jnp.zeros_like(packed_rows)
        packed_far[...] = jnp.zeros_like(packed_far)
        lax.fori_loop(0, sz.pairs, bucket_sums, 0)
        onehot = near_onehot(sz)
        values = packed_rows[...]
        upper = values.astype(bf16)
        lower = (values - upper.astype(f32)).astype(bf16)
        table = dot_nt(upper, onehot) + dot_nt(lower, onehot)
        far = jnp.sum(packed_far[...], axis=-1, keepdims=True)
        one_far = jnp.broadcast_to((lanes == 0).astype(f32), (8, BLK)).astype(bf16)
        farthest = dot_nt(one_far, onehot[:, :BLK])[0:1]
        return table + far * farthest

    def copy_m(k):
        return remote(
            small_mine.at[xor(me, k)], small_from.at[k], send_m.at[k], recv_m.at[k], (rep, xor(me, k))
        )

    def small_start(table):
        gain_one_grad = gain_one_grads[0]
        for grad in gain_one_grads[1:]:
            gain_one_grad = gain_one_grad + grad
        tall = jnp.concatenate(
            [
                jnp.zeros((GAIN_ONE, width), f32),
                gain_one_grad,
                gain_two_grad,
                jnp.zeros((TABLE - GAIN_TWO - 1, width), f32),
                table,
                jnp.zeros((BLK - TABLE - 16, width), f32),
            ],
            axis=0,
        )
        whole = (packed[...] + tall.T).reshape(group, sz.rows, BLK)
        if sz.small != sz.rows:
            whole = jnp.concatenate(
                [whole, jnp.zeros((group, sz.small - sz.rows, BLK), f32)], axis=1
            )
        small_mine[...] = whole.astype(bf16)

        def start_m(k, carry):
            copy_m(k).start()
            return carry

        lax.fori_loop(1, group, start_m, 0)

    def copy_f():
        return remote(
            small_final.at[core], small_final.at[core], send_m.at[0], recv_m.at[0], (sibling, me)
        )

    def small_sum():
        small_final[core] = small_mine[me].astype(f32)

        def add(k, carry):
            copy_m(k).wait()
            small_final[core] += small_from[k].astype(f32)
            return carry

        lax.fori_loop(1, group, add, 0)
        copy_f().start()

    def small_end():
        remote(
            small_final.at[1 - core], small_final.at[1 - core], send_m.at[0], recv_m.at[0],
            (sibling, me),
        ).wait_recv()
        gsmall_ref[...] = small_final[0] + small_final[1]
        copy_f().wait_send()

    def results():
        def wait_r(k, carry):
            copy_r(k, xor(me, k)).wait_recv()
            return carry

        lax.fori_loop(group // 2, group, wait_r, 0)
        loads[7].wait()
        for i in range(blocks):
            rows = slice(i * BLK, (i + 1) * BLK)
            valid = (iota((BLK, 1), 0) + i * BLK < length).astype(f32)
            total = resid_ref[rows, :] + dot_nn(pick_ref[rows, :], returned[...])
            out_ref[rows, :] = (total * valid).astype(bf16)

    table = None
    for act in PLAN_T:
        if act == "T":
            table = table_grad()
        elif act == "M":
            small_start(table)
        elif act == "R":
            results()
        elif act == "m":
            small_sum()
        elif act == "e":
            small_end()
        elif isinstance(act, int):
            input_grad(act)
        else:
            step(*act)
    for u in range(1, 1 + parts):
        step(u, 5)
    for h in range(2):
        cols = slice(h * half, (h + 1) * half)
        go_ref[:, cols] = final[0][h, : sz.rows]
        for j in range(parts):
            at = slice(h * half + j * BLK, h * half + (j + 1) * BLK)
            for m, ref in enumerate((gq_ref, gk_ref, gv_ref)):
                ref[:, at] = final[1 + j][h, m * sz.rows : (m + 1) * sz.rows]

    def sent_r(k, carry):
        copy_r(k, me).wait_send()
        return carry

    lax.fori_loop(group // 2, group, sent_r, 0)


def backward_call(sz, lengths, tokens, cotangent, routes, slots, saved, results, near, back, dots):
    seq, width, group, line = sz.seq, sz.width, sz.group, sz.line
    shape = jax.ShapeDtypeStruct
    dma = pltpu.SemaphoreType.DMA
    w, qkv, probs, att, resid, pick, n2, gate, small = saved
    units = unit_shapes(sz)
    buffers = []
    for rows, cols in units:
        buffers += [
            pltpu.VMEM((group, rows, cols), bf16),
            pltpu.VMEM((group, rows, cols), bf16),
            pltpu.VMEM((group, rows, cols), bf16),
            pltpu.VMEM((group // 2, rows, cols), bf16),
            pltpu.VMEM((2 * line, rows, cols), bf16),
            pltpu.VMEM((2, rows, cols), f32),
        ]
    dense = shape((sz.rows, width), f32)
    return pl.pallas_call(
        functools.partial(backward_kernel, sz),
        out_shape=[
            shape((seq, width), bf16),
            shape((seq, width), f32),
            dense,
            dense,
            dense,
            dense,
            shape((sz.small, BLK), f32),
        ],
        in_specs=[pl.BlockSpec(memory_space=pltpu.SMEM)] + [vmem()] * 8 + [anywhere()] * 9,
        out_specs=[vmem()] * 7,
        scratch_shapes=[
            pltpu.VMEM((sz.pairs, seq, 2 * seq), bf16),
            pltpu.VMEM((4, width, width), bf16),
            pltpu.VMEM((3, seq, width), bf16),
            pltpu.VMEM((seq, width), bf16),
            pltpu.VMEM((seq, width), f32),
            pltpu.VMEM((seq, sz.slots), bf16),
            pltpu.VMEM((sz.slots, width), bf16),
            pltpu.VMEM((sz.slots, width), bf16),
            pltpu.VMEM((seq, width), bf16),
            pltpu.VMEM((seq, width), f32),
            pltpu.VMEM((seq, width), bf16),
            pltpu.VMEM((3, seq, width), bf16),
            pltpu.VMEM((seq, 2 * seq), bf16),
            pltpu.VMEM((2, 2 * seq, BLK), bf16),
            pltpu.VMEM((seq, width), bf16),
            pltpu.VMEM((width, seq), bf16),
            pltpu.VMEM((sz.pairs, 2 * BLK, 2 * BLK), f32),
            pltpu.VMEM((sz.pairs, 8, 2 * BLK), f32),
            pltpu.VMEM((2, width, 3 * BLK), f32),
            pltpu.VMEM((width, width), f32),
            pltpu.VMEM((width, BLK), f32),
            pltpu.VMEM((16, 3 * BLK), f32),
            pltpu.VMEM((16, BLK), f32),
            pltpu.VMEM((group, sz.small, BLK), bf16),
            pltpu.VMEM((group, sz.small, BLK), bf16),
            pltpu.VMEM((2, sz.small, BLK), f32),
            dma((8,)),
            dma((sz.pairs, seq // BLK)),
            dma((group,)),
            dma((group,)),
            dma((len(units), 3 + line)),
            dma((len(units), 3 + line)),
            dma((group,)),
            dma((group,)),
        ]
        + buffers,
        compiler_params=pltpu.CompilerParams(
            collective_id=2, has_side_effects=True, vmem_limit_bytes=VMEM_LIMIT
        ),
    )(
        lengths, tokens, cotangent, routes, slots, n2, gate, small, dots, w, qkv, probs, att, resid,
        pick, results, near, back,
    )


def shards(
    tokens, lengths, routes, slots, norm_one, w_query, w_key, w_value, w_output, bias_table, norm_two,
    router, expert_in, expert_out, cotangent, *, reps, group,
):
    seq, width = tokens.shape
    rows = w_query.shape[0]
    heads = bias_table.shape[1]
    experts = router.shape[1]
    sz = Sizes(
        reps, group, seq, width, heads, experts, expert_in.shape[2], rows, bias_table.shape[0] * group
    )
    fill = lambda count: jnp.zeros((rows, count), bf16)
    few = bias_table.shape[0]
    small = jnp.concatenate(
        [
            router,
            fill(GAIN_ONE - experts),
            norm_one[:, None],
            norm_two[:, None],
            fill(TABLE - GAIN_TWO - 1),
            jnp.pad(bias_table, ((0, rows - few), (0, BLK - TABLE - heads))),
        ],
        axis=1,
    )
    small = jnp.pad(small, ((0, sz.small - rows), (0, 0)))
    weights = (w_query, w_key, w_value, w_output)
    routes, slots = routes.T, slots.T
    (w, qkv, probs, att, resid, grads, far, pick, n2, sent, scales, gate, small_all) = forward_call(
        sz, lengths, tokens, routes, slots, small, weights, cotangent
    )
    dots, results, near, back, grad_in, grad_out = expert_call(sz, sent, scales, grads, far, expert_in, expert_out)
    saved = (w, qkv, probs, att, resid, pick, n2, gate, small_all)
    output, grad_tokens, gq, gk, gv, go, gsmall = backward_call(
        sz, lengths, tokens, cotangent, routes, slots, saved, results, near, back, dots
    )
    grad_in, grad_out = grad_in[None], grad_out[None]
    if reps > 2:
        same = [[r for r in range(reps) if r % 2 == c] for c in range(2)]
        grad_in, grad_out = (
            lax.psum_scatter(
                grad, "rep", scatter_dimension=2, axis_index_groups=same, tiled=True
            )
            for grad in (grad_in, grad_out)
        )
        gq, gk, gv, go, gsmall = lax.psum(
            (gq, gk, gv, go, gsmall), "rep", axis_index_groups=same
        )
    return (
        output,
        grad_tokens,
        gsmall[:rows, GAIN_ONE],
        gq,
        gk,
        gv,
        go,
        gsmall[: bias_table.shape[0], TABLE : TABLE + heads],
        gsmall[:rows, GAIN_TWO],
        gsmall[:rows, :experts],
        grad_in,
        grad_out,
    )


def solution(mesh):
    both = ("rep", "shard")
    return jax.shard_map(
        functools.partial(shards, reps=mesh.shape["rep"], group=mesh.shape["shard"]),
        mesh=mesh,
        in_specs=(
            P(both, None),
            P(both),
            P(both, None),
            P(both, None),
            P("shard"),
            P("shard", None),
            P("shard", None),
            P("shard", None),
            P("shard", None),
            P("shard", None),
            P("shard"),
            P("shard", None),
            P("shard", None, None),
            P("shard", None, None),
            P(both, None),
        ),
        out_specs=(
            P(both, None),
            P(both, None),
            P("shard"),
            P("shard", None),
            P("shard", None),
            P("shard", None),
            P("shard", None),
            P("shard", None),
            P("shard"),
            P("shard", None),
            P("shard", None, "rep"),
            P("shard", None, "rep"),
        ),
        check_vma=False,
    )
```

```python
import functools

import jax
import jax.numpy as jnp
from jax import lax
from jax.experimental import pallas as pl
from jax.experimental.pallas import tpu as pltpu
from jax.sharding import PartitionSpec as P

MESH = pl.DeviceIdType.MESH
norm_eps = 1e-06
score_scale = 0.125
cutoffs = (19, 21, 24, 27, 31, 35, 40, 46, 52, 59, 67, 77, 87, 99, 113)
f32 = jnp.float32
bf16 = jnp.bfloat16
GAIN_ONE, GAIN_TWO, TABLE = 64, 65, 80
BLK = 128
VMEM_LIMIT = 60 * 2**20
NEG = -1e30
PLAN_H = ((), ((1, 1),), ((2, 1),))
PLAN_J = (((1, 0),), ((2, 0),), ((3, 0), (1, 2), (0, 2)))
PLAN_T = (
    "T", (3, 1), (2, 2), 0, (1, 3), (0, 3), 1, (3, 2), (2, 3), 2, 3, "M", (3, 3), (1, 4), (0, 4), "R", "m", (2, 4),
    (0, 5), (3, 4), "e",
)


def dot_nn(a, b):
    return lax.dot_general(a, b, (((1,), (0,)), ((), ())), preferred_element_type=f32)


def dot_nt(a, b):
    return lax.dot_general(a, b, (((1,), (1,)), ((), ())), preferred_element_type=f32)


def dot_tn(a, b):
    return lax.dot_general(a, b, (((0,), (0,)), ((), ())), preferred_element_type=f32)


def iota(shape, dim):
    return lax.broadcasted_iota(jnp.int32, shape, dim)


class Sizes:
    def __init__(self, reps, group, seq, width, heads, experts, ff, rows, buckets):
        self.reps, self.group, self.seq, self.width = reps, group, seq, width
        self.heads, self.experts, self.ff, self.rows = heads, experts, ff, rows
        self.buckets = buckets
        self.cap = 2 * seq // experts
        self.slots = experts * self.cap
        self.line = group // 4
        self.half = width // 2
        self.small = -(-rows // 16) * 16
        self.share = self.small // 16
        self.piece = 4 * rows
        self.pairs = heads // 2
        self.chunks = ((0, self.piece),)

    def relative(self, half, place):
        first, second = (1, 2) if half == 0 else (2, 1)
        line = place % self.line
        return line * 4 + (place // self.line % 2) * first + (place // (2 * self.line)) * second


def peers(sz):
    rep = lax.axis_index("rep")
    me = lax.axis_index("shard")
    return rep, me, lax.rem(rep, 2), rep + 1 - 2 * lax.rem(rep, 2)


def xor(a, b):
    return jnp.bitwise_xor(a, b)


def greet(sz, rep, me, sibling):
    barrier = pltpu.get_barrier_semaphore()

    def signal(k, carry):
        pl.semaphore_signal(barrier, inc=1, device_id=(rep, xor(me, k)), device_id_type=MESH)
        return carry

    lax.fori_loop(1, sz.group, signal, 0)
    pl.semaphore_signal(barrier, inc=1, device_id=(sibling, me), device_id_type=MESH)
    pl.semaphore_wait(barrier, sz.group)


def remote(src, dst, send, recv, device):
    return pltpu.make_async_remote_copy(
        src_ref=src, dst_ref=dst, send_sem=send, recv_sem=recv, device_id=device, device_id_type=MESH
    )


def send_order(group):
    order = list(range(group // 2, group)) + list(range(1, group // 2))
    return order


def row_block(index, size):
    return pl.ds(pl.multiple_of(index * size, size), size)


def row_block8(index, size):
    return pl.ds(pl.multiple_of(index * size, 8), size)


def target_slots(sz, routes, slots):
    return jnp.where(slots < sz.cap, routes * sz.cap + slots, -1)


def bias_tiles(sz, small_t, vector, tiles):
    lane = iota((1, 3 * BLK), 1)
    distance = jnp.where(lane <= BLK, BLK - lane, 4 * BLK - lane)
    bucket = jnp.where(distance < 16, distance, 16)
    for cutoff in cutoffs:
        bucket = bucket + (distance >= cutoff).astype(jnp.int32)
    per = sz.buckets // sz.group
    shape = (sz.group, sz.rows, 3 * BLK)
    inner = iota(shape, 1)
    named = jnp.where(inner < per, iota(shape, 0) * per + inner, -1)
    onehot = (named == bucket[None]).astype(f32).reshape(sz.width, 3 * BLK).astype(bf16)
    table = small_t[TABLE : TABLE + 16].astype(bf16)
    values = dot_nn(table, onehot)
    values = values - values[:, 0:1]
    vector[...] = jnp.where((lane > BLK) & (lane < 2 * BLK), NEG, values)

    def tile(pair, carry):
        for b in range(2):
            row = jnp.broadcast_to(vector[pl.ds(2 * pair + b, 1), :], (BLK, 3 * BLK))
            turned = pltpu.roll(row, 0, 1, stride=1, stride_axis=0)[:, : 2 * BLK]
            tiles[pair, :, b * BLK : (b + 1) * BLK] = turned.T
        return carry

    lax.fori_loop(0, sz.pairs, tile, 0)


def forward_kernel(
    sz,
    len_ref,
    tok_ref,
    routes_ref,
    slots_ref,
    one_ref,
    two_ref,
    router_ref,
    table_ref,
    wq_ref,
    wk_ref,
    wv_ref,
    wo_ref,
    cot_ref,
    w_out,
    qkv_out,
    probs_out,
    att_out,
    resid_out,
    garr_out,
    far_out,
    pick_out,
    n2_out,
    rows_out,
    cs_out,
    gate_out,
    small_out,
    pieces,
    gsend,
    relay,
    vector,
    tiles,
    probs,
    wide,
    whole,
    qkv,
    att,
    resid_all,
    pick_all,
    mask,
    send_z,
    recv_z,
    send_b,
    recv_b,
    send_c,
    recv_c,
    send_s,
    recv_s,
    send_m,
    recv_m,
    send_g,
    recv_g,
    send_p,
    keep,
    keep_rows,
    small_ref,
    small_wide,
    small_tall,
):
    rep, me, core, sibling = peers(sz)
    seq, width, half, line = sz.seq, sz.width, sz.half, sz.line
    place_a = me // 4
    near = jnp.where(core == 0, 1, 2)
    last = jnp.where(core == 0, 2, 1)

    small_wide[...] = jnp.zeros_like(small_wide)
    small_wide[0 : sz.experts, 0 : sz.rows] = router_ref[...].astype(f32)
    small_wide[GAIN_ONE : GAIN_ONE + 1, 0 : sz.rows] = one_ref[...].astype(f32)
    small_wide[GAIN_TWO : GAIN_TWO + 1, 0 : sz.rows] = two_ref[...].astype(f32)
    few = table_ref.shape[0]
    small_ref[...] = small_wide[...].T[: sz.small].astype(bf16)
    table = table_ref[...].astype(f32)
    small_tall[...] = small_ref[...].astype(f32)
    small_tall[0:few, TABLE : TABLE + sz.heads] = table
    small_ref[...] = small_tall[...].astype(bf16)

    for h in range(2):
        cols = slice(h * half, (h + 1) * half)
        if sz.rows % 16 == 0:
            for m, ref in enumerate((wq_ref, wk_ref, wv_ref, wo_ref)):
                pieces[h, 0, m * sz.rows : (m + 1) * sz.rows, :] = ref[:, cols]
        else:
            stacked = [ref[:, cols].astype(f32) for ref in (wq_ref, wk_ref, wv_ref, wo_ref)]
            pieces[h, 0] = jnp.concatenate(stacked, axis=0).astype(bf16)

    greet(sz, rep, me, sibling)

    chunks = sz.chunks

    def block(ch, slot):
        lo, hi = chunks[ch]
        return pieces.at[core, slot, pl.ds(lo, hi - lo)]

    def copy_z(ch, up, source, to):
        slot = xor(source, to)
        return remote(
            block(ch, xor(source, place_a)),
            block(ch, slot),
            send_z.at[ch, up, xor(source, place_a)],
            recv_z.at[ch, slot],
            (rep, me + (to - place_a) * 4),
        )

    def copy_b(ch, i):
        return remote(
            block(ch, i),
            block(ch, line + i),
            send_b.at[ch, i],
            recv_b.at[ch, i],
            (rep, xor(me, near)),
        )

    def copy_c(ch, i):
        return remote(
            block(ch, i),
            block(ch, 2 * line + i),
            send_c.at[ch, i],
            recv_c.at[ch, i],
            (rep, xor(me, last)),
        )

    def copy_s(ch, i):
        return remote(
            block(ch, i), block(ch, i), send_s.at[ch, i], recv_s.at[ch, i], (sibling, me)
        )

    def forward_z(ch, t):
        for up, step in ((1, 1), (0, -1)):
            source = place_a - step * t
            to = place_a + step
            there = (source >= 0) & (source < line)
            onward = there & (to >= 0) & (to < line)

            @pl.when(there)
            def _(up=up, source=source, to=to, onward=onward):
                slot = xor(source, place_a)
                if t > 0:
                    remote(
                        block(ch, slot), block(ch, slot), send_z.at[ch, up, slot],
                        recv_z.at[ch, slot], (rep, me),
                    ).wait_recv()

                @pl.when(onward)
                def _():
                    copy_z(ch, up, source, to).start()

                if t > 0:
                    copy_b(ch, slot).start()
                    copy_c(ch, slot).start()
                    copy_s(ch, slot).start()

    def wait_sent_z(ch):
        for t in range(line - 1):
            for up, step in ((1, 1), (0, -1)):
                source = place_a - step * t
                to = place_a + step
                onward = (source >= 0) & (source < line) & (to >= 0) & (to < line)

                @pl.when(onward)
                def _(up=up, source=source, to=to):
                    copy_z(ch, up, source, to).wait_send()

    def start_own(ch):
        forward_z(ch, 0)
        copy_b(ch, 0).start()
        copy_c(ch, 0).start()

    def from_b(ch, i):
        copy_b(ch, i).wait_recv()
        copy_c(ch, line + i).start()
        copy_s(ch, line + i).start()

    def from_c(ch, i):
        copy_c(ch, i).wait_recv()
        copy_s(ch, 2 * line + i).start()

    def each(ch, do, start, stop):
        def one(i, carry):
            do(ch, i)
            return carry

        lax.fori_loop(start, stop, one, 0)

    def gather_stages(ch):
        def begin():
            from_b(ch, 0)
            forward_z(ch, 1)

        def middle():
            for t in range(2, line):
                forward_z(ch, t)

        return (
            begin,
            middle,
            lambda: each(ch, from_b, 1, line),
            lambda: each(ch, from_c, 0, line),
            lambda: each(ch, from_c, line, 2 * line),
        )

    def gather(ch):
        for stage in gather_stages(ch):
            stage()

    def finish(ch):
        def sent_b(i, carry):
            copy_b(ch, i).wait_send()
            return carry

        def sent_c(i, carry):
            copy_c(ch, i).wait_send()
            return carry

        def sent_s(i, carry):
            copy_s(ch, i).wait_send()
            return carry

        wait_sent_z(ch)
        lax.fori_loop(0, line, sent_b, 0)
        lax.fori_loop(0, 2 * line, sent_c, 0)
        lax.fori_loop(1, sz.group, sent_s, 0)

    def from_sibling(ch):
        def wait(i, carry):
            lo, hi = chunks[ch]
            other = pieces.at[1 - core, i, pl.ds(lo, hi - lo)]
            remote(other, other, send_s.at[ch, i], recv_s.at[ch, i], (sibling, me)).wait_recv()
            return carry

        lax.fori_loop(1, sz.group, wait, 0)

    chunk_rest, chunk_last = 0, len(chunks) - 1
    start_own(chunk_rest)

    def copy_m(k):
        return remote(
            small_ref, small_out.at[me], send_m.at[k], recv_m.at[k], (rep, xor(me, k))
        )

    def start_m(k, carry):
        copy_m(k).start()
        return carry

    lax.fori_loop(1, sz.group, start_m, 0)
    small_out[me] = small_ref[...]

    def keep_copy(n, src, dst):
        return pltpu.make_async_copy(src, dst, keep.at[n])

    places = jnp.concatenate(
        [routes_ref[...], slots_ref[...], jnp.zeros((4, seq), jnp.int32)], axis=0
    )
    places = places.astype(f32).T.astype(jnp.int32)
    route = places[:, 0:2]
    slot = places[:, 2:4]
    target = target_slots(sz, route, slot)
    first, second = target[:, 0:1], target[:, 1:2]
    wide_lane = iota((1, 256), 1)
    for j in range(sz.slots // 256):
        lane = wide_lane + j * 256
        pick = ((first == lane) | (second == lane)).astype(f32).astype(bf16)
        pick_all[:, j * 256 : (j + 1) * 256] = pick
        gsend[j * 256 : (j + 1) * 256, :] = dot_tn(pick, cot_ref[...]).astype(bf16)
    keep_copy(0, pick_all, pick_out).start()

    low_bits = lax.rem(me, 4)

    def copy_far(z):
        return remote(
            gsend.at[row_block(xor(place_a, z), 4 * sz.cap)],
            relay.at[z],
            send_g.at[4 * z],
            recv_g.at[4 * z],
            (rep, xor(me, 4 * z)),
        )

    def copy_plane(z, k):
        if z == 0:
            src = gsend.at[row_block(xor(me, k), sz.cap)]
        else:
            src = relay.at[z, row_block(xor(low_bits, k), sz.cap)]
        return remote(
            src,
            garr_out.at[pl.ds((4 * z + k) * sz.cap, sz.cap)],
            send_g.at[4 * z + k],
            recv_g.at[4 * z + k],
            (rep, xor(me, k)),
        )

    def own_rows(z):
        if z == 0:
            src = gsend.at[row_block(me, sz.cap)]
        else:
            src = relay.at[z, row_block(low_bits, sz.cap)]
        return pltpu.make_async_copy(
            src, garr_out.at[pl.ds(4 * z * sz.cap, sz.cap)], keep_rows.at[z]
        )

    def keep_far(z):
        return pltpu.make_async_copy(
            relay.at[z], far_out.at[z - line // 2], keep_rows.at[z]
        )

    def pass_on(z):
        if z > 0:
            copy_far(z).wait_recv()
        own_rows(z).start()
        for k in range(1, 4):
            copy_plane(z, k).start()

    far_order = list(range(line // 2, line)) + list(range(1, line // 2))
    begin, middle, rest_b, low_c, high_c = gather_stages(chunk_rest)
    begin()
    middle()
    rest_b()
    for z in far_order:
        copy_far(z).start()

    def wait_m(k, carry):
        remote(
            small_ref, small_out.at[xor(me, k)], send_m.at[k], recv_m.at[k], (rep, xor(me, k))
        ).wait()
        return carry

    lax.fori_loop(1, sz.group, wait_m, 0)
    small = small_out[...].astype(f32)[:, : sz.rows].reshape(width, BLK)
    small_t = small.T
    gain_one = small_t[GAIN_ONE : GAIN_ONE + 1]
    gain_two = small_t[GAIN_TWO : GAIN_TWO + 1]
    for i in range(seq // BLK):
        rows = slice(i * BLK, (i + 1) * BLK)
        x = tok_ref[rows, :].astype(f32)
        scale = lax.rsqrt(jnp.mean(x * x, axis=-1, keepdims=True) + norm_eps)
        n2_out[rows, :] = (x * scale * gain_one).astype(bf16)
    low_c()
    bias_tiles(sz, small_t, vector, tiles)
    length = len_ref[0]
    mask[...] = jnp.broadcast_to(jnp.where(iota((seq, 1), 0) < length, 0.0, NEG), (seq, BLK))
    high_c()
    from_sibling(chunk_rest)
    pass_on(0)

    def assemble(low, high):
        for place in range(sz.group):
            for h in range(2):
                source = xor(me, sz.relative(h, place))
                cols = slice(h * half, (h + 1) * half)
                if sz.rows % 16 == 0:
                    for m in range(low, high):
                        whole[m, row_block(source, sz.rows), cols] = pieces[
                            h, place, m * sz.rows : (m + 1) * sz.rows, :
                        ]
                else:
                    tall = pieces[h, place, :, :].astype(f32)
                    for m in range(low, high):
                        wide[m, row_block8(source, sz.rows), cols] = tall[
                            m * sz.rows : (m + 1) * sz.rows
                        ]
        if sz.rows % 16 != 0:
            for m in range(low, high):
                whole[m] = wide[m].astype(bf16)

    assemble(0, 3)
    keep_copy(2, whole.at[pl.ds(0, 3)], w_out.at[pl.ds(0, 3)]).start()
    for m in range(3):
        qkv[m] = dot_nn(n2_out[...], whole[m]).astype(bf16)
    keep_copy(3, qkv, qkv_out).start()

    low = iota((1, BLK), 1) < width // sz.heads
    halves = [jnp.where(low, 1.0, 0.0).astype(bf16), jnp.where(low, 0.0, 1.0).astype(bf16)]
    size = width // sz.heads

    def copy_p(pair, i):
        part = (pair, pl.ds(0, (i + 1) * BLK), pl.ds(2 * i * BLK, 2 * BLK))
        return pltpu.make_async_copy(probs.at[part], probs_out.at[part], send_p.at[pair, i])

    def attend(pair, carry):
        cols = row_block(pair, BLK)
        query = qkv[0, :, cols] * jnp.asarray(score_scale, bf16)
        key = qkv[1, :, cols]
        value_t = qkv[2, :, cols].T
        for i in range(seq // BLK):
            rows = slice(i * BLK, (i + 1) * BLK)
            keys = (i + 1) * BLK
            both = jnp.concatenate([query[rows] * halves[0], query[rows] * halves[1]], axis=0)
            scores = dot_nt(key[:keys], both)
            tile = tiles[pair]
            if i == 0:
                scores = scores + tile[BLK:]
            elif i == 1:
                scores = scores + tile
            else:
                scores = jnp.concatenate(
                    [scores[: keys - 2 * BLK], scores[keys - 2 * BLK :] + tile], axis=0
                )
            hidden = mask[:keys, :]
            scores = scores + jnp.concatenate([hidden, hidden], axis=1)
            raised = jnp.exp(scores - jnp.max(scores, axis=0, keepdims=True))
            soft = raised * (1.0 / jnp.sum(raised, axis=0, keepdims=True))
            soft = soft.astype(bf16)
            probs[pair, :keys, 2 * i * BLK : 2 * (i + 1) * BLK] = soft
            mixed = dot_nn(value_t[:, :keys], soft)
            mixed = jnp.concatenate([mixed[:size, :BLK], mixed[size:, BLK:]], axis=0)
            att[rows, cols] = mixed.T.astype(bf16)
        for i in range(seq // BLK):
            copy_p(pair, i).start()
        return carry

    lax.fori_loop(0, sz.pairs, attend, 0)
    keep_copy(4, att, att_out).start()
    assemble(3, 4)
    keep_copy(5, whole.at[pl.ds(3, 1)], w_out.at[pl.ds(3, 1)]).start()

    router = small.astype(bf16)
    for i in range(seq // BLK):
        rows = slice(i * BLK, (i + 1) * BLK)
        resid = tok_ref[rows, :].astype(f32) + dot_nn(att[rows, :], whole[3])
        resid_all[rows, :] = resid
        scale = lax.rsqrt(jnp.mean(resid * resid, axis=-1, keepdims=True) + norm_eps)
        normed = (resid * scale * gain_two).astype(bf16)
        n2_out[rows, :] = normed
        logits = dot_nn(normed, router)
        lane = iota((1, BLK), 1)
        logit = [
            jnp.sum(jnp.where(lane == route[rows, c : c + 1], logits, 0.0), axis=-1, keepdims=True)
            for c in range(2)
        ]
        share_one = 1.0 / (1.0 + jnp.exp(logit[1] - logit[0]))
        share_two = 1.0 / (1.0 + jnp.exp(logit[0] - logit[1]))
        gate_out[rows, :] = jnp.where(
            lane == 0, share_one, jnp.where(lane == 1, share_two, 0.0)
        )
    keep_copy(6, resid_all, resid_out).start()

    cs_out[...] = jnp.zeros_like(cs_out)
    normed = n2_out[...]
    combine_one = gate_out[:, 0:1]
    combine_two = gate_out[:, 1:2]
    per = 256 // sz.cap
    for j in range(sz.slots // 256):
        lane = wide_lane + j * 256
        pick = pick_all[:, j * 256 : (j + 1) * 256]
        rows_out[j * 256 : (j + 1) * 256, :] = dot_tn(pick, normed).astype(bf16)
        weight = jnp.where(first == lane, combine_one, jnp.where(second == lane, combine_two, 0.0))
        weight = jnp.sum(weight, axis=0, keepdims=True)
        for e in range(per):
            cs_out[j * per + e, 0:1, 0 : sz.cap] = weight[:, e * sz.cap : (e + 1) * sz.cap]

    for z in range(1, line // 2):
        pass_on(z)
    for z in range(line // 2, line):
        copy_far(z).wait_recv()
        keep_far(z).start()
    for z in range(line):
        if z > 0:
            copy_far(z).wait_send()
        if z < line // 2:
            own_rows(z).wait()
            for k in range(1, 4):
                copy_plane(z, k).wait()
        else:
            keep_far(z).wait()
    finish(0)

    def wait_p(pair, carry):
        for i in range(seq // BLK):
            copy_p(pair, i).wait()
        return carry

    lax.fori_loop(0, sz.pairs, wait_p, 0)
    keep_copy(0, pick_all, pick_out).wait()
    keep_copy(2, whole.at[pl.ds(0, 3)], w_out.at[pl.ds(0, 3)]).wait()
    keep_copy(3, qkv, qkv_out).wait()
    keep_copy(4, att, att_out).wait()
    keep_copy(5, whole.at[pl.ds(3, 1)], w_out.at[pl.ds(3, 1)]).wait()
    keep_copy(6, resid_all, resid_out).wait()


def vmem():
    return pl.BlockSpec(memory_space=pltpu.VMEM)


def anywhere():
    return pl.BlockSpec(memory_space=pl.ANY)


def forward_call(sz, lengths, tokens, routes, slots, parameters, weights, cotangent):
    seq, width, group = sz.seq, sz.width, sz.group
    shape = jax.ShapeDtypeStruct
    dma = pltpu.SemaphoreType.DMA
    wide = (4, width, width) if sz.rows % 16 else (4, 8, BLK)
    parts = len(sz.chunks)
    return pl.pallas_call(
        functools.partial(forward_kernel, sz),
        out_shape=[
            shape((4, width, width), bf16),
            shape((3, seq, width), bf16),
            shape((sz.pairs, seq, 2 * seq), bf16),
            shape((seq, width), bf16),
            shape((seq, width), f32),
            shape((sz.slots // 2, width), bf16),
            shape((sz.line // 2, 4 * sz.cap, width), bf16),
            shape((seq, sz.slots), bf16),
            shape((seq, width), bf16),
            shape((sz.slots, width), bf16),
            shape((sz.experts, 8, BLK), f32),
            shape((seq, BLK), f32),
            shape((group, sz.small, BLK), bf16),
        ],
        in_specs=[pl.BlockSpec(memory_space=pltpu.SMEM)] + [vmem()] * 12,
        out_specs=[anywhere()] * 8 + [vmem()] * 5,
        scratch_shapes=[
            pltpu.VMEM((2, group, sz.piece, sz.half), bf16),
            pltpu.VMEM((sz.slots, width), bf16),
            pltpu.VMEM((sz.line, 4 * sz.cap, width), bf16),
            pltpu.VMEM((16, 3 * BLK), f32),
            pltpu.VMEM((sz.pairs, 2 * BLK, 2 * BLK), f32),
            pltpu.VMEM((sz.pairs, seq, 2 * seq), bf16),
            pltpu.VMEM(wide, f32),
            pltpu.VMEM((4, width, width), bf16),
            pltpu.VMEM((3, seq, width), bf16),
            pltpu.VMEM((seq, width), bf16),
            pltpu.VMEM((seq, width), f32),
            pltpu.VMEM((seq, sz.slots), bf16),
            pltpu.VMEM((seq, BLK), f32),
            dma((parts, 2, sz.line)),
            dma((parts, sz.line)),
            dma((parts, sz.line)),
            dma((parts, sz.line)),
            dma((parts, 2 * sz.line)),
            dma((parts, 2 * sz.line)),
            dma((parts, group)),
            dma((parts, group)),
            dma((group,)),
            dma((group,)),
            dma((group,)),
            dma((group,)),
            dma((sz.pairs, seq // BLK)),
            dma((8,)),
            dma((sz.line,)),
            pltpu.VMEM((sz.small, BLK), bf16),
            pltpu.VMEM((BLK, BLK), f32),
            pltpu.VMEM((sz.small, BLK), f32),
        ],
        compiler_params=pltpu.CompilerParams(
            collective_id=0, has_side_effects=True, vmem_limit_bytes=VMEM_LIMIT
        ),
    )(lengths, tokens, routes, slots, *parameters, *weights, cotangent)


def gelu_parts(v):
    density = jnp.exp2(v * v * -0.7213475204444817 - 1.3257480647361593)
    base = 1.0 + 0.23164189 * jnp.abs(v)
    t = pl.reciprocal(base, approx=True)
    t = t * (2.0 - base * t)
    poly = t * (
        0.3193815351 + t * (-0.3565637813 + t * (1.7814779373 + t * (-1.8212559795 + t * 1.3302744289)))
    )
    tail = poly * density
    below = jnp.where(v < 0.0, tail, 1.0 - tail)
    return v * below, below + v * density


def column_of(row):
    return jnp.broadcast_to(row, (BLK, BLK)).T


def expert_kernel(
    sz,
    cs_ref,
    rows_ref,
    grads_hbm,
    far_hbm,
    win_ref,
    wout_ref,
    dots_out,
    results_out,
    near_out,
    back_out,
    grad_in_out,
    grad_out_out,
    win,
    wout,
    arrived,
    scales,
    arrived_t,
    scaled,
    scaled_t,
    hidden,
    pre_grad,
    back_send,
    dots_send,
    sums,
    others,
    totals,
    grads_ref,
    results_ref,
    load,
    send_r,
    recv_r,
    send_c,
    recv_c,
    send_b,
    recv_b,
    send_d,
    recv_d,
    send_n,
    recv_n,
    send_w,
    recv_w,
    keep_w,
    keep_r,
    far_own,
    send_f,
    recv_f,
):
    rep, me, core, sibling = peers(sz)
    group, cap, width = sz.group, sz.cap, sz.width
    loads = [
        pltpu.make_async_copy(win_ref.at[0], win, load.at[0]),
        pltpu.make_async_copy(wout_ref.at[0], wout, load.at[1]),
        pltpu.make_async_copy(grads_hbm, grads_ref.at[pl.ds(0, sz.slots // 2)], load.at[2]),
        pltpu.make_async_copy(
            rows_ref.at[row_block(me, cap)], arrived.at[pl.ds(0, cap)], load.at[3]
        ),
    ]
    for copy in loads:
        copy.start()
    low_bits = lax.rem(me, 4)
    later = [
        pltpu.make_async_copy(
            far_hbm.at[n, row_block(low_bits, cap)],
            grads_ref.at[pl.ds((sz.slots // 2) + 4 * n * cap, cap)],
            far_own.at[n],
        )
        for n in range(sz.line // 2)
    ]
    for copy in later:
        copy.start()
    greet(sz, rep, me, sibling)

    def copy_f(n, k):
        return remote(
            far_hbm.at[n, row_block(xor(low_bits, k), cap)],
            grads_ref.at[pl.ds((sz.slots // 2) + (4 * n + k) * cap, cap)],
            send_f.at[n, k],
            recv_f.at[n, k],
            (rep, xor(me, k)),
        )

    def copy_r(k):
        to = xor(me, k)
        return remote(
            rows_ref.at[row_block(to, cap)], arrived.at[row_block(k, cap)],
            send_r.at[k], recv_r.at[k], (rep, to),
        )

    def copy_c(k):
        to = xor(me, k)
        return remote(cs_ref.at[to], scales.at[k], send_c.at[k], recv_c.at[k], (rep, to))

    def copy_b(k):
        return remote(
            back_send.at[row_block(k, cap)], back_out.at[row_block(me, cap)],
            send_b.at[k], recv_b.at[k], (rep, xor(me, k)),
        )

    def copy_n(k):
        return remote(
            results_ref.at[row_block(k, cap)], near_out.at[row_block(me, cap)],
            send_n.at[k], recv_n.at[k], (rep, xor(me, k)),
        )

    def copy_d(k):
        return remote(
            dots_send.at[k], dots_out.at[me], send_d.at[k], recv_d.at[k], (rep, xor(me, k))
        )

    def start_r(k, carry):
        copy_c(k).start()
        copy_r(k).start()
        return carry

    per = 256 // cap
    groups = sz.slots // 256
    early = list(range(groups // 2, groups - 1)) + list(range(0, groups // 2))
    for g in early:
        lax.fori_loop(max(g * per, 1), (g + 1) * per, start_r, 0)
    for n in range(sz.line // 2):
        for k in range(1, 4):
            copy_f(n, k).start()
    scales[0] = cs_ref[me]
    dots_send[...] = jnp.zeros_like(dots_send)
    for copy in loads:
        copy.wait()

    step = 1024

    def keep_results(g):
        span = pl.ds(g * 256, 256)
        return pltpu.make_async_copy(results_ref.at[span], results_out.at[span], keep_r.at[g])

    def rows_of(g):
        start = g * per

        def arrive(k, carry):
            copy_c(k).wait_recv()
            copy_r(k).wait_recv()
            return carry

        lax.fori_loop(max(start, 1), start + per, arrive, 0)
        for n in range(sz.line // 2):
            if (sz.slots // 2 + 4 * n * cap) // 256 == g:
                later[n].wait()
                for k in range(1, 4):
                    copy_f(n, k).wait_recv()
        span = slice(g * 256, (g + 1) * 256)
        x = arrived[span, :]
        arrived_t[:, span] = x.T
        columns = [column_of(scales[start + i, 0:1, :])[:cap, 0:1] for i in range(per)]
        column = jnp.concatenate(columns, axis=0)
        raw = grads_ref[span, :].astype(f32)
        scaled[span, :] = (raw * column).astype(bf16)
        scaled_t[:, span] = scaled[span, :].T

        def part(j, carry):
            cols = row_block(j, step)
            pre = dot_nn(arrived[span, :], win[:, cols])
            grad_hidden = dot_nn(scaled[span, :], wout[:, cols])
            act, slope = gelu_parts(pre)
            hidden[span, cols] = act.astype(bf16)
            pre_grad[span, cols] = (grad_hidden * slope).astype(bf16)
            return carry

        lax.fori_loop(0, sz.ff // step, part, 0)
        back_send[span, :] = dot_nt(pre_grad[span, :], win[...]).astype(bf16)

        def send_back(k, carry):
            copy_b(k).start()
            return carry

        lax.fori_loop(max(start, 1), start + per, send_back, 0)
        results = dot_nt(hidden[span, :], wout[...])
        results_ref[span, :] = (results * column).astype(bf16)
        if g < groups // 2:

            def send_near(k, carry):
                copy_n(k).start()
                return carry

            lax.fori_loop(max(start, 1), start + per, send_near, 0)
        else:
            keep_results(g).start()
        dots = jnp.sum(results * raw, axis=-1, keepdims=True)
        for i in range(per):
            tall = jnp.broadcast_to(dots[i * cap : (i + 1) * cap], (cap, BLK))
            if cap < BLK:
                tall = jnp.concatenate([tall, jnp.zeros((BLK - cap, BLK), f32)], axis=0)
            dots_send[start + i, 0:1, :] = tall.T[0:1, :]

        def send_dots(k, carry):
            copy_d(k).start()
            return carry

        lax.fori_loop(max(start, 1), start + per, send_dots, 0)

    def start_last():
        def sent(k, carry):
            copy_r(k).wait_send()
            return carry

        for g in early:
            lax.fori_loop(max(g * per, 1), (g + 1) * per, sent, 0)
        lax.fori_loop((groups - 1) * per, groups * per, start_r, 0)

    for g in range(groups):
        if g == 1:
            start_last()
        rows_of(g)
    own_back = pltpu.make_async_copy(
        back_send.at[pl.ds(0, cap)], back_out.at[row_block(me, cap)], load.at[4]
    )
    own_back.start()
    own_near = pltpu.make_async_copy(
        results_ref.at[pl.ds(0, cap)], near_out.at[row_block(me, cap)], load.at[5]
    )
    own_near.start()
    dots_out[me] = dots_send[0]

    size = sz.ff // sz.reps
    cut = 512 if size > 512 else size
    subs = size // cut
    pieces = sz.reps // 2 * subs

    def columns_of(parity, i):
        return pl.ds(pl.multiple_of((2 * (i // subs) + parity) * size + (i % subs) * cut, BLK), cut)

    def copy_w(m, i):
        return remote(
            sums.at[m, i], others.at[m, i], send_w.at[m, i], recv_w.at[m, i], (sibling, me)
        )

    def copy_k(m, i):
        return pltpu.make_async_copy(
            totals.at[m, i], (grad_in_out, grad_out_out)[m].at[:, pl.ds(i * cut, cut)], keep_w.at[m, i]
        )

    for i in range(pieces):
        cols = columns_of(1 - core, i)
        sums[0, i] = dot_nn(arrived_t[...], pre_grad[:, cols]).astype(bf16)
        copy_w(0, i).start()
        sums[1, i] = dot_nn(scaled_t[...], hidden[:, cols]).astype(bf16)
        copy_w(1, i).start()
    for i in range(pieces):
        cols = columns_of(core, i)
        for m, left, right in ((0, arrived_t, pre_grad), (1, scaled_t, hidden)):
            total = dot_nn(left[...], right[:, cols])
            copy_w(m, i).wait_recv()
            totals[m, i] = (total + others[m, i].astype(f32)).astype(bf16)
            copy_k(m, i).start()

    def finish(k, carry):
        copy_c(k).wait_send()
        copy_b(k).wait_send()
        copy_d(k).wait_send()
        from_back = remote(
            back_send.at[row_block(k, cap)], back_out.at[row_block(xor(me, k), cap)],
            send_b.at[k], recv_b.at[k], (rep, xor(me, k)),
        )
        from_back.wait_recv()
        from_dots = remote(
            dots_send.at[k], dots_out.at[xor(me, k)], send_d.at[k], recv_d.at[k], (rep, xor(me, k))
        )
        from_dots.wait_recv()
        return carry

    lax.fori_loop(1, group, finish, 0)

    def sent_last(k, carry):
        copy_r(k).wait_send()
        return carry

    lax.fori_loop((groups - 1) * per, groups * per, sent_last, 0)

    def end_near(k, carry):
        copy_n(k).wait()
        return carry

    lax.fori_loop(1, group // 2, end_near, 0)
    for n in range(sz.line // 2):
        for k in range(1, 4):
            copy_f(n, k).wait_send()
    for g in range(groups // 2, groups):
        keep_results(g).wait()
    own_back.wait()
    own_near.wait()
    for i in range(pieces):
        for m in range(2):
            copy_w(m, i).wait_send()
            copy_k(m, i).wait()


def expert_call(sz, rows, scales, grads, far, weight_in, weight_out):
    group, width, ff, slots = sz.group, sz.width, sz.ff, sz.slots
    shape = jax.ShapeDtypeStruct
    dma = pltpu.SemaphoreType.DMA
    size = ff // sz.reps
    cut = 512 if size > 512 else size
    pieces = sz.reps // 2 * (size // cut)
    return pl.pallas_call(
        functools.partial(expert_kernel, sz),
        out_shape=[
            shape((sz.experts, 8, BLK), f32),
            shape((slots, width), bf16),
            shape((slots, width), bf16),
            shape((slots, width), bf16),
            shape((width, ff // 2), bf16),
            shape((width, ff // 2), bf16),
        ],
        in_specs=[vmem()] + [anywhere()] * 5,
        out_specs=[vmem()] + [anywhere()] * 5,
        scratch_shapes=[
            pltpu.VMEM((width, ff), bf16),
            pltpu.VMEM((width, ff), bf16),
            pltpu.VMEM((slots, width), bf16),
            pltpu.VMEM((group, 8, BLK), f32),
            pltpu.VMEM((width, slots), bf16),
            pltpu.VMEM((slots, width), bf16),
            pltpu.VMEM((width, slots), bf16),
            pltpu.VMEM((slots, ff), bf16),
            pltpu.VMEM((slots, ff), bf16),
            pltpu.VMEM((slots, width), bf16),
            pltpu.VMEM((group, 8, BLK), f32),
            pltpu.VMEM((2, pieces, width, cut), bf16),
            pltpu.VMEM((2, pieces, width, cut), bf16),
            pltpu.VMEM((2, pieces, width, cut), bf16),
            pltpu.VMEM((slots, width), bf16),
            pltpu.VMEM((slots, width), bf16),
            dma((6,)),
        ]
        + [dma((group,))] * 10
        + [dma((2, pieces))] * 3
        + [dma((slots // 256,)), dma((sz.line // 2,)), dma((sz.line // 2, 4)), dma((sz.line // 2, 4))],
        compiler_params=pltpu.CompilerParams(
            collective_id=1, has_side_effects=True, vmem_limit_bytes=VMEM_LIMIT
        ),
    )(scales, rows, grads, far, weight_in, weight_out)


def near_onehot(sz):
    lane = iota((1, 3 * BLK), 1)
    distance = jnp.where(lane <= BLK, BLK + lane, lane - 2 * BLK)
    bucket = jnp.where(distance < 16, distance, 16)
    for cutoff in cutoffs:
        bucket = bucket + (distance >= cutoff).astype(jnp.int32)
    per = sz.buckets // sz.group
    shape = (sz.group, sz.rows, 3 * BLK)
    inner = iota(shape, 1)
    named = jnp.where(inner < per, iota(shape, 0) * per + inner, -1)
    return (named == bucket[None]).astype(f32).reshape(sz.width, 3 * BLK).astype(bf16)


def unit_shapes(sz):
    up = lambda n: -(-n // 16) * 16
    return [(up(sz.rows), sz.half)] + [(up(3 * sz.rows), BLK)] * (sz.half // BLK)


def backward_kernel(
    sz,
    len_ref,
    tok_ref,
    cot_ref,
    routes_ref,
    slots_ref,
    n2_ref,
    gate_ref,
    small_ref,
    dots_ref,
    w_hbm,
    qkv_hbm,
    probs_hbm,
    att_hbm,
    resid_hbm,
    pick_hbm,
    results_hbm,
    near_hbm,
    back_hbm,
    out_ref,
    gtok_ref,
    gq_ref,
    gk_ref,
    gv_ref,
    go_ref,
    gsmall_ref,
    *scratch,
):
    units = unit_shapes(sz)
    (
        probs, w_ref, qkv_ref, att_ref, resid_ref, pick_ref, back_ref, returned, total_bf, gres, gatt,
        dqkv, dscore, stacks, normed, normed_t, near_sum, far_sum, sums, wide, packed, packed_rows,
        packed_far, small_mine, small_from, small_final,
        load, load_p, send_r, recv_r, send_x, recv_x, send_m, recv_m,
    ) = scratch[:34]
    buffers = scratch[34:]
    mine = buffers[0::6]
    theirs = buffers[1::6]
    from_sib = buffers[2::6]
    from_one = buffers[3::6]
    from_two = buffers[4::6]
    final = buffers[5::6]
    rep, me, core, sibling = peers(sz)
    seq, width, half, line, group = sz.seq, sz.width, sz.half, sz.line, sz.group
    near = jnp.where(core == 0, 1, 2)
    last = jnp.where(core == 0, 2, 1)
    cap = sz.cap
    blocks = seq // BLK

    def fetch(n, src, dst):
        return pltpu.make_async_copy(src, dst, load.at[n])

    same_half = row_block(lax.div(me, group // 2), sz.slots // 2)
    loads = [
        fetch(0, back_hbm, back_ref),
        fetch(1, pick_hbm, pick_ref),
        fetch(2, resid_hbm, resid_ref),
        fetch(3, w_hbm.at[3], w_ref.at[3]),
        fetch(4, att_hbm, att_ref),
        fetch(5, qkv_hbm, qkv_ref),
        fetch(6, w_hbm.at[pl.ds(0, 3)], w_ref.at[pl.ds(0, 3)]),
        fetch(7, near_hbm.at[same_half], returned.at[same_half]),
    ]

    def copy_p(pair, i):
        part = (pair, pl.ds(0, (i + 1) * BLK), pl.ds(2 * i * BLK, 2 * BLK))
        return pltpu.make_async_copy(probs_hbm.at[part], probs.at[part], load_p.at[pair, i])

    def start_p(pair, carry):
        for i in range(blocks):
            copy_p(pair, i).start()
        return carry

    for copy in loads[:6]:
        copy.start()
    lax.fori_loop(0, sz.pairs, start_p, 0)
    for copy in loads[6:]:
        copy.start()
    greet(sz, rep, me, sibling)

    def copy_r(k, owner):
        return remote(
            results_hbm.at[row_block(k, cap)], returned.at[row_block(owner, cap)],
            send_r.at[k], recv_r.at[k], (rep, xor(me, k)),
        )

    def start_r(k, carry):
        copy_r(k, me).start()
        return carry

    lax.fori_loop(group // 2, group, start_r, 0)

    def copy_x(u, stage):
        if stage == 0:
            src, dst, to = theirs[u], from_sib[u], (sibling, me)
        elif stage == 1:
            src, dst, to = mine[u].at[pl.ds(group // 2, group // 2)], from_one[u], (rep, xor(me, last))
        elif stage == 2:
            src, dst, to = mine[u].at[pl.ds(line, line)], from_two[u].at[pl.ds(0, line)], (rep, xor(me, near))
        elif stage == 3:
            src, dst, to = final[u].at[core], final[u].at[core], (sibling, me)
        else:
            z = stage - 3
            src, dst, to = mine[u].at[z], from_two[u].at[line + z], (rep, xor(me, 4 * z))
        return remote(src, dst, send_x.at[u, stage], recv_x.at[u, stage], to)

    def add_into(ref, start, stop, other, skip=0):
        def add(p, carry):
            ref[p] = (ref[p].astype(f32) + other[p + skip].astype(f32)).astype(bf16)
            return carry

        lax.fori_loop(start, stop, add, 0)

    def step(u, number):
        if number == 0:
            copy_x(u, 0).start()
        elif number == 1:
            copy_x(u, 0).wait_recv()
            add_into(mine[u], group // 2, group, from_sib[u])
            copy_x(u, 1).start()
            add_into(mine[u], 0, group // 2, from_sib[u])
        elif number == 2:
            copy_x(u, 1).wait_recv()
            add_into(mine[u], line, 2 * line, from_one[u])
            copy_x(u, 2).start()
            add_into(mine[u], 0, line, from_one[u])
        elif number == 3:
            copy_x(u, 2).wait_recv()
            add_into(mine[u], 0, line, from_two[u])
            for z in range(1, line):
                copy_x(u, 3 + z).start()
        elif number == 4:
            total = mine[u][0].astype(f32)
            for z in range(1, line):
                copy_x(u, 3 + z).wait_recv()
                total = total + from_two[u][line + z].astype(f32)
            final[u][core] = total
            copy_x(u, 3).start()
        else:
            remote(
                final[u].at[1 - core], final[u].at[1 - core], send_x.at[u, 3], recv_x.at[u, 3],
                (sibling, me),
            ).wait_recv()
            for stage in range(3 + line):
                copy_x(u, stage).wait_send()

    def owner_of(p, swap):
        one, two = (last, near) if swap else (near, last)
        rel = lax.rem(p, line) * 4 + lax.rem(lax.div(p, line), 2) * one + lax.div(p, 2 * line) * two
        return xor(me, rel)

    def fill(u, read):
        def put(p, carry):
            mine[u][p] = read(core, owner_of(p, False)).astype(bf16)
            theirs[u][p] = read(1 - core, owner_of(p, True)).astype(bf16)
            return carry

        lax.fori_loop(0, group, put, 0)

    def padded(value, u):
        short = units[u][0] - value.shape[0]
        if short:
            value = jnp.concatenate([value, jnp.zeros((short, value.shape[1]), f32)], axis=0)
        return value

    small = small_ref[...].astype(f32)[:, : sz.rows].reshape(width, BLK)
    small_t = small.T
    gain_one = small_t[GAIN_ONE : GAIN_ONE + 1]
    gain_two = small_t[GAIN_TWO : GAIN_TWO + 1]
    router = small.astype(bf16)
    length = len_ref[0]

    places = jnp.concatenate(
        [routes_ref[...], slots_ref[...], jnp.zeros((4, seq), jnp.int32)], axis=0
    )
    places = places.astype(f32).T.astype(jnp.int32)
    route = places[:, 0:2]
    target = target_slots(sz, route, places[:, 2:4])
    first, second = target[:, 0:1], target[:, 1:2]
    dot_one = jnp.zeros((seq, BLK), f32)
    dot_two = jnp.zeros((seq, BLK), f32)
    lanes = iota((1, BLK), 1)
    per = BLK // cap
    for j in range(sz.slots // BLK):
        row = jnp.concatenate([dots_ref[j * per + e, 0:1, 0:cap] for e in range(per)], axis=1)
        lane = lanes + j * BLK
        dot_one = dot_one + jnp.where(first == lane, row, 0.0)
        dot_two = dot_two + jnp.where(second == lane, row, 0.0)
    dot_one = jnp.sum(dot_one, axis=-1, keepdims=True)
    dot_two = jnp.sum(dot_two, axis=-1, keepdims=True)
    share = gate_ref[:, 0:1] * gate_ref[:, 1:2] * (dot_one - dot_two)
    grad_logits = share * (
        (lanes == route[:, 0:1]).astype(f32) - (lanes == route[:, 1:2]).astype(f32)
    )
    grad_logits = grad_logits.astype(bf16)
    packed[...] = dot_tn(n2_ref[...], grad_logits)

    for copy in loads[:3]:
        copy.wait()
    gain_two_grad = jnp.zeros((1, width), f32)
    for i in range(blocks):
        rows = slice(i * BLK, (i + 1) * BLK)
        grad = dot_nn(pick_ref[rows, :], back_ref[...]) + dot_nt(grad_logits[rows], router)
        resid = resid_ref[rows, :]
        scale = lax.rsqrt(jnp.mean(resid * resid, axis=-1, keepdims=True) + norm_eps)
        gain_two_grad = gain_two_grad + jnp.sum(grad * resid * scale, axis=0, keepdims=True)
        valid = (iota((BLK, 1), 0) + i * BLK < length).astype(f32)
        grad_out = cot_ref[rows, :].astype(f32) * valid
        moved = grad * gain_two
        mean = jnp.mean(moved * resid, axis=-1, keepdims=True)
        total = grad_out + scale * moved - resid * (scale * scale * scale * mean)
        gres[rows, :] = total
        total_bf[rows, :] = total.astype(bf16)
    loads[3].wait()
    loads[4].wait()
    gatt[...] = dot_nt(total_bf[...], w_ref[3]).astype(bf16)
    wide[...] = dot_tn(att_ref[...], total_bf[...])

    def read_o(h, s):
        cols = pl.ds(pl.multiple_of(h * half, BLK), half)
        return padded(wide[row_block8(s, sz.rows), cols], 0)

    fill(0, read_o)
    step(0, 0)

    for i in range(blocks):
        rows = slice(i * BLK, (i + 1) * BLK)
        x = tok_ref[rows, :].astype(f32)
        scale = lax.rsqrt(jnp.mean(x * x, axis=-1, keepdims=True) + norm_eps)
        normed[rows, :] = (x * scale * gain_one).astype(bf16)
    normed_t[...] = normed[...].T
    step(0, 1)

    low = iota((1, BLK), 1) < width // sz.heads
    halves = [jnp.where(low, 1.0, 0.0).astype(bf16), jnp.where(low, 0.0, 1.0).astype(bf16)]

    size = width // sz.heads
    loads[5].wait()

    def back_pair(pair):
        cols = row_block(pair, BLK)
        query = qkv_ref[0, :, cols]
        key = qkv_ref[1, :, cols]
        key_t = key.T
        value = qkv_ref[2, :, cols]
        grads = gatt[:, cols]
        for i in range(blocks):
            copy_p(pair, i).wait()
        for i in range(blocks):
            rows = slice(i * BLK, (i + 1) * BLK)
            keys = (i + 1) * BLK
            at = slice(2 * i * BLK, 2 * (i + 1) * BLK)
            both = jnp.concatenate([grads[rows] * halves[0], grads[rows] * halves[1]], axis=0)
            stacks[0, at, :] = jnp.concatenate(
                [query[rows] * halves[0], query[rows] * halves[1]], axis=0
            )
            stacks[1, at, :] = both
            soft = probs[pair, :keys, at].astype(f32)
            product = soft * dot_nt(value[:keys], both)
            grad_score = product - soft * jnp.sum(product, axis=0, keepdims=True)
            if i == 0:
                near_sum[pair, :BLK] = jnp.zeros((BLK, 2 * BLK), f32)
                near_sum[pair, BLK:] = grad_score
                far_sum[pair] = jnp.zeros((8, 2 * BLK), f32)
            else:
                near_sum[pair] += grad_score[keys - 2 * BLK :]
                if i >= 2:
                    far = grad_score[: keys - 2 * BLK].reshape((keys - 2 * BLK) // 8, 8, 2 * BLK)
                    far_sum[pair] += jnp.sum(far, axis=0)
            low_score = grad_score.astype(bf16)
            dscore[:keys, at] = low_score
            moved = dot_nn(key_t[:, :keys], low_score)
            moved = jnp.concatenate([moved[:size, :BLK], moved[size:, BLK:]], axis=0)
            dqkv[0, rows, cols] = (moved.T * score_scale).astype(bf16)
        for i in range(blocks):
            rows = slice(i * BLK, (i + 1) * BLK)
            below = slice(2 * i * BLK, 2 * seq)
            grad_key = dot_nn(dscore[rows, below], stacks[0, below, :])
            grad_value = dot_nn(probs[pair, rows, below], stacks[1, below, :])
            dqkv[1, rows, cols] = (grad_key * score_scale).astype(bf16)
            dqkv[2, rows, cols] = grad_value.astype(bf16)

    parts = half // BLK
    for j in range(parts):

        def one(h, carry, j=j):
            pair = h * parts + j
            back_pair(pair)
            cols = row_block(pair, BLK)
            grads = jnp.concatenate([dqkv[m, :, cols] for m in range(3)], axis=1)
            sums[h] = dot_nn(normed_t[...], grads)
            return carry

        one(0, 0)
        for u, n in PLAN_H[j]:
            step(u, n)
        one(1, 0)

        def read_j(h, s):
            rows = row_block8(s, sz.rows)
            value = sums[h, rows, :]
            return padded(
                jnp.concatenate([value[:, m * BLK : (m + 1) * BLK] for m in range(3)], axis=0), 1
            )

        fill(1 + j, read_j)
        for u, n in PLAN_J[j]:
            step(u, n)

    loads[6].wait()
    gain_one_grads = []

    def input_grad(i):
        rows = slice(i * BLK, (i + 1) * BLK)
        grad = dot_nt(dqkv[0, rows, :], w_ref[0]) + dot_nt(dqkv[1, rows, :], w_ref[1])
        grad = grad + dot_nt(dqkv[2, rows, :], w_ref[2])
        x = tok_ref[rows, :].astype(f32)
        scale = lax.rsqrt(jnp.mean(x * x, axis=-1, keepdims=True) + norm_eps)
        gain_one_grads.append(jnp.sum(grad * x * scale, axis=0, keepdims=True))
        moved = grad * gain_one
        mean = jnp.mean(moved * x, axis=-1, keepdims=True)
        gtok_ref[rows, :] = gres[rows, :] + scale * moved - x * (scale * scale * scale * mean)

    flip = (iota((2 * BLK, 2 * BLK), 0) + iota((2 * BLK, 2 * BLK), 1) == 2 * BLK - 1)
    flip = flip.astype(f32).astype(bf16)

    def bucket_sums(pair, carry):
        turned = dot_nn(flip, near_sum[pair].astype(bf16))
        far = jnp.sum(far_sum[pair], axis=0, keepdims=True)
        for b in range(2):
            tall = jnp.concatenate(
                [turned[:, b * BLK : (b + 1) * BLK], jnp.zeros((2 * BLK, 2 * BLK), f32)], axis=1
            )
            rolled = pltpu.roll(tall, BLK + 1, 1, stride=1, stride_axis=0)
            packed_rows[pl.ds(2 * pair + b, 1), :] = jnp.sum(rolled, axis=0, keepdims=True)
            packed_far[pl.ds(2 * pair + b, 1), :] = far[:, b * BLK : (b + 1) * BLK]
        return carry

    def table_grad():
        packed_rows[...] = jnp.zeros_like(packed_rows)
        packed_far[...] = jnp.zeros_like(packed_far)
        lax.fori_loop(0, sz.pairs, bucket_sums, 0)
        onehot = near_onehot(sz)
        values = packed_rows[...]
        upper = values.astype(bf16)
        lower = (values - upper.astype(f32)).astype(bf16)
        table = dot_nt(upper, onehot) + dot_nt(lower, onehot)
        far = jnp.sum(packed_far[...], axis=-1, keepdims=True)
        one_far = jnp.broadcast_to((lanes == 0).astype(f32), (8, BLK)).astype(bf16)
        farthest = dot_nt(one_far, onehot[:, :BLK])[0:1]
        return table + far * farthest

    def copy_m(k):
        return remote(
            small_mine.at[xor(me, k)], small_from.at[k], send_m.at[k], recv_m.at[k], (rep, xor(me, k))
        )

    def small_start(table):
        gain_one_grad = gain_one_grads[0]
        for grad in gain_one_grads[1:]:
            gain_one_grad = gain_one_grad + grad
        tall = jnp.concatenate(
            [
                jnp.zeros((GAIN_ONE, width), f32),
                gain_one_grad,
                gain_two_grad,
                jnp.zeros((TABLE - GAIN_TWO - 1, width), f32),
                table,
                jnp.zeros((BLK - TABLE - 16, width), f32),
            ],
            axis=0,
        )
        whole = (packed[...] + tall.T).reshape(group, sz.rows, BLK)
        if sz.small != sz.rows:
            whole = jnp.concatenate(
                [whole, jnp.zeros((group, sz.small - sz.rows, BLK), f32)], axis=1
            )
        small_mine[...] = whole.astype(bf16)

        def start_m(k, carry):
            copy_m(k).start()
            return carry

        lax.fori_loop(1, group, start_m, 0)

    def copy_f():
        return remote(
            small_final.at[core], small_final.at[core], send_m.at[0], recv_m.at[0], (sibling, me)
        )

    def small_sum():
        small_final[core] = small_mine[me].astype(f32)

        def add(k, carry):
            copy_m(k).wait()
            small_final[core] += small_from[k].astype(f32)
            return carry

        lax.fori_loop(1, group, add, 0)
        copy_f().start()

    def small_end():
        remote(
            small_final.at[1 - core], small_final.at[1 - core], send_m.at[0], recv_m.at[0],
            (sibling, me),
        ).wait_recv()
        gsmall_ref[...] = small_final[0] + small_final[1]
        copy_f().wait_send()

    def results():
        def wait_r(k, carry):
            copy_r(k, xor(me, k)).wait_recv()
            return carry

        lax.fori_loop(group // 2, group, wait_r, 0)
        loads[7].wait()
        for i in range(blocks):
            rows = slice(i * BLK, (i + 1) * BLK)
            valid = (iota((BLK, 1), 0) + i * BLK < length).astype(f32)
            total = resid_ref[rows, :] + dot_nn(pick_ref[rows, :], returned[...])
            out_ref[rows, :] = (total * valid).astype(bf16)

    table = None
    for act in PLAN_T:
        if act == "T":
            table = table_grad()
        elif act == "M":
            small_start(table)
        elif act == "R":
            results()
        elif act == "m":
            small_sum()
        elif act == "e":
            small_end()
        elif isinstance(act, int):
            input_grad(act)
        else:
            step(*act)
    for u in range(1, 1 + parts):
        step(u, 5)
    for h in range(2):
        cols = slice(h * half, (h + 1) * half)
        go_ref[:, cols] = final[0][h, : sz.rows]
        for j in range(parts):
            at = slice(h * half + j * BLK, h * half + (j + 1) * BLK)
            for m, ref in enumerate((gq_ref, gk_ref, gv_ref)):
                ref[:, at] = final[1 + j][h, m * sz.rows : (m + 1) * sz.rows]

    def sent_r(k, carry):
        copy_r(k, me).wait_send()
        return carry

    lax.fori_loop(group // 2, group, sent_r, 0)


def backward_call(sz, lengths, tokens, cotangent, routes, slots, saved, results, near, back, dots):
    seq, width, group, line = sz.seq, sz.width, sz.group, sz.line
    shape = jax.ShapeDtypeStruct
    dma = pltpu.SemaphoreType.DMA
    w, qkv, probs, att, resid, pick, n2, gate, small = saved
    units = unit_shapes(sz)
    buffers = []
    for rows, cols in units:
        buffers += [
            pltpu.VMEM((group, rows, cols), bf16),
            pltpu.VMEM((group, rows, cols), bf16),
            pltpu.VMEM((group, rows, cols), bf16),
            pltpu.VMEM((group // 2, rows, cols), bf16),
            pltpu.VMEM((2 * line, rows, cols), bf16),
            pltpu.VMEM((2, rows, cols), f32),
        ]
    dense = shape((sz.rows, width), f32)
    return pl.pallas_call(
        functools.partial(backward_kernel, sz),
        out_shape=[
            shape((seq, width), bf16),
            shape((seq, width), f32),
            dense,
            dense,
            dense,
            dense,
            shape((sz.small, BLK), f32),
        ],
        in_specs=[pl.BlockSpec(memory_space=pltpu.SMEM)] + [vmem()] * 8 + [anywhere()] * 9,
        out_specs=[vmem()] * 7,
        scratch_shapes=[
            pltpu.VMEM((sz.pairs, seq, 2 * seq), bf16),
            pltpu.VMEM((4, width, width), bf16),
            pltpu.VMEM((3, seq, width), bf16),
            pltpu.VMEM((seq, width), bf16),
            pltpu.VMEM((seq, width), f32),
            pltpu.VMEM((seq, sz.slots), bf16),
            pltpu.VMEM((sz.slots, width), bf16),
            pltpu.VMEM((sz.slots, width), bf16),
            pltpu.VMEM((seq, width), bf16),
            pltpu.VMEM((seq, width), f32),
            pltpu.VMEM((seq, width), bf16),
            pltpu.VMEM((3, seq, width), bf16),
            pltpu.VMEM((seq, 2 * seq), bf16),
            pltpu.VMEM((2, 2 * seq, BLK), bf16),
            pltpu.VMEM((seq, width), bf16),
            pltpu.VMEM((width, seq), bf16),
            pltpu.VMEM((sz.pairs, 2 * BLK, 2 * BLK), f32),
            pltpu.VMEM((sz.pairs, 8, 2 * BLK), f32),
            pltpu.VMEM((2, width, 3 * BLK), f32),
            pltpu.VMEM((width, width), f32),
            pltpu.VMEM((width, BLK), f32),
            pltpu.VMEM((16, 3 * BLK), f32),
            pltpu.VMEM((16, BLK), f32),
            pltpu.VMEM((group, sz.small, BLK), bf16),
            pltpu.VMEM((group, sz.small, BLK), bf16),
            pltpu.VMEM((2, sz.small, BLK), f32),
            dma((8,)),
            dma((sz.pairs, seq // BLK)),
            dma((group,)),
            dma((group,)),
            dma((len(units), 3 + line)),
            dma((len(units), 3 + line)),
            dma((group,)),
            dma((group,)),
        ]
        + buffers,
        compiler_params=pltpu.CompilerParams(
            collective_id=2, has_side_effects=True, vmem_limit_bytes=VMEM_LIMIT
        ),
    )(
        lengths, tokens, cotangent, routes, slots, n2, gate, small, dots, w, qkv, probs, att, resid,
        pick, results, near, back,
    )


def finish_kernel(
    sz, cuts, in_ref, out_ref, result_ref, tokens_ref, q_ref, k_ref, v_ref, o_ref, small_ref,
    to_in, to_out, to_result, to_tokens, to_q, to_k, to_v, to_o, to_one, to_two, to_router, to_table,
    *scratch,
):
    held, wide, load, store = scratch[:8], scratch[8:10], scratch[10], scratch[11]
    moves = []

    def move(n, src, dst, parts):
        size = src.shape[0] // parts
        for i in range(parts):
            at = pl.ds(i * size, size)
            moves.append((n, at, src, dst))

    move(2, result_ref, to_result, 1)
    move(3, tokens_ref, to_tokens, 2)
    for n, src, dst in ((4, q_ref, to_q), (5, k_ref, to_k), (6, v_ref, to_v), (7, o_ref, to_o)):
        move(n, src, dst, 1)
    move(0, in_ref, to_in, cuts)
    move(1, out_ref, to_out, cuts)
    ins, outs = [], []
    for i, (n, at, src, dst) in enumerate(moves):
        ins.append(pltpu.make_async_copy(src.at[at], held[n].at[at], load.at[i]))
        kept = wide[n] if n < 2 else held[n]
        outs.append(pltpu.make_async_copy(kept.at[at], dst.at[at], store.at[i]))
    for copy in ins:
        copy.start()
    small = small_ref[...]
    tall = jnp.concatenate([small, jnp.zeros((BLK - sz.small, BLK), f32)], axis=0).T
    to_router[...] = tall[: sz.experts, : sz.rows]
    to_one[...] = tall[GAIN_ONE : GAIN_ONE + 1, : sz.rows]
    to_two[...] = tall[GAIN_TWO : GAIN_TWO + 1, : sz.rows]
    to_table[...] = small[: to_table.shape[0], TABLE : TABLE + sz.heads]
    for (n, at, src, dst), came, goes in zip(moves, ins, outs):
        came.wait()
        if n < 2:
            wide[n][at, :] = held[n][at, :].astype(f32)
        goes.start()
    for copy in outs:
        copy.wait()


def finish_call(sz, grad_in, grad_out, result, tokens, dense, small):
    shape = jax.ShapeDtypeStruct
    cuts = 6
    whole = [grad_in, grad_out, result, tokens, *dense]
    kinds = [f32, f32] + [x.dtype for x in whole[2:]]
    return pl.pallas_call(
        functools.partial(finish_kernel, sz, cuts),
        out_shape=[shape(x.shape, kind) for x, kind in zip(whole, kinds)]
        + [
            shape((1, sz.rows), f32),
            shape((1, sz.rows), f32),
            shape((sz.experts, sz.rows), f32),
            shape((sz.buckets // sz.group, sz.heads), f32),
        ],
        in_specs=[anywhere()] * 8 + [vmem()],
        out_specs=[anywhere()] * 8 + [vmem()] * 4,
        scratch_shapes=[pltpu.VMEM(x.shape, x.dtype) for x in whole]
        + [pltpu.VMEM(x.shape, f32) for x in whole[:2]]
        + [pltpu.SemaphoreType.DMA((2 * cuts + 8,))] * 2,
        compiler_params=pltpu.CompilerParams(vmem_limit_bytes=VMEM_LIMIT),
    )(*whole, small)


def shards(
    tokens, lengths, routes, slots, norm_one, w_query, w_key, w_value, w_output, bias_table, norm_two,
    router, expert_in, expert_out, cotangent, *, reps, group,
):
    seq, width = tokens.shape
    rows = w_query.shape[0]
    heads = bias_table.shape[1]
    experts = router.shape[1]
    sz = Sizes(
        reps, group, seq, width, heads, experts, expert_in.shape[2], rows, bias_table.shape[0] * group
    )
    parameters = (norm_one[None], norm_two[None], router.T, bias_table)
    weights = (w_query, w_key, w_value, w_output)
    routes, slots = routes.T, slots.T
    (w, qkv, probs, att, resid, grads, far, pick, n2, sent, scales, gate, small_all) = forward_call(
        sz, lengths, tokens, routes, slots, parameters, weights, cotangent
    )
    dots, results, near, back, grad_in, grad_out = expert_call(sz, sent, scales, grads, far, expert_in, expert_out)
    saved = (w, qkv, probs, att, resid, pick, n2, gate, small_all)
    output, grad_tokens, gq, gk, gv, go, gsmall = backward_call(
        sz, lengths, tokens, cotangent, routes, slots, saved, results, near, back, dots
    )
    if reps > 2:
        same = [[r for r in range(reps) if r % 2 == c] for c in range(2)]
        grad_in, grad_out = (
            lax.psum_scatter(grad, "rep", scatter_dimension=1, axis_index_groups=same, tiled=True)
            for grad in (grad_in, grad_out)
        )
        gq, gk, gv, go, gsmall = lax.psum((gq, gk, gv, go, gsmall), "rep", axis_index_groups=same)
    (grad_in, grad_out, output, grad_tokens, gq, gk, gv, go, g_one, g_two, g_router, g_table) = (
        finish_call(sz, grad_in, grad_out, output, grad_tokens, (gq, gk, gv, go), gsmall)
    )
    return (
        output,
        grad_tokens,
        g_one[0],
        gq,
        gk,
        gv,
        go,
        g_table,
        g_two[0],
        g_router.T,
        grad_in[None],
        grad_out[None],
    )


def solution(mesh):
    both = ("rep", "shard")
    return jax.shard_map(
        functools.partial(shards, reps=mesh.shape["rep"], group=mesh.shape["shard"]),
        mesh=mesh,
        in_specs=(
            P(both, None),
            P(both),
            P(both, None),
            P(both, None),
            P("shard"),
            P("shard", None),
            P("shard", None),
            P("shard", None),
            P("shard", None),
            P("shard", None),
            P("shard"),
            P("shard", None),
            P("shard", None, None),
            P("shard", None, None),
            P(both, None),
        ),
        out_specs=(
            P(both, None),
            P(both, None),
            P("shard"),
            P("shard", None),
            P("shard", None),
            P("shard", None),
            P("shard", None),
            P("shard", None),
            P("shard"),
            P("shard", None),
            P("shard", None, "rep"),
            P("shard", None, "rep"),
        ),
        check_vma=False,
    )
```

```python
import functools

import jax
import jax.numpy as jnp
from jax import lax
from jax.experimental import pallas as pl
from jax.experimental.pallas import tpu as pltpu
from jax.sharding import PartitionSpec as P

MESH = pl.DeviceIdType.MESH
norm_eps = 1e-06
score_scale = 0.125
cutoffs = (19, 21, 24, 27, 31, 35, 40, 46, 52, 59, 67, 77, 87, 99, 113)
f32 = jnp.float32
bf16 = jnp.bfloat16
GAIN_ONE, GAIN_TWO, TABLE = 64, 65, 80
BLK = 128
VMEM_LIMIT = 60 * 2**20
NEG = -1e30
PLAN_H = ((), ((1, 1),), ((2, 1),))
PLAN_J = (((1, 0),), ((2, 0), (0, 2)), ((3, 0), (1, 2), (0, 3)))
PLAN_T = (
    "T", (3, 1), (2, 2), 0, (1, 3), (0, 3.5), 1, (3, 2), (2, 3), (1, 3.5), 2, 3, "M", (3, 3), (2, 3.5), (1, 4), (0, 4),
    "R", (3, 3.5), "m", (2, 4), (0, 5), (3, 4), "e",
)


def dot_nn(a, b):
    return lax.dot_general(a, b, (((1,), (0,)), ((), ())), preferred_element_type=f32)


def dot_nt(a, b):
    return lax.dot_general(a, b, (((1,), (1,)), ((), ())), preferred_element_type=f32)


def dot_tn(a, b):
    return lax.dot_general(a, b, (((0,), (0,)), ((), ())), preferred_element_type=f32)


def iota(shape, dim):
    return lax.broadcasted_iota(jnp.int32, shape, dim)


class Sizes:
    def __init__(self, reps, group, seq, width, heads, experts, ff, rows, buckets):
        self.reps, self.group, self.seq, self.width = reps, group, seq, width
        self.heads, self.experts, self.ff, self.rows = heads, experts, ff, rows
        self.buckets = buckets
        self.cap = 2 * seq // experts
        self.slots = experts * self.cap
        self.line = group // 4
        self.half = width // 2
        self.small = -(-rows // 16) * 16
        self.share = self.small // 16
        self.piece = 4 * rows
        self.pairs = heads // 2
        self.chunks = ((0, self.piece),)

    def relative(self, half, place):
        first, second = (1, 2) if half == 0 else (2, 1)
        line = place % self.line
        return line * 4 + (place // self.line % 2) * first + (place // (2 * self.line)) * second


def peers(sz):
    rep = lax.axis_index("rep")
    me = lax.axis_index("shard")
    return rep, me, lax.rem(rep, 2), rep + 1 - 2 * lax.rem(rep, 2)


def xor(a, b):
    return jnp.bitwise_xor(a, b)


def greet(sz, rep, me, sibling):
    barrier = pltpu.get_barrier_semaphore()

    def signal(k, carry):
        pl.semaphore_signal(barrier, inc=1, device_id=(rep, xor(me, k)), device_id_type=MESH)
        return carry

    lax.fori_loop(1, sz.group, signal, 0)
    pl.semaphore_signal(barrier, inc=1, device_id=(sibling, me), device_id_type=MESH)


def met(sz):
    pl.semaphore_wait(pltpu.get_barrier_semaphore(), sz.group)


def remote(src, dst, send, recv, device):
    return pltpu.make_async_remote_copy(
        src_ref=src, dst_ref=dst, send_sem=send, recv_sem=recv, device_id=device, device_id_type=MESH
    )


def send_order(group):
    order = list(range(group // 2, group)) + list(range(1, group // 2))
    return order


def row_block(index, size):
    return pl.ds(pl.multiple_of(index * size, size), size)


def row_block8(index, size):
    return pl.ds(pl.multiple_of(index * size, 8), size)


def target_slots(sz, routes, slots):
    return jnp.where(slots < sz.cap, routes * sz.cap + slots, -1)


def bias_tiles(sz, small_t, vector, tiles):
    lane = iota((1, 3 * BLK), 1)
    distance = jnp.where(lane <= BLK, BLK - lane, 4 * BLK - lane)
    bucket = jnp.where(distance < 16, distance, 16)
    for cutoff in cutoffs:
        bucket = bucket + (distance >= cutoff).astype(jnp.int32)
    per = sz.buckets // sz.group
    shape = (sz.group, sz.rows, 3 * BLK)
    inner = iota(shape, 1)
    named = jnp.where(inner < per, iota(shape, 0) * per + inner, -1)
    onehot = (named == bucket[None]).astype(f32).reshape(sz.width, 3 * BLK).astype(bf16)
    table = small_t[TABLE : TABLE + 16].astype(bf16)
    values = dot_nn(table, onehot)
    values = values - values[:, 0:1]
    vector[...] = jnp.where((lane > BLK) & (lane < 2 * BLK), NEG, values)

    def tile(pair, carry):
        for b in range(2):
            row = jnp.broadcast_to(vector[pl.ds(2 * pair + b, 1), :], (BLK, 3 * BLK))
            turned = pltpu.roll(row, 0, 1, stride=1, stride_axis=0)[:, : 2 * BLK]
            tiles[pair, :, b * BLK : (b + 1) * BLK] = turned.T
        return carry

    lax.fori_loop(0, sz.pairs, tile, 0)


def forward_kernel(
    sz,
    len_ref,
    tok_ref,
    routes_ref,
    slots_ref,
    one_ref,
    two_ref,
    router_ref,
    table_ref,
    wq_ref,
    wk_ref,
    wv_ref,
    wo_ref,
    cot_ref,
    w_out,
    qkv_out,
    probs_out,
    att_out,
    resid_out,
    garr_out,
    far_out,
    normed_out,
    pick_out,
    n2_out,
    rows_out,
    cs_out,
    gate_out,
    small_out,
    pieces,
    gsend,
    relay,
    vector,
    tiles,
    probs,
    wide,
    whole,
    qkv,
    att,
    resid_all,
    pick_all,
    mask,
    send_z,
    recv_z,
    send_b,
    recv_b,
    send_c,
    recv_c,
    send_s,
    recv_s,
    send_m,
    recv_m,
    send_g,
    recv_g,
    send_p,
    keep,
    keep_rows,
    small_ref,
    small_wide,
    small_tall,
    normed_t,
):
    rep, me, core, sibling = peers(sz)
    seq, width, half, line = sz.seq, sz.width, sz.half, sz.line
    place_a = me // 4
    near = jnp.where(core == 0, 1, 2)
    last = jnp.where(core == 0, 2, 1)

    greet(sz, rep, me, sibling)

    small_wide[...] = jnp.zeros_like(small_wide)
    small_wide[0 : sz.experts, 0 : sz.rows] = router_ref[...].astype(f32)
    small_wide[GAIN_ONE : GAIN_ONE + 1, 0 : sz.rows] = one_ref[...].astype(f32)
    small_wide[GAIN_TWO : GAIN_TWO + 1, 0 : sz.rows] = two_ref[...].astype(f32)
    few = table_ref.shape[0]
    small_ref[...] = small_wide[...].T[: sz.small].astype(bf16)
    table = table_ref[...].astype(f32)
    small_tall[...] = small_ref[...].astype(f32)
    small_tall[0:few, TABLE : TABLE + sz.heads] = table
    small_ref[...] = small_tall[...].astype(bf16)

    for h in range(2):
        cols = slice(h * half, (h + 1) * half)
        if sz.rows % 16 == 0:
            for m, ref in enumerate((wq_ref, wk_ref, wv_ref, wo_ref)):
                pieces[h, 0, m * sz.rows : (m + 1) * sz.rows, :] = ref[:, cols]
        else:
            stacked = [ref[:, cols].astype(f32) for ref in (wq_ref, wk_ref, wv_ref, wo_ref)]
            pieces[h, 0] = jnp.concatenate(stacked, axis=0).astype(bf16)

    met(sz)

    chunks = sz.chunks

    def block(ch, slot):
        lo, hi = chunks[ch]
        return pieces.at[core, slot, pl.ds(lo, hi - lo)]

    def copy_z(ch, up, source, to):
        slot = xor(source, to)
        return remote(
            block(ch, xor(source, place_a)),
            block(ch, slot),
            send_z.at[ch, up, xor(source, place_a)],
            recv_z.at[ch, slot],
            (rep, me + (to - place_a) * 4),
        )

    def copy_b(ch, i):
        return remote(
            block(ch, i),
            block(ch, line + i),
            send_b.at[ch, i],
            recv_b.at[ch, i],
            (rep, xor(me, near)),
        )

    def copy_c(ch, i):
        return remote(
            block(ch, i),
            block(ch, 2 * line + i),
            send_c.at[ch, i],
            recv_c.at[ch, i],
            (rep, xor(me, last)),
        )

    def copy_s(ch, i):
        return remote(
            block(ch, i), block(ch, i), send_s.at[ch, i], recv_s.at[ch, i], (sibling, me)
        )

    def forward_z(ch, t):
        for up, step in ((1, 1), (0, -1)):
            source = place_a - step * t
            to = place_a + step
            there = (source >= 0) & (source < line)
            onward = there & (to >= 0) & (to < line)

            @pl.when(there)
            def _(up=up, source=source, to=to, onward=onward):
                slot = xor(source, place_a)
                if t > 0:
                    remote(
                        block(ch, slot), block(ch, slot), send_z.at[ch, up, slot],
                        recv_z.at[ch, slot], (rep, me),
                    ).wait_recv()

                @pl.when(onward)
                def _():
                    copy_z(ch, up, source, to).start()

                if t > 0:
                    copy_b(ch, slot).start()
                    copy_c(ch, slot).start()
                    copy_s(ch, slot).start()

    def wait_sent_z(ch):
        for t in range(line - 1):
            for up, step in ((1, 1), (0, -1)):
                source = place_a - step * t
                to = place_a + step
                onward = (source >= 0) & (source < line) & (to >= 0) & (to < line)

                @pl.when(onward)
                def _(up=up, source=source, to=to):
                    copy_z(ch, up, source, to).wait_send()

    def start_own(ch):
        forward_z(ch, 0)
        copy_b(ch, 0).start()
        copy_c(ch, 0).start()

    def from_b(ch, i):
        copy_b(ch, i).wait_recv()
        copy_c(ch, line + i).start()
        copy_s(ch, line + i).start()

    def from_c(ch, i):
        copy_c(ch, i).wait_recv()
        copy_s(ch, 2 * line + i).start()

    def each(ch, do, start, stop):
        def one(i, carry):
            do(ch, i)
            return carry

        lax.fori_loop(start, stop, one, 0)

    def gather_stages(ch):
        def begin():
            from_b(ch, 0)
            forward_z(ch, 1)

        def middle():
            for t in range(2, line):
                forward_z(ch, t)

        return (
            begin,
            middle,
            lambda: each(ch, from_b, 1, line),
            lambda: each(ch, from_c, 0, line),
            lambda: each(ch, from_c, line, 2 * line),
        )

    def gather(ch):
        for stage in gather_stages(ch):
            stage()

    def finish(ch):
        def sent_b(i, carry):
            copy_b(ch, i).wait_send()
            return carry

        def sent_c(i, carry):
            copy_c(ch, i).wait_send()
            return carry

        def sent_s(i, carry):
            copy_s(ch, i).wait_send()
            return carry

        wait_sent_z(ch)
        lax.fori_loop(0, line, sent_b, 0)
        lax.fori_loop(0, 2 * line, sent_c, 0)
        lax.fori_loop(1, sz.group, sent_s, 0)

    def from_sibling(ch):
        def wait(i, carry):
            lo, hi = chunks[ch]
            other = pieces.at[1 - core, i, pl.ds(lo, hi - lo)]
            remote(other, other, send_s.at[ch, i], recv_s.at[ch, i], (sibling, me)).wait_recv()
            return carry

        lax.fori_loop(1, sz.group, wait, 0)

    chunk_rest, chunk_last = 0, len(chunks) - 1
    start_own(chunk_rest)

    def copy_m(k):
        return remote(
            small_ref, small_out.at[me], send_m.at[k], recv_m.at[k], (rep, xor(me, k))
        )

    def start_m(k, carry):
        copy_m(k).start()
        return carry

    lax.fori_loop(1, sz.group, start_m, 0)
    small_out[me] = small_ref[...]

    def keep_copy(n, src, dst):
        return pltpu.make_async_copy(src, dst, keep.at[n])

    places = jnp.concatenate(
        [routes_ref[...], slots_ref[...], jnp.zeros((4, seq), jnp.int32)], axis=0
    )
    places = places.astype(f32).T.astype(jnp.int32)
    route = places[:, 0:2]
    slot = places[:, 2:4]
    target = target_slots(sz, route, slot)
    first, second = target[:, 0:1], target[:, 1:2]
    wide_lane = iota((1, 256), 1)
    for j in range(sz.slots // 256):
        lane = wide_lane + j * 256
        pick = ((first == lane) | (second == lane)).astype(f32).astype(bf16)
        pick_all[:, j * 256 : (j + 1) * 256] = pick
        gsend[j * 256 : (j + 1) * 256, :] = dot_tn(pick, cot_ref[...]).astype(bf16)
    keep_copy(0, pick_all, pick_out).start()

    low_bits = lax.rem(me, 4)

    def copy_far(z):
        return remote(
            gsend.at[row_block(xor(place_a, z), 4 * sz.cap)],
            relay.at[z],
            send_g.at[4 * z],
            recv_g.at[4 * z],
            (rep, xor(me, 4 * z)),
        )

    def copy_plane(z, k):
        if z == 0:
            src = gsend.at[row_block(xor(me, k), sz.cap)]
        else:
            src = relay.at[z, row_block(xor(low_bits, k), sz.cap)]
        return remote(
            src,
            garr_out.at[pl.ds((4 * z + k) * sz.cap, sz.cap)],
            send_g.at[4 * z + k],
            recv_g.at[4 * z + k],
            (rep, xor(me, k)),
        )

    def own_rows(z):
        if z == 0:
            src = gsend.at[row_block(me, sz.cap)]
        else:
            src = relay.at[z, row_block(low_bits, sz.cap)]
        return pltpu.make_async_copy(
            src, garr_out.at[pl.ds(4 * z * sz.cap, sz.cap)], keep_rows.at[z]
        )

    def keep_far(z):
        return pltpu.make_async_copy(
            relay.at[z], far_out.at[z - line // 2], keep_rows.at[z]
        )

    def pass_on(z):
        if z > 0:
            copy_far(z).wait_recv()
        own_rows(z).start()
        for k in range(1, 4):
            copy_plane(z, k).start()

    far_order = list(range(line // 2, line)) + list(range(1, line // 2))
    begin, middle, rest_b, low_c, high_c = gather_stages(chunk_rest)
    begin()
    middle()
    rest_b()
    for z in far_order:
        copy_far(z).start()

    def wait_m(k, carry):
        remote(
            small_ref, small_out.at[xor(me, k)], send_m.at[k], recv_m.at[k], (rep, xor(me, k))
        ).wait()
        return carry

    lax.fori_loop(1, sz.group, wait_m, 0)
    small = small_out[...].astype(f32)[:, : sz.rows].reshape(width, BLK)
    small_t = small.T
    gain_one = small_t[GAIN_ONE : GAIN_ONE + 1]
    gain_two = small_t[GAIN_TWO : GAIN_TWO + 1]
    for i in range(seq // BLK):
        rows = slice(i * BLK, (i + 1) * BLK)
        x = tok_ref[rows, :].astype(f32)
        scale = lax.rsqrt(jnp.mean(x * x, axis=-1, keepdims=True) + norm_eps)
        n2_out[rows, :] = (x * scale * gain_one).astype(bf16)
    low_c()
    bias_tiles(sz, small_t, vector, tiles)
    length = len_ref[0]
    mask[...] = jnp.broadcast_to(jnp.where(iota((seq, 1), 0) < length, 0.0, NEG), (seq, BLK))
    high_c()
    from_sibling(chunk_rest)
    pass_on(0)

    def assemble(low, high):
        for place in range(sz.group):
            for h in range(2):
                source = xor(me, sz.relative(h, place))
                cols = slice(h * half, (h + 1) * half)
                if sz.rows % 16 == 0:
                    for m in range(low, high):
                        whole[m, row_block(source, sz.rows), cols] = pieces[
                            h, place, m * sz.rows : (m + 1) * sz.rows, :
                        ]
                else:
                    tall = pieces[h, place, :, :].astype(f32)
                    for m in range(low, high):
                        wide[m, row_block8(source, sz.rows), cols] = tall[
                            m * sz.rows : (m + 1) * sz.rows
                        ]
        if sz.rows % 16 != 0:
            for m in range(low, high):
                whole[m] = wide[m].astype(bf16)

    assemble(0, 3)
    keep_copy(2, whole.at[pl.ds(0, 3)], w_out.at[pl.ds(0, 3)]).start()
    for m in range(3):
        qkv[m] = dot_nn(n2_out[...], whole[m]).astype(bf16)
    keep_copy(3, qkv, qkv_out).start()
    normed_t[...] = n2_out[...].T
    keep_copy(1, normed_t, normed_out).start()

    low = iota((1, BLK), 1) < width // sz.heads
    halves = [jnp.where(low, 1.0, 0.0).astype(bf16), jnp.where(low, 0.0, 1.0).astype(bf16)]
    size = width // sz.heads

    def copy_p(pair, i):
        part = (pair, pl.ds(0, (i + 1) * BLK), pl.ds(2 * i * BLK, 2 * BLK))
        return pltpu.make_async_copy(probs.at[part], probs_out.at[part], send_p.at[pair, i])

    def attend(pair, carry):
        cols = row_block(pair, BLK)
        query = qkv[0, :, cols] * jnp.asarray(score_scale, bf16)
        key = qkv[1, :, cols]
        value_t = qkv[2, :, cols].T
        for i in range(seq // BLK):
            rows = slice(i * BLK, (i + 1) * BLK)
            keys = (i + 1) * BLK
            both = jnp.concatenate([query[rows] * halves[0], query[rows] * halves[1]], axis=0)
            scores = dot_nt(key[:keys], both)
            tile = tiles[pair]
            if i == 0:
                scores = scores + tile[BLK:]
            elif i == 1:
                scores = scores + tile
            else:
                scores = jnp.concatenate(
                    [scores[: keys - 2 * BLK], scores[keys - 2 * BLK :] + tile], axis=0
                )
            hidden = mask[:keys, :]
            scores = scores + jnp.concatenate([hidden, hidden], axis=1)
            raised = jnp.exp(scores - jnp.max(scores, axis=0, keepdims=True))
            soft = raised * (1.0 / jnp.sum(raised, axis=0, keepdims=True))
            soft = soft.astype(bf16)
            probs[pair, :keys, 2 * i * BLK : 2 * (i + 1) * BLK] = soft
            mixed = dot_nn(value_t[:, :keys], soft)
            mixed = jnp.concatenate([mixed[:size, :BLK], mixed[size:, BLK:]], axis=0)
            att[rows, cols] = mixed.T.astype(bf16)
        for i in range(seq // BLK):
            copy_p(pair, i).start()
        return carry

    lax.fori_loop(0, sz.pairs, attend, 0)
    keep_copy(4, att, att_out).start()
    assemble(3, 4)
    keep_copy(5, whole.at[pl.ds(3, 1)], w_out.at[pl.ds(3, 1)]).start()

    router = small.astype(bf16)
    for i in range(seq // BLK):
        rows = slice(i * BLK, (i + 1) * BLK)
        resid = tok_ref[rows, :].astype(f32) + dot_nn(att[rows, :], whole[3])
        resid_all[rows, :] = resid
        scale = lax.rsqrt(jnp.mean(resid * resid, axis=-1, keepdims=True) + norm_eps)
        normed = (resid * scale * gain_two).astype(bf16)
        n2_out[rows, :] = normed
        logits = dot_nn(normed, router)
        lane = iota((1, BLK), 1)
        logit = [
            jnp.sum(jnp.where(lane == route[rows, c : c + 1], logits, 0.0), axis=-1, keepdims=True)
            for c in range(2)
        ]
        share_one = 1.0 / (1.0 + jnp.exp(logit[1] - logit[0]))
        share_two = 1.0 / (1.0 + jnp.exp(logit[0] - logit[1]))
        gate_out[rows, :] = jnp.where(
            lane == 0, share_one, jnp.where(lane == 1, share_two, 0.0)
        )
    keep_copy(6, resid_all, resid_out).start()

    cs_out[...] = jnp.zeros_like(cs_out)
    normed = n2_out[...]
    combine_one = gate_out[:, 0:1]
    combine_two = gate_out[:, 1:2]
    per = 256 // sz.cap
    for j in range(sz.slots // 256):
        lane = wide_lane + j * 256
        pick = pick_all[:, j * 256 : (j + 1) * 256]
        rows_out[j * 256 : (j + 1) * 256, :] = dot_tn(pick, normed).astype(bf16)
        weight = jnp.where(first == lane, combine_one, jnp.where(second == lane, combine_two, 0.0))
        weight = jnp.sum(weight, axis=0, keepdims=True)
        for e in range(per):
            cs_out[j * per + e, 0:1, 0 : sz.cap] = weight[:, e * sz.cap : (e + 1) * sz.cap]

    for z in range(1, line // 2):
        pass_on(z)
    for z in range(line // 2, line):
        copy_far(z).wait_recv()
        keep_far(z).start()
    for z in range(line):
        if z > 0:
            copy_far(z).wait_send()
        if z < line // 2:
            own_rows(z).wait()
            for k in range(1, 4):
                copy_plane(z, k).wait()
        else:
            keep_far(z).wait()
    finish(0)

    def wait_p(pair, carry):
        for i in range(seq // BLK):
            copy_p(pair, i).wait()
        return carry

    lax.fori_loop(0, sz.pairs, wait_p, 0)
    keep_copy(0, pick_all, pick_out).wait()
    keep_copy(2, whole.at[pl.ds(0, 3)], w_out.at[pl.ds(0, 3)]).wait()
    keep_copy(3, qkv, qkv_out).wait()
    keep_copy(1, normed_t, normed_out).wait()
    keep_copy(4, att, att_out).wait()
    keep_copy(5, whole.at[pl.ds(3, 1)], w_out.at[pl.ds(3, 1)]).wait()
    keep_copy(6, resid_all, resid_out).wait()


def vmem():
    return pl.BlockSpec(memory_space=pltpu.VMEM)


def anywhere():
    return pl.BlockSpec(memory_space=pl.ANY)


def forward_call(sz, lengths, tokens, routes, slots, parameters, weights, cotangent):
    seq, width, group = sz.seq, sz.width, sz.group
    shape = jax.ShapeDtypeStruct
    dma = pltpu.SemaphoreType.DMA
    wide = (4, width, width) if sz.rows % 16 else (4, 8, BLK)
    parts = len(sz.chunks)
    return pl.pallas_call(
        functools.partial(forward_kernel, sz),
        out_shape=[
            shape((4, width, width), bf16),
            shape((3, seq, width), bf16),
            shape((sz.pairs, seq, 2 * seq), bf16),
            shape((seq, width), bf16),
            shape((seq, width), f32),
            shape((sz.slots // 2, width), bf16),
            shape((sz.line // 2, 4 * sz.cap, width), bf16),
            shape((width, seq), bf16),
            shape((seq, sz.slots), bf16),
            shape((seq, width), bf16),
            shape((sz.slots, width), bf16),
            shape((sz.experts, 8, BLK), f32),
            shape((seq, BLK), f32),
            shape((group, sz.small, BLK), bf16),
        ],
        in_specs=[pl.BlockSpec(memory_space=pltpu.SMEM)] + [vmem()] * 12,
        out_specs=[anywhere()] * 9 + [vmem()] * 5,
        scratch_shapes=[
            pltpu.VMEM((2, group, sz.piece, sz.half), bf16),
            pltpu.VMEM((sz.slots, width), bf16),
            pltpu.VMEM((sz.line, 4 * sz.cap, width), bf16),
            pltpu.VMEM((16, 3 * BLK), f32),
            pltpu.VMEM((sz.pairs, 2 * BLK, 2 * BLK), f32),
            pltpu.VMEM((sz.pairs, seq, 2 * seq), bf16),
            pltpu.VMEM(wide, f32),
            pltpu.VMEM((4, width, width), bf16),
            pltpu.VMEM((3, seq, width), bf16),
            pltpu.VMEM((seq, width), bf16),
            pltpu.VMEM((seq, width), f32),
            pltpu.VMEM((seq, sz.slots), bf16),
            pltpu.VMEM((seq, BLK), f32),
            dma((parts, 2, sz.line)),
            dma((parts, sz.line)),
            dma((parts, sz.line)),
            dma((parts, sz.line)),
            dma((parts, 2 * sz.line)),
            dma((parts, 2 * sz.line)),
            dma((parts, group)),
            dma((parts, group)),
            dma((group,)),
            dma((group,)),
            dma((group,)),
            dma((group,)),
            dma((sz.pairs, seq // BLK)),
            dma((8,)),
            dma((sz.line,)),
            pltpu.VMEM((sz.small, BLK), bf16),
            pltpu.VMEM((BLK, BLK), f32),
            pltpu.VMEM((sz.small, BLK), f32),
            pltpu.VMEM((width, seq), bf16),
        ],
        compiler_params=pltpu.CompilerParams(
            collective_id=0, has_side_effects=True, vmem_limit_bytes=VMEM_LIMIT
        ),
    )(lengths, tokens, routes, slots, *parameters, *weights, cotangent)


def gelu_parts(v):
    density = jnp.exp2(v * v * -0.7213475204444817 - 1.3257480647361593)
    base = 1.0 + 0.23164189 * jnp.abs(v)
    t = pl.reciprocal(base, approx=True)
    t = t * (2.0 - base * t)
    poly = t * (
        0.3193815351 + t * (-0.3565637813 + t * (1.7814779373 + t * (-1.8212559795 + t * 1.3302744289)))
    )
    tail = poly * density
    below = jnp.where(v < 0.0, tail, 1.0 - tail)
    return v * below, below + v * density


def column_of(row):
    return jnp.broadcast_to(row, (BLK, BLK)).T


def expert_kernel(
    sz,
    cs_ref,
    rows_ref,
    grads_hbm,
    far_hbm,
    win_ref,
    wout_ref,
    dots_out,
    relay_out,
    near_out,
    back_out,
    grad_in_out,
    grad_out_out,
    win,
    wout,
    arrived,
    scales,
    arrived_t,
    scaled,
    scaled_t,
    hidden,
    pre_grad,
    back_send,
    dots_send,
    sums,
    others,
    totals,
    grads_ref,
    results_ref,
    load,
    send_r,
    recv_r,
    send_c,
    recv_c,
    send_b,
    recv_b,
    send_d,
    recv_d,
    send_n,
    recv_n,
    send_w,
    recv_w,
    keep_w,
    keep_r,
    far_own,
    send_f,
    recv_f,
    send_p,
    recv_p,
):
    rep, me, core, sibling = peers(sz)
    group, cap, width = sz.group, sz.cap, sz.width
    greet(sz, rep, me, sibling)
    loads = [
        pltpu.make_async_copy(win_ref.at[0], win, load.at[0]),
        pltpu.make_async_copy(wout_ref.at[0], wout, load.at[1]),
        pltpu.make_async_copy(grads_hbm, grads_ref.at[pl.ds(0, sz.slots // 2)], load.at[2]),
        pltpu.make_async_copy(
            rows_ref.at[row_block(me, cap)], arrived.at[pl.ds(0, cap)], load.at[3]
        ),
    ]
    for copy in loads:
        copy.start()
    low_bits = lax.rem(me, 4)
    later = [
        pltpu.make_async_copy(
            far_hbm.at[n, row_block(low_bits, cap)],
            grads_ref.at[pl.ds((sz.slots // 2) + 4 * n * cap, cap)],
            far_own.at[n],
        )
        for n in range(sz.line // 2)
    ]
    for copy in later:
        copy.start()
    met(sz)

    def copy_f(n, k):
        return remote(
            far_hbm.at[n, row_block(xor(low_bits, k), cap)],
            grads_ref.at[pl.ds((sz.slots // 2) + (4 * n + k) * cap, cap)],
            send_f.at[n, k],
            recv_f.at[n, k],
            (rep, xor(me, k)),
        )

    def copy_r(k):
        to = xor(me, k)
        return remote(
            rows_ref.at[row_block(to, cap)], arrived.at[row_block(k, cap)],
            send_r.at[k], recv_r.at[k], (rep, to),
        )

    def copy_c(k):
        to = xor(me, k)
        return remote(cs_ref.at[to], scales.at[k], send_c.at[k], recv_c.at[k], (rep, to))

    def copy_b(k):
        return remote(
            back_send.at[row_block(k, cap)], back_out.at[row_block(me, cap)],
            send_b.at[k], recv_b.at[k], (rep, xor(me, k)),
        )

    def copy_n(k):
        return remote(
            results_ref.at[row_block(k, cap)], near_out.at[row_block(me, cap)],
            send_n.at[k], recv_n.at[k], (rep, xor(me, k)),
        )

    def copy_d(k):
        return remote(
            dots_send.at[k], dots_out.at[me], send_d.at[k], recv_d.at[k], (rep, xor(me, k))
        )

    def start_r(k, carry):
        copy_c(k).start()
        copy_r(k).start()
        return carry

    per = 256 // cap
    groups = sz.slots // 256
    early = list(range(groups // 2, groups - 1)) + list(range(0, groups // 2))
    for g in early:
        lax.fori_loop(max(g * per, 1), (g + 1) * per, start_r, 0)
    for n in range(sz.line // 2):
        for k in range(1, 4):
            copy_f(n, k).start()
    scales[0] = cs_ref[me]
    dots_send[...] = jnp.zeros_like(dots_send)
    for copy in loads:
        copy.wait()

    step = 1024

    def copy_p(j):
        return remote(
            results_ref.at[row_block(group // 2 + j, cap)],
            relay_out.at[lax.div(j, 4), row_block(low_bits, cap)],
            send_p.at[j], recv_p.at[j], (rep, xor(me, lax.rem(j, 4))),
        )

    def own_p(n):
        return pltpu.make_async_copy(
            results_ref.at[pl.ds((group // 2 + 4 * n) * cap, cap)],
            relay_out.at[n, row_block(low_bits, cap)],
            keep_r.at[n],
        )

    def rows_of(g):
        start = g * per

        def arrive(k, carry):
            copy_c(k).wait_recv()
            copy_r(k).wait_recv()
            return carry

        lax.fori_loop(max(start, 1), start + per, arrive, 0)
        for n in range(sz.line // 2):
            if (sz.slots // 2 + 4 * n * cap) // 256 == g:
                later[n].wait()
                for k in range(1, 4):
                    copy_f(n, k).wait_recv()
        span = slice(g * 256, (g + 1) * 256)
        x = arrived[span, :]
        arrived_t[:, span] = x.T
        columns = [column_of(scales[start + i, 0:1, :])[:cap, 0:1] for i in range(per)]
        column = jnp.concatenate(columns, axis=0)
        raw = grads_ref[span, :].astype(f32)
        scaled[span, :] = (raw * column).astype(bf16)
        scaled_t[:, span] = scaled[span, :].T

        def part(j, carry):
            cols = row_block(j, step)
            pre = dot_nn(arrived[span, :], win[:, cols])
            grad_hidden = dot_nn(scaled[span, :], wout[:, cols])
            act, slope = gelu_parts(pre)
            hidden[span, cols] = act.astype(bf16)
            pre_grad[span, cols] = (grad_hidden * slope).astype(bf16)
            return carry

        lax.fori_loop(0, sz.ff // step, part, 0)
        back_send[span, :] = dot_nt(pre_grad[span, :], win[...]).astype(bf16)

        def send_back(k, carry):
            copy_b(k).start()
            return carry

        lax.fori_loop(max(start, 1), start + per, send_back, 0)
        results = dot_nt(hidden[span, :], wout[...])
        results_ref[span, :] = (results * column).astype(bf16)
        if g < groups // 2:

            def send_near(k, carry):
                copy_n(k).start()
                return carry

            lax.fori_loop(max(start, 1), start + per, send_near, 0)
        else:
            for j in range(start - group // 2, start - group // 2 + per):
                if j % 4:
                    copy_p(j).start()
                else:
                    own_p(j // 4).start()
        dots = jnp.sum(results * raw, axis=-1, keepdims=True)
        for i in range(per):
            tall = jnp.broadcast_to(dots[i * cap : (i + 1) * cap], (cap, BLK))
            if cap < BLK:
                tall = jnp.concatenate([tall, jnp.zeros((BLK - cap, BLK), f32)], axis=0)
            dots_send[start + i, 0:1, :] = tall.T[0:1, :]

        def send_dots(k, carry):
            copy_d(k).start()
            return carry

        lax.fori_loop(max(start, 1), start + per, send_dots, 0)

    def start_last():
        def sent(k, carry):
            copy_r(k).wait_send()
            return carry

        for g in early:
            lax.fori_loop(max(g * per, 1), (g + 1) * per, sent, 0)
        lax.fori_loop((groups - 1) * per, groups * per, start_r, 0)

    for g in range(groups):
        if g == 1:
            start_last()
        rows_of(g)
    own_back = pltpu.make_async_copy(
        back_send.at[pl.ds(0, cap)], back_out.at[row_block(me, cap)], load.at[4]
    )
    own_back.start()
    own_near = pltpu.make_async_copy(
        results_ref.at[pl.ds(0, cap)], near_out.at[row_block(me, cap)], load.at[5]
    )
    own_near.start()
    dots_out[me] = dots_send[0]

    size = sz.ff // sz.reps
    cut = 512 if size > 512 else size
    subs = size // cut
    pieces = sz.reps // 2 * subs

    def columns_of(parity, i):
        return pl.ds(pl.multiple_of((2 * (i // subs) + parity) * size + (i % subs) * cut, BLK), cut)

    def copy_w(m, i):
        return remote(
            sums.at[m, i], others.at[m, i], send_w.at[m, i], recv_w.at[m, i], (sibling, me)
        )

    def copy_k(m, i):
        return pltpu.make_async_copy(
            totals.at[m, i], (grad_in_out, grad_out_out)[m].at[:, pl.ds(i * cut, cut)], keep_w.at[m, i]
        )

    for i in range(pieces):
        cols = columns_of(1 - core, i)
        sums[0, i] = dot_nn(arrived_t[...], pre_grad[:, cols]).astype(bf16)
        copy_w(0, i).start()
        sums[1, i] = dot_nn(scaled_t[...], hidden[:, cols]).astype(bf16)
        copy_w(1, i).start()
    for i in range(pieces):
        cols = columns_of(core, i)
        for m, left, right in ((0, arrived_t, pre_grad), (1, scaled_t, hidden)):
            total = dot_nn(left[...], right[:, cols])
            copy_w(m, i).wait_recv()
            totals[m, i] = (total + others[m, i].astype(f32)).astype(bf16)
            copy_k(m, i).start()

    def finish(k, carry):
        copy_c(k).wait_send()
        copy_b(k).wait_send()
        copy_d(k).wait_send()
        from_back = remote(
            back_send.at[row_block(k, cap)], back_out.at[row_block(xor(me, k), cap)],
            send_b.at[k], recv_b.at[k], (rep, xor(me, k)),
        )
        from_back.wait_recv()
        from_dots = remote(
            dots_send.at[k], dots_out.at[xor(me, k)], send_d.at[k], recv_d.at[k], (rep, xor(me, k))
        )
        from_dots.wait_recv()
        return carry

    lax.fori_loop(1, group, finish, 0)

    def sent_last(k, carry):
        copy_r(k).wait_send()
        return carry

    lax.fori_loop((groups - 1) * per, groups * per, sent_last, 0)

    def end_near(k, carry):
        copy_n(k).wait()
        return carry

    lax.fori_loop(1, group // 2, end_near, 0)
    for n in range(sz.line // 2):
        for k in range(1, 4):
            copy_f(n, k).wait_send()
    for j in range(group // 2):
        if j % 4:
            copy_p(j).wait()
        else:
            own_p(j // 4).wait()
    own_back.wait()
    own_near.wait()
    for i in range(pieces):
        for m in range(2):
            copy_w(m, i).wait_send()
            copy_k(m, i).wait()


def expert_call(sz, rows, scales, grads, far, weight_in, weight_out):
    group, width, ff, slots = sz.group, sz.width, sz.ff, sz.slots
    shape = jax.ShapeDtypeStruct
    dma = pltpu.SemaphoreType.DMA
    size = ff // sz.reps
    cut = 512 if size > 512 else size
    pieces = sz.reps // 2 * (size // cut)
    return pl.pallas_call(
        functools.partial(expert_kernel, sz),
        out_shape=[
            shape((sz.experts, 8, BLK), f32),
            shape((sz.line // 2, 4 * sz.cap, width), bf16),
            shape((slots, width), bf16),
            shape((slots, width), bf16),
            shape((width, ff // 2), bf16),
            shape((width, ff // 2), bf16),
        ],
        in_specs=[vmem()] + [anywhere()] * 5,
        out_specs=[vmem()] + [anywhere()] * 5,
        scratch_shapes=[
            pltpu.VMEM((width, ff), bf16),
            pltpu.VMEM((width, ff), bf16),
            pltpu.VMEM((slots, width), bf16),
            pltpu.VMEM((group, 8, BLK), f32),
            pltpu.VMEM((width, slots), bf16),
            pltpu.VMEM((slots, width), bf16),
            pltpu.VMEM((width, slots), bf16),
            pltpu.VMEM((slots, ff), bf16),
            pltpu.VMEM((slots, ff), bf16),
            pltpu.VMEM((slots, width), bf16),
            pltpu.VMEM((group, 8, BLK), f32),
            pltpu.VMEM((2, pieces, width, cut), bf16),
            pltpu.VMEM((2, pieces, width, cut), bf16),
            pltpu.VMEM((2, pieces, width, cut), bf16),
            pltpu.VMEM((slots, width), bf16),
            pltpu.VMEM((slots, width), bf16),
            dma((6,)),
        ]
        + [dma((group,))] * 10
        + [dma((2, pieces))] * 3
        + [dma((sz.line // 2,)), dma((sz.line // 2,)), dma((sz.line // 2, 4)), dma((sz.line // 2, 4))]
        + [dma((group // 2,))] * 2,
        compiler_params=pltpu.CompilerParams(
            collective_id=1, has_side_effects=True, vmem_limit_bytes=VMEM_LIMIT
        ),
    )(scales, rows, grads, far, weight_in, weight_out)


def near_onehot(sz):
    lane = iota((1, 3 * BLK), 1)
    distance = jnp.where(lane <= BLK, BLK + lane, lane - 2 * BLK)
    bucket = jnp.where(distance < 16, distance, 16)
    for cutoff in cutoffs:
        bucket = bucket + (distance >= cutoff).astype(jnp.int32)
    per = sz.buckets // sz.group
    shape = (sz.group, sz.rows, 3 * BLK)
    inner = iota(shape, 1)
    named = jnp.where(inner < per, iota(shape, 0) * per + inner, -1)
    return (named == bucket[None]).astype(f32).reshape(sz.width, 3 * BLK).astype(bf16)


def unit_shapes(sz):
    up = lambda n: -(-n // 16) * 16
    return [(up(sz.rows), sz.half)] + [(up(3 * sz.rows), BLK)] * (sz.half // BLK)


def backward_kernel(
    sz,
    len_ref,
    tok_ref,
    cot_ref,
    routes_ref,
    slots_ref,
    n2_ref,
    gate_ref,
    small_ref,
    dots_ref,
    w_hbm,
    qkv_hbm,
    probs_hbm,
    att_hbm,
    resid_hbm,
    pick_hbm,
    results_hbm,
    near_hbm,
    normed_hbm,
    back_hbm,
    out_ref,
    gtok_ref,
    gq_ref,
    gk_ref,
    gv_ref,
    go_ref,
    gsmall_ref,
    *scratch,
):
    units = unit_shapes(sz)
    (
        probs, w_ref, qkv_ref, att_ref, resid_ref, pick_ref, back_ref, returned, total_bf, gres, gatt,
        dqkv, dscore, stacks, normed_t, near_sum, far_sum, sums, wide, packed, packed_rows,
        packed_far, small_mine, small_from, small_final,
        load, load_p, send_r, recv_r, send_x, recv_x, send_m, recv_m,
    ) = scratch[:33]
    buffers = scratch[33:]
    mine = buffers[0::6]
    theirs = buffers[1::6]
    from_sib = buffers[2::6]
    from_one = buffers[3::6]
    from_two = buffers[4::6]
    final = buffers[5::6]
    rep, me, core, sibling = peers(sz)
    seq, width, half, line, group = sz.seq, sz.width, sz.half, sz.line, sz.group
    near = jnp.where(core == 0, 1, 2)
    last = jnp.where(core == 0, 2, 1)
    cap = sz.cap
    blocks = seq // BLK

    def fetch(n, src, dst):
        return pltpu.make_async_copy(src, dst, load.at[n])

    same_half = row_block(lax.div(me, group // 2), sz.slots // 2)
    loads = [
        fetch(0, back_hbm, back_ref),
        fetch(1, pick_hbm, pick_ref),
        fetch(2, resid_hbm, resid_ref),
        fetch(3, w_hbm.at[3], w_ref.at[3]),
        fetch(4, att_hbm, att_ref),
        fetch(5, qkv_hbm, qkv_ref),
        fetch(6, w_hbm.at[pl.ds(0, 3)], w_ref.at[pl.ds(0, 3)]),
        fetch(7, near_hbm.at[same_half], returned.at[same_half]),
        fetch(8, normed_hbm, normed_t),
    ]

    def copy_p(pair, i):
        part = (pair, pl.ds(0, (i + 1) * BLK), pl.ds(2 * i * BLK, 2 * BLK))
        return pltpu.make_async_copy(probs_hbm.at[part], probs.at[part], load_p.at[pair, i])

    def start_p(pair, carry):
        for i in range(blocks):
            copy_p(pair, i).start()
        return carry

    greet(sz, rep, me, sibling)
    for copy in loads[:6]:
        copy.start()
    lax.fori_loop(0, sz.pairs, start_p, 0)
    for copy in loads[6:]:
        copy.start()

    far_planes = range(line // 2, line)
    place_a = lax.div(me, 4)

    def copy_r(z):
        return remote(
            results_hbm.at[z - line // 2], returned.at[row_block(place_a, 4 * cap)],
            send_r.at[z], recv_r.at[z], (rep, xor(me, 4 * z)),
        )

    met(sz)
    for z in far_planes:
        copy_r(z).start()

    far_stages = [4, 5] if line == 4 else list(range(4, 3 + line))

    def copy_x(u, stage):
        if stage == 0:
            src, dst, to = theirs[u], from_sib[u], (sibling, me)
        elif stage == 1:
            src, dst, to = mine[u].at[pl.ds(group // 2, group // 2)], from_one[u], (rep, xor(me, last))
        elif stage == 2:
            src, dst, to = mine[u].at[pl.ds(line, line)], from_two[u].at[pl.ds(0, line)], (rep, xor(me, near))
        elif stage == 3:
            src, dst, to = final[u].at[core], final[u].at[core], (sibling, me)
        elif line == 4:
            if stage == 4:
                src, dst = mine[u].at[pl.ds(1, 2)], from_two[u].at[pl.ds(line, 2)]
                to = (rep, xor(me, 4))
            else:
                src, dst, to = mine[u].at[3], from_two[u].at[line + 2], (rep, xor(me, 12))
        else:
            z = stage - 3
            src, dst, to = mine[u].at[z], from_two[u].at[line + z], (rep, xor(me, 4 * z))
        return remote(src, dst, send_x.at[u, stage], recv_x.at[u, stage], to)

    def add_into(ref, start, stop, other, skip=0):
        def add(p, carry):
            ref[p] = (ref[p].astype(f32) + other[p + skip].astype(f32)).astype(bf16)
            return carry

        lax.fori_loop(start, stop, add, 0)

    def step(u, number):
        if number == 0:
            copy_x(u, 0).start()
        elif number == 1:
            copy_x(u, 0).wait_recv()
            add_into(mine[u], group // 2, group, from_sib[u])
            copy_x(u, 1).start()
            add_into(mine[u], 0, group // 2, from_sib[u])
        elif number == 2:
            copy_x(u, 1).wait_recv()
            add_into(mine[u], line, 2 * line, from_one[u])
            copy_x(u, 2).start()
            add_into(mine[u], 0, line, from_one[u])
        elif number == 3:
            copy_x(u, 2).wait_recv()
            add_into(mine[u], 0, line, from_two[u])
            for stage in far_stages[:1] if line == 4 else far_stages:
                copy_x(u, stage).start()
        elif number == 3.5:
            if line == 4:
                copy_x(u, 4).wait_recv()
                across = mine[u][3].astype(f32) + from_two[u][line + 1].astype(f32)
                mine[u][3] = across.astype(bf16)
                copy_x(u, 5).start()
        elif number == 4:
            total = mine[u][0].astype(f32)
            if line == 4:
                copy_x(u, 5).wait_recv()
                total = total + from_two[u][line].astype(f32) + from_two[u][line + 2].astype(f32)
            else:
                for z in range(1, line):
                    copy_x(u, 3 + z).wait_recv()
                    total = total + from_two[u][line + z].astype(f32)
            final[u][core] = total
            copy_x(u, 3).start()
        else:
            remote(
                final[u].at[1 - core], final[u].at[1 - core], send_x.at[u, 3], recv_x.at[u, 3],
                (sibling, me),
            ).wait_recv()
            for stage in list(range(4)) + far_stages:
                copy_x(u, stage).wait_send()

    def owner_of(p, swap):
        one, two = (last, near) if swap else (near, last)
        rel = lax.rem(p, line) * 4 + lax.rem(lax.div(p, line), 2) * one + lax.div(p, 2 * line) * two
        return xor(me, rel)

    def fill(u, read):
        def put(p, carry):
            mine[u][p] = read(core, owner_of(p, False)).astype(bf16)
            theirs[u][p] = read(1 - core, owner_of(p, True)).astype(bf16)
            return carry

        lax.fori_loop(0, group, put, 0)

    def padded(value, u):
        short = units[u][0] - value.shape[0]
        if short:
            value = jnp.concatenate([value, jnp.zeros((short, value.shape[1]), f32)], axis=0)
        return value

    small = small_ref[...].astype(f32)[:, : sz.rows].reshape(width, BLK)
    small_t = small.T
    gain_one = small_t[GAIN_ONE : GAIN_ONE + 1]
    gain_two = small_t[GAIN_TWO : GAIN_TWO + 1]
    router = small.astype(bf16)
    length = len_ref[0]

    places = jnp.concatenate(
        [routes_ref[...], slots_ref[...], jnp.zeros((4, seq), jnp.int32)], axis=0
    )
    places = places.astype(f32).T.astype(jnp.int32)
    route = places[:, 0:2]
    target = target_slots(sz, route, places[:, 2:4])
    first, second = target[:, 0:1], target[:, 1:2]
    dot_one = jnp.zeros((seq, BLK), f32)
    dot_two = jnp.zeros((seq, BLK), f32)
    lanes = iota((1, BLK), 1)
    per = BLK // cap
    for j in range(sz.slots // BLK):
        row = jnp.concatenate([dots_ref[j * per + e, 0:1, 0:cap] for e in range(per)], axis=1)
        lane = lanes + j * BLK
        dot_one = dot_one + jnp.where(first == lane, row, 0.0)
        dot_two = dot_two + jnp.where(second == lane, row, 0.0)
    dot_one = jnp.sum(dot_one, axis=-1, keepdims=True)
    dot_two = jnp.sum(dot_two, axis=-1, keepdims=True)
    share = gate_ref[:, 0:1] * gate_ref[:, 1:2] * (dot_one - dot_two)
    grad_logits = share * (
        (lanes == route[:, 0:1]).astype(f32) - (lanes == route[:, 1:2]).astype(f32)
    )
    grad_logits = grad_logits.astype(bf16)
    packed[...] = dot_tn(n2_ref[...], grad_logits)

    for copy in loads[:3]:
        copy.wait()
    gain_two_grad = jnp.zeros((1, width), f32)
    for i in range(blocks):
        rows = slice(i * BLK, (i + 1) * BLK)
        grad = dot_nn(pick_ref[rows, :], back_ref[...]) + dot_nt(grad_logits[rows], router)
        resid = resid_ref[rows, :]
        scale = lax.rsqrt(jnp.mean(resid * resid, axis=-1, keepdims=True) + norm_eps)
        gain_two_grad = gain_two_grad + jnp.sum(grad * resid * scale, axis=0, keepdims=True)
        valid = (iota((BLK, 1), 0) + i * BLK < length).astype(f32)
        grad_out = cot_ref[rows, :].astype(f32) * valid
        moved = grad * gain_two
        mean = jnp.mean(moved * resid, axis=-1, keepdims=True)
        total = grad_out + scale * moved - resid * (scale * scale * scale * mean)
        gres[rows, :] = total
        total_bf[rows, :] = total.astype(bf16)
    loads[3].wait()
    loads[4].wait()
    gatt[...] = dot_nt(total_bf[...], w_ref[3]).astype(bf16)
    wide[...] = dot_tn(att_ref[...], total_bf[...])

    def read_o(h, s):
        cols = pl.ds(pl.multiple_of(h * half, BLK), half)
        return padded(wide[row_block8(s, sz.rows), cols], 0)

    fill(0, read_o)
    step(0, 0)

    loads[8].wait()
    step(0, 1)

    low = iota((1, BLK), 1) < width // sz.heads
    halves = [jnp.where(low, 1.0, 0.0).astype(bf16), jnp.where(low, 0.0, 1.0).astype(bf16)]

    size = width // sz.heads
    loads[5].wait()

    def back_pair(pair):
        cols = row_block(pair, BLK)
        query = qkv_ref[0, :, cols]
        key = qkv_ref[1, :, cols]
        key_t = key.T
        value = qkv_ref[2, :, cols]
        grads = gatt[:, cols]
        for i in range(blocks):
            copy_p(pair, i).wait()
        for i in range(blocks):
            rows = slice(i * BLK, (i + 1) * BLK)
            keys = (i + 1) * BLK
            at = slice(2 * i * BLK, 2 * (i + 1) * BLK)
            both = jnp.concatenate([grads[rows] * halves[0], grads[rows] * halves[1]], axis=0)
            stacks[0, at, :] = jnp.concatenate(
                [query[rows] * halves[0], query[rows] * halves[1]], axis=0
            )
            stacks[1, at, :] = both
            soft = probs[pair, :keys, at].astype(f32)
            product = soft * dot_nt(value[:keys], both)
            grad_score = product - soft * jnp.sum(product, axis=0, keepdims=True)
            if i == 0:
                near_sum[pair, :BLK] = jnp.zeros((BLK, 2 * BLK), f32)
                near_sum[pair, BLK:] = grad_score
                far_sum[pair] = jnp.zeros((8, 2 * BLK), f32)
            else:
                near_sum[pair] += grad_score[keys - 2 * BLK :]
                if i >= 2:
                    far = grad_score[: keys - 2 * BLK].reshape((keys - 2 * BLK) // 8, 8, 2 * BLK)
                    far_sum[pair] += jnp.sum(far, axis=0)
            low_score = grad_score.astype(bf16)
            dscore[:keys, at] = low_score
            moved = dot_nn(key_t[:, :keys], low_score)
            moved = jnp.concatenate([moved[:size, :BLK], moved[size:, BLK:]], axis=0)
            dqkv[0, rows, cols] = (moved.T * score_scale).astype(bf16)
        for i in range(blocks):
            rows = slice(i * BLK, (i + 1) * BLK)
            below = slice(2 * i * BLK, 2 * seq)
            grad_key = dot_nn(dscore[rows, below], stacks[0, below, :])
            grad_value = dot_nn(probs[pair, rows, below], stacks[1, below, :])
            dqkv[1, rows, cols] = (grad_key * score_scale).astype(bf16)
            dqkv[2, rows, cols] = grad_value.astype(bf16)

    parts = half // BLK
    for j in range(parts):

        def one(h, carry, j=j):
            pair = h * parts + j
            back_pair(pair)
            cols = row_block(pair, BLK)
            grads = jnp.concatenate([dqkv[m, :, cols] for m in range(3)], axis=1)
            sums[h] = dot_nn(normed_t[...], grads)
            return carry

        one(0, 0)
        for u, n in PLAN_H[j]:
            step(u, n)
        one(1, 0)

        def read_j(h, s):
            rows = row_block8(s, sz.rows)
            value = sums[h, rows, :]
            return padded(
                jnp.concatenate([value[:, m * BLK : (m + 1) * BLK] for m in range(3)], axis=0), 1
            )

        fill(1 + j, read_j)
        for u, n in PLAN_J[j]:
            step(u, n)

    loads[6].wait()
    gain_one_grads = []

    def input_grad(i):
        rows = slice(i * BLK, (i + 1) * BLK)
        grad = dot_nt(dqkv[0, rows, :], w_ref[0]) + dot_nt(dqkv[1, rows, :], w_ref[1])
        grad = grad + dot_nt(dqkv[2, rows, :], w_ref[2])
        x = tok_ref[rows, :].astype(f32)
        scale = lax.rsqrt(jnp.mean(x * x, axis=-1, keepdims=True) + norm_eps)
        gain_one_grads.append(jnp.sum(grad * x * scale, axis=0, keepdims=True))
        moved = grad * gain_one
        mean = jnp.mean(moved * x, axis=-1, keepdims=True)
        gtok_ref[rows, :] = gres[rows, :] + scale * moved - x * (scale * scale * scale * mean)

    flip = (iota((2 * BLK, 2 * BLK), 0) + iota((2 * BLK, 2 * BLK), 1) == 2 * BLK - 1)
    flip = flip.astype(f32).astype(bf16)

    def bucket_sums(pair, carry):
        turned = dot_nn(flip, near_sum[pair].astype(bf16))
        far = jnp.sum(far_sum[pair], axis=0, keepdims=True)
        for b in range(2):
            tall = jnp.concatenate(
                [turned[:, b * BLK : (b + 1) * BLK], jnp.zeros((2 * BLK, 2 * BLK), f32)], axis=1
            )
            rolled = pltpu.roll(tall, BLK + 1, 1, stride=1, stride_axis=0)
            packed_rows[pl.ds(2 * pair + b, 1), :] = jnp.sum(rolled, axis=0, keepdims=True)
            packed_far[pl.ds(2 * pair + b, 1), :] = far[:, b * BLK : (b + 1) * BLK]
        return carry

    def table_grad():
        packed_rows[...] = jnp.zeros_like(packed_rows)
        packed_far[...] = jnp.zeros_like(packed_far)
        lax.fori_loop(0, sz.pairs, bucket_sums, 0)
        onehot = near_onehot(sz)
        values = packed_rows[...]
        upper = values.astype(bf16)
        lower = (values - upper.astype(f32)).astype(bf16)
        table = dot_nt(upper, onehot) + dot_nt(lower, onehot)
        far = jnp.sum(packed_far[...], axis=-1, keepdims=True)
        one_far = jnp.broadcast_to((lanes == 0).astype(f32), (8, BLK)).astype(bf16)
        farthest = dot_nt(one_far, onehot[:, :BLK])[0:1]
        return table + far * farthest

    def copy_m(k):
        return remote(
            small_mine.at[xor(me, k)], small_from.at[k], send_m.at[k], recv_m.at[k], (rep, xor(me, k))
        )

    def small_start(table):
        gain_one_grad = gain_one_grads[0]
        for grad in gain_one_grads[1:]:
            gain_one_grad = gain_one_grad + grad
        tall = jnp.concatenate(
            [
                jnp.zeros((GAIN_ONE, width), f32),
                gain_one_grad,
                gain_two_grad,
                jnp.zeros((TABLE - GAIN_TWO - 1, width), f32),
                table,
                jnp.zeros((BLK - TABLE - 16, width), f32),
            ],
            axis=0,
        )
        whole = (packed[...] + tall.T).reshape(group, sz.rows, BLK)
        if sz.small != sz.rows:
            whole = jnp.concatenate(
                [whole, jnp.zeros((group, sz.small - sz.rows, BLK), f32)], axis=1
            )
        small_mine[...] = whole.astype(bf16)

        def start_m(k, carry):
            copy_m(k).start()
            return carry

        lax.fori_loop(1, group, start_m, 0)

    def copy_f():
        return remote(
            small_final.at[core], small_final.at[core], send_m.at[0], recv_m.at[0], (sibling, me)
        )

    def small_sum():
        small_final[core] = small_mine[me].astype(f32)

        def add(k, carry):
            copy_m(k).wait()
            small_final[core] += small_from[k].astype(f32)
            return carry

        lax.fori_loop(1, group, add, 0)
        copy_f().start()

    def small_end():
        remote(
            small_final.at[1 - core], small_final.at[1 - core], send_m.at[0], recv_m.at[0],
            (sibling, me),
        ).wait_recv()
        gsmall_ref[...] = small_final[0] + small_final[1]
        copy_f().wait_send()

    def results():
        for z in far_planes:
            remote(
                results_hbm.at[z - line // 2], returned.at[row_block(xor(place_a, z), 4 * cap)],
                send_r.at[z], recv_r.at[z], (rep, xor(me, 4 * z)),
            ).wait_recv()
        loads[7].wait()
        for i in range(blocks):
            rows = slice(i * BLK, (i + 1) * BLK)
            valid = (iota((BLK, 1), 0) + i * BLK < length).astype(f32)
            total = resid_ref[rows, :] + dot_nn(pick_ref[rows, :], returned[...])
            out_ref[rows, :] = (total * valid).astype(bf16)

    table = None
    for act in PLAN_T:
        if act == "T":
            table = table_grad()
        elif act == "M":
            small_start(table)
        elif act == "R":
            results()
        elif act == "m":
            small_sum()
        elif act == "e":
            small_end()
        elif isinstance(act, int):
            input_grad(act)
        else:
            step(*act)
    for u in range(1, 1 + parts):
        step(u, 5)
    for h in range(2):
        cols = slice(h * half, (h + 1) * half)
        go_ref[:, cols] = final[0][h, : sz.rows]
        for j in range(parts):
            at = slice(h * half + j * BLK, h * half + (j + 1) * BLK)
            for m, ref in enumerate((gq_ref, gk_ref, gv_ref)):
                ref[:, at] = final[1 + j][h, m * sz.rows : (m + 1) * sz.rows]

    for z in far_planes:
        copy_r(z).wait_send()


def backward_call(sz, lengths, tokens, cotangent, routes, slots, saved, results, near, back, dots):
    seq, width, group, line = sz.seq, sz.width, sz.group, sz.line
    shape = jax.ShapeDtypeStruct
    dma = pltpu.SemaphoreType.DMA
    w, qkv, probs, att, resid, pick, n2, gate, small, normed = saved
    units = unit_shapes(sz)
    buffers = []
    for rows, cols in units:
        buffers += [
            pltpu.VMEM((group, rows, cols), bf16),
            pltpu.VMEM((group, rows, cols), bf16),
            pltpu.VMEM((group, rows, cols), bf16),
            pltpu.VMEM((group // 2, rows, cols), bf16),
            pltpu.VMEM((2 * line, rows, cols), bf16),
            pltpu.VMEM((2, rows, cols), f32),
        ]
    dense = shape((sz.rows, width), f32)
    return pl.pallas_call(
        functools.partial(backward_kernel, sz),
        out_shape=[
            shape((seq, width), bf16),
            shape((seq, width), f32),
            dense,
            dense,
            dense,
            dense,
            shape((sz.small, BLK), f32),
        ],
        in_specs=[pl.BlockSpec(memory_space=pltpu.SMEM)] + [vmem()] * 8 + [anywhere()] * 10,
        out_specs=[vmem()] * 7,
        scratch_shapes=[
            pltpu.VMEM((sz.pairs, seq, 2 * seq), bf16),
            pltpu.VMEM((4, width, width), bf16),
            pltpu.VMEM((3, seq, width), bf16),
            pltpu.VMEM((seq, width), bf16),
            pltpu.VMEM((seq, width), f32),
            pltpu.VMEM((seq, sz.slots), bf16),
            pltpu.VMEM((sz.slots, width), bf16),
            pltpu.VMEM((sz.slots, width), bf16),
            pltpu.VMEM((seq, width), bf16),
            pltpu.VMEM((seq, width), f32),
            pltpu.VMEM((seq, width), bf16),
            pltpu.VMEM((3, seq, width), bf16),
            pltpu.VMEM((seq, 2 * seq), bf16),
            pltpu.VMEM((2, 2 * seq, BLK), bf16),
            pltpu.VMEM((width, seq), bf16),
            pltpu.VMEM((sz.pairs, 2 * BLK, 2 * BLK), f32),
            pltpu.VMEM((sz.pairs, 8, 2 * BLK), f32),
            pltpu.VMEM((2, width, 3 * BLK), f32),
            pltpu.VMEM((width, width), f32),
            pltpu.VMEM((width, BLK), f32),
            pltpu.VMEM((16, 3 * BLK), f32),
            pltpu.VMEM((16, BLK), f32),
            pltpu.VMEM((group, sz.small, BLK), bf16),
            pltpu.VMEM((group, sz.small, BLK), bf16),
            pltpu.VMEM((2, sz.small, BLK), f32),
            dma((9,)),
            dma((sz.pairs, seq // BLK)),
            dma((group,)),
            dma((group,)),
            dma((len(units), 3 + line)),
            dma((len(units), 3 + line)),
            dma((group,)),
            dma((group,)),
        ]
        + buffers,
        compiler_params=pltpu.CompilerParams(
            collective_id=2, has_side_effects=True, vmem_limit_bytes=VMEM_LIMIT
        ),
    )(
        lengths, tokens, cotangent, routes, slots, n2, gate, small, dots, w, qkv, probs, att, resid,
        pick, results, near, normed, back,
    )


def finish_kernel(
    sz, cuts, in_ref, out_ref, result_ref, tokens_ref, q_ref, k_ref, v_ref, o_ref, small_ref,
    to_in, to_out, to_result, to_tokens, to_q, to_k, to_v, to_o, to_one, to_two, to_router, to_table,
    *scratch,
):
    held, wide, load, store = scratch[:8], scratch[8:10], scratch[10], scratch[11]
    moves = []

    def move(n, src, dst, parts):
        size = src.shape[0] // parts
        for i in range(parts):
            at = pl.ds(i * size, size)
            moves.append((n, at, src, dst))

    move(2, result_ref, to_result, 1)
    move(3, tokens_ref, to_tokens, 2)
    for n, src, dst in ((4, q_ref, to_q), (5, k_ref, to_k), (6, v_ref, to_v), (7, o_ref, to_o)):
        move(n, src, dst, 1)
    move(0, in_ref, to_in, cuts)
    move(1, out_ref, to_out, cuts)
    ins, outs = [], []
    for i, (n, at, src, dst) in enumerate(moves):
        ins.append(pltpu.make_async_copy(src.at[at], held[n].at[at], load.at[i]))
        kept = wide[n] if n < 2 else held[n]
        outs.append(pltpu.make_async_copy(kept.at[at], dst.at[at], store.at[i]))
    for copy in ins:
        copy.start()
    small = small_ref[...]
    tall = jnp.concatenate([small, jnp.zeros((BLK - sz.small, BLK), f32)], axis=0).T
    to_router[...] = tall[: sz.experts, : sz.rows]
    to_one[...] = tall[GAIN_ONE : GAIN_ONE + 1, : sz.rows]
    to_two[...] = tall[GAIN_TWO : GAIN_TWO + 1, : sz.rows]
    to_table[...] = small[: to_table.shape[0], TABLE : TABLE + sz.heads]
    for (n, at, src, dst), came, goes in zip(moves, ins, outs):
        came.wait()
        if n < 2:
            wide[n][at, :] = held[n][at, :].astype(f32)
        goes.start()
    for copy in outs:
        copy.wait()


def finish_call(sz, grad_in, grad_out, result, tokens, dense, small):
    shape = jax.ShapeDtypeStruct
    cuts = 6
    whole = [grad_in, grad_out, result, tokens, *dense]
    kinds = [f32, f32] + [x.dtype for x in whole[2:]]
    return pl.pallas_call(
        functools.partial(finish_kernel, sz, cuts),
        out_shape=[shape(x.shape, kind) for x, kind in zip(whole, kinds)]
        + [
            shape((1, sz.rows), f32),
            shape((1, sz.rows), f32),
            shape((sz.experts, sz.rows), f32),
            shape((sz.buckets // sz.group, sz.heads), f32),
        ],
        in_specs=[anywhere()] * 8 + [vmem()],
        out_specs=[anywhere()] * 8 + [vmem()] * 4,
        scratch_shapes=[pltpu.VMEM(x.shape, x.dtype) for x in whole]
        + [pltpu.VMEM(x.shape, f32) for x in whole[:2]]
        + [pltpu.SemaphoreType.DMA((2 * cuts + 8,))] * 2,
        compiler_params=pltpu.CompilerParams(vmem_limit_bytes=VMEM_LIMIT),
    )(*whole, small)


def shards(
    tokens, lengths, routes, slots, norm_one, w_query, w_key, w_value, w_output, bias_table, norm_two,
    router, expert_in, expert_out, cotangent, *, reps, group,
):
    seq, width = tokens.shape
    rows = w_query.shape[0]
    heads = bias_table.shape[1]
    experts = router.shape[1]
    sz = Sizes(
        reps, group, seq, width, heads, experts, expert_in.shape[2], rows, bias_table.shape[0] * group
    )
    parameters = (norm_one[None], norm_two[None], router.T, bias_table)
    weights = (w_query, w_key, w_value, w_output)
    routes, slots = routes.T, slots.T
    (w, qkv, probs, att, resid, grads, far, normed, pick, n2, sent, scales, gate, small_all) = forward_call(
        sz, lengths, tokens, routes, slots, parameters, weights, cotangent
    )
    dots, results, near, back, grad_in, grad_out = expert_call(sz, sent, scales, grads, far, expert_in, expert_out)
    saved = (w, qkv, probs, att, resid, pick, n2, gate, small_all, normed)
    output, grad_tokens, gq, gk, gv, go, gsmall = backward_call(
        sz, lengths, tokens, cotangent, routes, slots, saved, results, near, back, dots
    )
    if reps > 2:
        same = [[r for r in range(reps) if r % 2 == c] for c in range(2)]
        grad_in, grad_out = (
            lax.psum_scatter(grad, "rep", scatter_dimension=1, axis_index_groups=same, tiled=True)
            for grad in (grad_in, grad_out)
        )
        gq, gk, gv, go, gsmall = lax.psum((gq, gk, gv, go, gsmall), "rep", axis_index_groups=same)
    (grad_in, grad_out, output, grad_tokens, gq, gk, gv, go, g_one, g_two, g_router, g_table) = (
        finish_call(sz, grad_in, grad_out, output, grad_tokens, (gq, gk, gv, go), gsmall)
    )
    return (
        output,
        grad_tokens,
        g_one[0],
        gq,
        gk,
        gv,
        go,
        g_table,
        g_two[0],
        g_router.T,
        grad_in[None],
        grad_out[None],
    )


def solution(mesh):
    both = ("rep", "shard")
    return jax.shard_map(
        functools.partial(shards, reps=mesh.shape["rep"], group=mesh.shape["shard"]),
        mesh=mesh,
        in_specs=(
            P(both, None),
            P(both),
            P(both, None),
            P(both, None),
            P("shard"),
            P("shard", None),
            P("shard", None),
            P("shard", None),
            P("shard", None),
            P("shard", None),
            P("shard"),
            P("shard", None),
            P("shard", None, None),
            P("shard", None, None),
            P(both, None),
        ),
        out_specs=(
            P(both, None),
            P(both, None),
            P("shard"),
            P("shard", None),
            P("shard", None),
            P("shard", None),
            P("shard", None),
            P("shard", None),
            P("shard"),
            P("shard", None),
            P("shard", None, "rep"),
            P("shard", None, "rep"),
        ),
        check_vma=False,
    )
```

```python
import functools

import jax
import jax.numpy as jnp
from jax import lax
from jax.experimental import pallas as pl
from jax.experimental.pallas import tpu as pltpu
from jax.sharding import PartitionSpec as P

MESH = pl.DeviceIdType.MESH
norm_eps = 1e-06
score_scale = 0.125
cutoffs = (19, 21, 24, 27, 31, 35, 40, 46, 52, 59, 67, 77, 87, 99, 113)
f32 = jnp.float32
bf16 = jnp.bfloat16
GAIN_ONE, GAIN_TWO, TABLE = 64, 65, 80
BLK = 128
VMEM_LIMIT = 60 * 2**20
NEG = -1e30
PLAN_H = ((), ((1, 1),), ((2, 1),))
PLAN_J = (((1, 0),), ((2, 0), (0, 2)), ((3, 0), (1, 2), (0, 3)))
PLAN_T = (
    "T", (3, 1), (2, 2), 0, (1, 3), (0, 3.5), 1, (3, 2), (2, 3), (1, 3.5), 2, 3, "M", (3, 3), (2, 3.5), (1, 4), (0, 4),
    "R", (3, 3.5), "m", (2, 4), (0, 5), (3, 4), "e",
)


def dot_nn(a, b):
    return lax.dot_general(a, b, (((1,), (0,)), ((), ())), preferred_element_type=f32)


def dot_nt(a, b):
    return lax.dot_general(a, b, (((1,), (1,)), ((), ())), preferred_element_type=f32)


def dot_tn(a, b):
    return lax.dot_general(a, b, (((0,), (0,)), ((), ())), preferred_element_type=f32)


def iota(shape, dim):
    return lax.broadcasted_iota(jnp.int32, shape, dim)


class Sizes:
    def __init__(self, reps, group, seq, width, heads, experts, ff, rows, buckets):
        self.reps, self.group, self.seq, self.width = reps, group, seq, width
        self.heads, self.experts, self.ff, self.rows = heads, experts, ff, rows
        self.buckets = buckets
        self.cap = 2 * seq // experts
        self.slots = experts * self.cap
        self.line = group // 4
        self.half = width // 2
        self.small = -(-rows // 16) * 16
        self.share = self.small // 16
        self.piece = 4 * rows
        self.pairs = heads // 2
        self.chunks = ((0, self.piece),)

    def relative(self, half, place):
        first, second = (1, 2) if half == 0 else (2, 1)
        line = place % self.line
        return line * 4 + (place // self.line % 2) * first + (place // (2 * self.line)) * second


def peers(sz):
    rep = lax.axis_index("rep")
    me = lax.axis_index("shard")
    return rep, me, lax.rem(rep, 2), rep + 1 - 2 * lax.rem(rep, 2)


def xor(a, b):
    return jnp.bitwise_xor(a, b)


def greet(sz, rep, me, sibling):
    barrier = pltpu.get_barrier_semaphore()

    def signal(k, carry):
        pl.semaphore_signal(barrier, inc=1, device_id=(rep, xor(me, k)), device_id_type=MESH)
        return carry

    lax.fori_loop(1, sz.group, signal, 0)
    pl.semaphore_signal(barrier, inc=1, device_id=(sibling, me), device_id_type=MESH)


def met(sz):
    pl.semaphore_wait(pltpu.get_barrier_semaphore(), sz.group)


def remote(src, dst, send, recv, device):
    return pltpu.make_async_remote_copy(
        src_ref=src, dst_ref=dst, send_sem=send, recv_sem=recv, device_id=device, device_id_type=MESH
    )


def send_order(group):
    order = list(range(group // 2, group)) + list(range(1, group // 2))
    return order


def row_block(index, size):
    return pl.ds(pl.multiple_of(index * size, size), size)


def row_block8(index, size):
    return pl.ds(pl.multiple_of(index * size, 8), size)


def target_slots(sz, routes, slots):
    return jnp.where(slots < sz.cap, routes * sz.cap + slots, -1)


def bias_tiles(sz, small_t, vector, tiles):
    lane = iota((1, 3 * BLK), 1)
    distance = jnp.where(lane <= BLK, BLK - lane, 4 * BLK - lane)
    bucket = jnp.where(distance < 16, distance, 16)
    for cutoff in cutoffs:
        bucket = bucket + (distance >= cutoff).astype(jnp.int32)
    per = sz.buckets // sz.group
    shape = (sz.group, sz.rows, 3 * BLK)
    inner = iota(shape, 1)
    named = jnp.where(inner < per, iota(shape, 0) * per + inner, -1)
    onehot = (named == bucket[None]).astype(f32).reshape(sz.width, 3 * BLK).astype(bf16)
    table = small_t[TABLE : TABLE + 16].astype(bf16)
    values = dot_nn(table, onehot)
    values = values - values[:, 0:1]
    vector[...] = jnp.where((lane > BLK) & (lane < 2 * BLK), NEG, values)

    def tile(pair, carry):
        for b in range(2):
            row = jnp.broadcast_to(vector[pl.ds(2 * pair + b, 1), :], (BLK, 3 * BLK))
            turned = pltpu.roll(row, 0, 1, stride=1, stride_axis=0)[:, : 2 * BLK]
            tiles[pair, :, b * BLK : (b + 1) * BLK] = turned.T
        return carry

    lax.fori_loop(0, sz.pairs, tile, 0)


def forward_kernel(
    sz,
    len_ref,
    tok_ref,
    routes_ref,
    slots_ref,
    one_ref,
    two_ref,
    router_ref,
    table_ref,
    wq_ref,
    wk_ref,
    wv_ref,
    wo_ref,
    cot_ref,
    w_out,
    qkv_out,
    probs_out,
    att_out,
    resid_out,
    garr_out,
    far_out,
    normed_out,
    pick_out,
    n2_hbm,
    rows_hbm,
    cs_out,
    gate_out,
    small_out,
    pieces,
    gsend,
    relay,
    vector,
    tiles,
    probs,
    wide,
    whole,
    qkv,
    att,
    resid_all,
    pick_all,
    mask,
    send_z,
    recv_z,
    send_b,
    recv_b,
    send_c,
    recv_c,
    send_s,
    recv_s,
    send_m,
    recv_m,
    send_g,
    recv_g,
    send_p,
    keep,
    keep_rows,
    small_ref,
    small_wide,
    small_tall,
    normed_t,
    n2_out,
    rows_out,
):
    rep, me, core, sibling = peers(sz)
    seq, width, half, line = sz.seq, sz.width, sz.half, sz.line
    place_a = me // 4
    near = jnp.where(core == 0, 1, 2)
    last = jnp.where(core == 0, 2, 1)

    greet(sz, rep, me, sibling)

    small_wide[...] = jnp.zeros_like(small_wide)
    small_wide[0 : sz.experts, 0 : sz.rows] = router_ref[...].astype(f32)
    small_wide[GAIN_ONE : GAIN_ONE + 1, 0 : sz.rows] = one_ref[...].astype(f32)
    small_wide[GAIN_TWO : GAIN_TWO + 1, 0 : sz.rows] = two_ref[...].astype(f32)
    few = table_ref.shape[0]
    small_ref[...] = small_wide[...].T[: sz.small].astype(bf16)
    table = table_ref[...].astype(f32)
    small_tall[...] = small_ref[...].astype(f32)
    small_tall[0:few, TABLE : TABLE + sz.heads] = table
    small_ref[...] = small_tall[...].astype(bf16)

    for h in range(2):
        cols = slice(h * half, (h + 1) * half)
        if sz.rows % 16 == 0:
            for m, ref in enumerate((wq_ref, wk_ref, wv_ref, wo_ref)):
                pieces[h, 0, m * sz.rows : (m + 1) * sz.rows, :] = ref[:, cols]
        else:
            stacked = [ref[:, cols].astype(f32) for ref in (wq_ref, wk_ref, wv_ref, wo_ref)]
            pieces[h, 0] = jnp.concatenate(stacked, axis=0).astype(bf16)

    met(sz)

    chunks = sz.chunks

    def block(ch, slot):
        lo, hi = chunks[ch]
        return pieces.at[core, slot, pl.ds(lo, hi - lo)]

    def copy_z(ch, up, source, to):
        slot = xor(source, to)
        return remote(
            block(ch, xor(source, place_a)),
            block(ch, slot),
            send_z.at[ch, up, xor(source, place_a)],
            recv_z.at[ch, slot],
            (rep, me + (to - place_a) * 4),
        )

    def copy_b(ch, i):
        return remote(
            block(ch, i),
            block(ch, line + i),
            send_b.at[ch, i],
            recv_b.at[ch, i],
            (rep, xor(me, near)),
        )

    def copy_c(ch, i):
        return remote(
            block(ch, i),
            block(ch, 2 * line + i),
            send_c.at[ch, i],
            recv_c.at[ch, i],
            (rep, xor(me, last)),
        )

    def copy_s(ch, i):
        return remote(
            block(ch, i), block(ch, i), send_s.at[ch, i], recv_s.at[ch, i], (sibling, me)
        )

    def forward_z(ch, t):
        for up, step in ((1, 1), (0, -1)):
            source = place_a - step * t
            to = place_a + step
            there = (source >= 0) & (source < line)
            onward = there & (to >= 0) & (to < line)

            @pl.when(there)
            def _(up=up, source=source, to=to, onward=onward):
                slot = xor(source, place_a)
                if t > 0:
                    remote(
                        block(ch, slot), block(ch, slot), send_z.at[ch, up, slot],
                        recv_z.at[ch, slot], (rep, me),
                    ).wait_recv()

                @pl.when(onward)
                def _():
                    copy_z(ch, up, source, to).start()

                if t > 0:
                    copy_b(ch, slot).start()
                    copy_c(ch, slot).start()
                    copy_s(ch, slot).start()

    def wait_sent_z(ch):
        for t in range(line - 1):
            for up, step in ((1, 1), (0, -1)):
                source = place_a - step * t
                to = place_a + step
                onward = (source >= 0) & (source < line) & (to >= 0) & (to < line)

                @pl.when(onward)
                def _(up=up, source=source, to=to):
                    copy_z(ch, up, source, to).wait_send()

    def start_own(ch):
        forward_z(ch, 0)
        copy_b(ch, 0).start()
        copy_c(ch, 0).start()

    def from_b(ch, i):
        copy_b(ch, i).wait_recv()
        copy_c(ch, line + i).start()
        copy_s(ch, line + i).start()

    def from_c(ch, i):
        copy_c(ch, i).wait_recv()
        copy_s(ch, 2 * line + i).start()

    def each(ch, do, start, stop):
        def one(i, carry):
            do(ch, i)
            return carry

        lax.fori_loop(start, stop, one, 0)

    def gather_stages(ch):
        def begin():
            from_b(ch, 0)
            forward_z(ch, 1)

        def middle():
            for t in range(2, line):
                forward_z(ch, t)

        return (
            begin,
            middle,
            lambda: each(ch, from_b, 1, line),
            lambda: each(ch, from_c, 0, line),
            lambda: each(ch, from_c, line, 2 * line),
        )

    def gather(ch):
        for stage in gather_stages(ch):
            stage()

    def finish(ch):
        def sent_b(i, carry):
            copy_b(ch, i).wait_send()
            return carry

        def sent_c(i, carry):
            copy_c(ch, i).wait_send()
            return carry

        def sent_s(i, carry):
            copy_s(ch, i).wait_send()
            return carry

        wait_sent_z(ch)
        lax.fori_loop(0, line, sent_b, 0)
        lax.fori_loop(0, 2 * line, sent_c, 0)
        lax.fori_loop(1, sz.group, sent_s, 0)

    def from_sibling(ch):
        def wait(i, carry):
            lo, hi = chunks[ch]
            other = pieces.at[1 - core, i, pl.ds(lo, hi - lo)]
            remote(other, other, send_s.at[ch, i], recv_s.at[ch, i], (sibling, me)).wait_recv()
            return carry

        lax.fori_loop(1, sz.group, wait, 0)

    chunk_rest, chunk_last = 0, len(chunks) - 1
    start_own(chunk_rest)

    def copy_m(k):
        return remote(
            small_ref, small_out.at[me], send_m.at[k], recv_m.at[k], (rep, xor(me, k))
        )

    def start_m(k, carry):
        copy_m(k).start()
        return carry

    lax.fori_loop(1, sz.group, start_m, 0)
    small_out[me] = small_ref[...]

    def keep_copy(n, src, dst):
        return pltpu.make_async_copy(src, dst, keep.at[n])

    places = jnp.concatenate(
        [routes_ref[...], slots_ref[...], jnp.zeros((4, seq), jnp.int32)], axis=0
    )
    places = places.astype(f32).T.astype(jnp.int32)
    route = places[:, 0:2]
    slot = places[:, 2:4]
    target = target_slots(sz, route, slot)
    first, second = target[:, 0:1], target[:, 1:2]
    wide_lane = iota((1, 256), 1)
    for j in range(sz.slots // 256):
        lane = wide_lane + j * 256
        pick = ((first == lane) | (second == lane)).astype(f32).astype(bf16)
        pick_all[:, j * 256 : (j + 1) * 256] = pick
        gsend[j * 256 : (j + 1) * 256, :] = dot_tn(pick, cot_ref[...]).astype(bf16)
    keep_copy(0, pick_all, pick_out).start()

    low_bits = lax.rem(me, 4)

    def copy_far(z):
        return remote(
            gsend.at[row_block(xor(place_a, z), 4 * sz.cap)],
            relay.at[z],
            send_g.at[4 * z],
            recv_g.at[4 * z],
            (rep, xor(me, 4 * z)),
        )

    def copy_plane(z, k):
        if z == 0:
            src = gsend.at[row_block(xor(me, k), sz.cap)]
        else:
            src = relay.at[z, row_block(xor(low_bits, k), sz.cap)]
        return remote(
            src,
            garr_out.at[pl.ds((4 * z + k) * sz.cap, sz.cap)],
            send_g.at[4 * z + k],
            recv_g.at[4 * z + k],
            (rep, xor(me, k)),
        )

    def own_rows(z):
        if z == 0:
            src = gsend.at[row_block(me, sz.cap)]
        else:
            src = relay.at[z, row_block(low_bits, sz.cap)]
        return pltpu.make_async_copy(
            src, garr_out.at[pl.ds(4 * z * sz.cap, sz.cap)], keep_rows.at[z]
        )

    def keep_far(z):
        return pltpu.make_async_copy(
            relay.at[z], far_out.at[z - line // 2], keep_rows.at[z]
        )

    def pass_on(z):
        if z > 0:
            copy_far(z).wait_recv()
        own_rows(z).start()
        for k in range(1, 4):
            copy_plane(z, k).start()

    far_order = list(range(line // 2, line)) + list(range(1, line // 2))
    begin, middle, rest_b, low_c, high_c = gather_stages(chunk_rest)
    begin()
    middle()
    rest_b()
    for z in far_order:
        copy_far(z).start()

    def wait_m(k, carry):
        remote(
            small_ref, small_out.at[xor(me, k)], send_m.at[k], recv_m.at[k], (rep, xor(me, k))
        ).wait()
        return carry

    lax.fori_loop(1, sz.group, wait_m, 0)
    small = small_out[...].astype(f32)[:, : sz.rows].reshape(width, BLK)
    small_t = small.T
    gain_one = small_t[GAIN_ONE : GAIN_ONE + 1]
    gain_two = small_t[GAIN_TWO : GAIN_TWO + 1]
    for i in range(seq // BLK):
        rows = slice(i * BLK, (i + 1) * BLK)
        x = tok_ref[rows, :].astype(f32)
        scale = lax.rsqrt(jnp.mean(x * x, axis=-1, keepdims=True) + norm_eps)
        n2_out[rows, :] = (x * scale * gain_one).astype(bf16)
    low_c()
    bias_tiles(sz, small_t, vector, tiles)
    length = len_ref[0]
    mask[...] = jnp.broadcast_to(jnp.where(iota((seq, 1), 0) < length, 0.0, NEG), (seq, BLK))
    high_c()
    from_sibling(chunk_rest)
    pass_on(0)

    def assemble(low, high):
        for place in range(sz.group):
            for h in range(2):
                source = xor(me, sz.relative(h, place))
                cols = slice(h * half, (h + 1) * half)
                if sz.rows % 16 == 0:
                    for m in range(low, high):
                        whole[m, row_block(source, sz.rows), cols] = pieces[
                            h, place, m * sz.rows : (m + 1) * sz.rows, :
                        ]
                else:
                    tall = pieces[h, place, :, :].astype(f32)
                    for m in range(low, high):
                        wide[m, row_block8(source, sz.rows), cols] = tall[
                            m * sz.rows : (m + 1) * sz.rows
                        ]
        if sz.rows % 16 != 0:
            for m in range(low, high):
                whole[m] = wide[m].astype(bf16)

    assemble(0, 3)
    keep_copy(2, whole.at[pl.ds(0, 3)], w_out.at[pl.ds(0, 3)]).start()
    for m in range(3):
        qkv[m] = dot_nn(n2_out[...], whole[m]).astype(bf16)
    keep_copy(3, qkv, qkv_out).start()
    normed_t[...] = n2_out[...].T
    keep_copy(1, normed_t, normed_out).start()

    low = iota((1, BLK), 1) < width // sz.heads
    halves = [jnp.where(low, 1.0, 0.0).astype(bf16), jnp.where(low, 0.0, 1.0).astype(bf16)]
    size = width // sz.heads

    def copy_p(pair, i):
        part = (pair, pl.ds(0, (i + 1) * BLK), pl.ds(2 * i * BLK, 2 * BLK))
        return pltpu.make_async_copy(probs.at[part], probs_out.at[part], send_p.at[pair, i])

    def attend(pair, carry):
        cols = row_block(pair, BLK)
        query = qkv[0, :, cols] * jnp.asarray(score_scale, bf16)
        key = qkv[1, :, cols]
        value_t = qkv[2, :, cols].T
        for i in range(seq // BLK):
            rows = slice(i * BLK, (i + 1) * BLK)
            keys = (i + 1) * BLK
            both = jnp.concatenate([query[rows] * halves[0], query[rows] * halves[1]], axis=0)
            scores = dot_nt(key[:keys], both)
            tile = tiles[pair]
            if i == 0:
                scores = scores + tile[BLK:]
            elif i == 1:
                scores = scores + tile
            else:
                scores = jnp.concatenate(
                    [scores[: keys - 2 * BLK], scores[keys - 2 * BLK :] + tile], axis=0
                )
            hidden = mask[:keys, :]
            scores = scores + jnp.concatenate([hidden, hidden], axis=1)
            raised = jnp.exp(scores - jnp.max(scores, axis=0, keepdims=True))
            soft = raised * (1.0 / jnp.sum(raised, axis=0, keepdims=True))
            soft = soft.astype(bf16)
            probs[pair, :keys, 2 * i * BLK : 2 * (i + 1) * BLK] = soft
            mixed = dot_nn(value_t[:, :keys], soft)
            mixed = jnp.concatenate([mixed[:size, :BLK], mixed[size:, BLK:]], axis=0)
            att[rows, cols] = mixed.T.astype(bf16)
        for i in range(seq // BLK):
            copy_p(pair, i).start()
        return carry

    lax.fori_loop(0, sz.pairs, attend, 0)
    keep_copy(4, att, att_out).start()
    assemble(3, 4)
    keep_copy(5, whole.at[pl.ds(3, 1)], w_out.at[pl.ds(3, 1)]).start()

    router = small.astype(bf16)
    for i in range(seq // BLK):
        rows = slice(i * BLK, (i + 1) * BLK)
        resid = tok_ref[rows, :].astype(f32) + dot_nn(att[rows, :], whole[3])
        resid_all[rows, :] = resid
        scale = lax.rsqrt(jnp.mean(resid * resid, axis=-1, keepdims=True) + norm_eps)
        normed = (resid * scale * gain_two).astype(bf16)
        n2_out[rows, :] = normed
        logits = dot_nn(normed, router)
        lane = iota((1, BLK), 1)
        logit = [
            jnp.sum(jnp.where(lane == route[rows, c : c + 1], logits, 0.0), axis=-1, keepdims=True)
            for c in range(2)
        ]
        share_one = 1.0 / (1.0 + jnp.exp(logit[1] - logit[0]))
        share_two = 1.0 / (1.0 + jnp.exp(logit[0] - logit[1]))
        gate_out[rows, :] = jnp.where(
            lane == 0, share_one, jnp.where(lane == 1, share_two, 0.0)
        )
    keep_copy(6, resid_all, resid_out).start()

    keep_copy(7, n2_out, n2_hbm).start()
    cs_out[...] = jnp.zeros_like(cs_out)
    normed = n2_out[...]
    combine_one = gate_out[:, 0:1]
    combine_two = gate_out[:, 1:2]
    per = 256 // sz.cap
    for j in range(sz.slots // 256):
        lane = wide_lane + j * 256
        pick = pick_all[:, j * 256 : (j + 1) * 256]
        rows_out[j * 256 : (j + 1) * 256, :] = dot_tn(pick, normed).astype(bf16)
        weight = jnp.where(first == lane, combine_one, jnp.where(second == lane, combine_two, 0.0))
        weight = jnp.sum(weight, axis=0, keepdims=True)
        for e in range(per):
            cs_out[j * per + e, 0:1, 0 : sz.cap] = weight[:, e * sz.cap : (e + 1) * sz.cap]

    keep_copy(8, rows_out, rows_hbm).start()

    for z in range(1, line // 2):
        pass_on(z)
    for z in range(line // 2, line):
        copy_far(z).wait_recv()
        keep_far(z).start()
    for z in range(line):
        if z > 0:
            copy_far(z).wait_send()
        if z < line // 2:
            own_rows(z).wait()
            for k in range(1, 4):
                copy_plane(z, k).wait()
        else:
            keep_far(z).wait()
    finish(0)

    def wait_p(pair, carry):
        for i in range(seq // BLK):
            copy_p(pair, i).wait()
        return carry

    lax.fori_loop(0, sz.pairs, wait_p, 0)
    keep_copy(0, pick_all, pick_out).wait()
    keep_copy(2, whole.at[pl.ds(0, 3)], w_out.at[pl.ds(0, 3)]).wait()
    keep_copy(3, qkv, qkv_out).wait()
    keep_copy(7, n2_out, n2_hbm).wait()
    keep_copy(8, rows_out, rows_hbm).wait()
    keep_copy(1, normed_t, normed_out).wait()
    keep_copy(4, att, att_out).wait()
    keep_copy(5, whole.at[pl.ds(3, 1)], w_out.at[pl.ds(3, 1)]).wait()
    keep_copy(6, resid_all, resid_out).wait()


def vmem():
    return pl.BlockSpec(memory_space=pltpu.VMEM)


def anywhere():
    return pl.BlockSpec(memory_space=pl.ANY)


def forward_call(sz, lengths, tokens, routes, slots, parameters, weights, cotangent):
    seq, width, group = sz.seq, sz.width, sz.group
    shape = jax.ShapeDtypeStruct
    dma = pltpu.SemaphoreType.DMA
    wide = (4, width, width) if sz.rows % 16 else (4, 8, BLK)
    parts = len(sz.chunks)
    return pl.pallas_call(
        functools.partial(forward_kernel, sz),
        out_shape=[
            shape((4, width, width), bf16),
            shape((3, seq, width), bf16),
            shape((sz.pairs, seq, 2 * seq), bf16),
            shape((seq, width), bf16),
            shape((seq, width), f32),
            shape((sz.slots // 2, width), bf16),
            shape((sz.line // 2, 4 * sz.cap, width), bf16),
            shape((width, seq), bf16),
            shape((seq, sz.slots), bf16),
            shape((seq, width), bf16),
            shape((sz.slots, width), bf16),
            shape((sz.experts, 8, BLK), f32),
            shape((seq, BLK), f32),
            shape((group, sz.small, BLK), bf16),
        ],
        in_specs=[pl.BlockSpec(memory_space=pltpu.SMEM)] + [vmem()] * 12,
        out_specs=[anywhere()] * 11 + [vmem()] * 3,
        scratch_shapes=[
            pltpu.VMEM((2, group, sz.piece, sz.half), bf16),
            pltpu.VMEM((sz.slots, width), bf16),
            pltpu.VMEM((sz.line, 4 * sz.cap, width), bf16),
            pltpu.VMEM((16, 3 * BLK), f32),
            pltpu.VMEM((sz.pairs, 2 * BLK, 2 * BLK), f32),
            pltpu.VMEM((sz.pairs, seq, 2 * seq), bf16),
            pltpu.VMEM(wide, f32),
            pltpu.VMEM((4, width, width), bf16),
            pltpu.VMEM((3, seq, width), bf16),
            pltpu.VMEM((seq, width), bf16),
            pltpu.VMEM((seq, width), f32),
            pltpu.VMEM((seq, sz.slots), bf16),
            pltpu.VMEM((seq, BLK), f32),
            dma((parts, 2, sz.line)),
            dma((parts, sz.line)),
            dma((parts, sz.line)),
            dma((parts, sz.line)),
            dma((parts, 2 * sz.line)),
            dma((parts, 2 * sz.line)),
            dma((parts, group)),
            dma((parts, group)),
            dma((group,)),
            dma((group,)),
            dma((group,)),
            dma((group,)),
            dma((sz.pairs, seq // BLK)),
            dma((9,)),
            dma((sz.line,)),
            pltpu.VMEM((sz.small, BLK), bf16),
            pltpu.VMEM((BLK, BLK), f32),
            pltpu.VMEM((sz.small, BLK), f32),
            pltpu.VMEM((width, seq), bf16),
            pltpu.VMEM((seq, width), bf16),
            pltpu.VMEM((sz.slots, width), bf16),
        ],
        compiler_params=pltpu.CompilerParams(
            collective_id=0, has_side_effects=True, vmem_limit_bytes=VMEM_LIMIT
        ),
    )(lengths, tokens, routes, slots, *parameters, *weights, cotangent)


def gelu_parts(v):
    density = jnp.exp2(v * v * -0.7213475204444817 - 1.3257480647361593)
    base = 1.0 + 0.23164189 * jnp.abs(v)
    t = pl.reciprocal(base, approx=True)
    t = t * (2.0 - base * t)
    poly = t * (
        0.3193815351 + t * (-0.3565637813 + t * (1.7814779373 + t * (-1.8212559795 + t * 1.3302744289)))
    )
    tail = poly * density
    below = jnp.where(v < 0.0, tail, 1.0 - tail)
    return v * below, below + v * density


def column_of(row):
    return jnp.broadcast_to(row, (BLK, BLK)).T


def expert_kernel(
    sz,
    cs_ref,
    rows_ref,
    grads_hbm,
    far_hbm,
    win_ref,
    wout_ref,
    dots_out,
    relay_out,
    near_out,
    back_out,
    grad_in_out,
    grad_out_out,
    win,
    wout,
    arrived,
    scales,
    arrived_t,
    scaled,
    scaled_t,
    hidden,
    pre_grad,
    back_send,
    dots_send,
    sums,
    others,
    totals,
    grads_ref,
    results_ref,
    load,
    send_r,
    recv_r,
    send_c,
    recv_c,
    send_b,
    recv_b,
    send_d,
    recv_d,
    send_n,
    recv_n,
    send_w,
    recv_w,
    keep_w,
    keep_r,
    far_own,
    send_f,
    recv_f,
    send_p,
    recv_p,
):
    rep, me, core, sibling = peers(sz)
    group, cap, width = sz.group, sz.cap, sz.width
    greet(sz, rep, me, sibling)
    loads = [
        pltpu.make_async_copy(win_ref.at[0], win, load.at[0]),
        pltpu.make_async_copy(wout_ref.at[0], wout, load.at[1]),
        pltpu.make_async_copy(grads_hbm, grads_ref.at[pl.ds(0, sz.slots // 2)], load.at[2]),
        pltpu.make_async_copy(
            rows_ref.at[row_block(me, cap)], arrived.at[pl.ds(0, cap)], load.at[3]
        ),
    ]
    for copy in loads:
        copy.start()
    low_bits = lax.rem(me, 4)
    later = [
        pltpu.make_async_copy(
            far_hbm.at[n, row_block(low_bits, cap)],
            grads_ref.at[pl.ds((sz.slots // 2) + 4 * n * cap, cap)],
            far_own.at[n],
        )
        for n in range(sz.line // 2)
    ]
    for copy in later:
        copy.start()
    met(sz)

    def copy_f(n, k):
        return remote(
            far_hbm.at[n, row_block(xor(low_bits, k), cap)],
            grads_ref.at[pl.ds((sz.slots // 2) + (4 * n + k) * cap, cap)],
            send_f.at[n, k],
            recv_f.at[n, k],
            (rep, xor(me, k)),
        )

    def copy_r(k):
        to = xor(me, k)
        return remote(
            rows_ref.at[row_block(to, cap)], arrived.at[row_block(k, cap)],
            send_r.at[k], recv_r.at[k], (rep, to),
        )

    def copy_c(k):
        to = xor(me, k)
        return remote(cs_ref.at[to], scales.at[k], send_c.at[k], recv_c.at[k], (rep, to))

    def copy_b(k):
        return remote(
            back_send.at[row_block(k, cap)], back_out.at[row_block(me, cap)],
            send_b.at[k], recv_b.at[k], (rep, xor(me, k)),
        )

    def copy_n(k):
        return remote(
            results_ref.at[row_block(k, cap)], near_out.at[row_block(me, cap)],
            send_n.at[k], recv_n.at[k], (rep, xor(me, k)),
        )

    def copy_d(k):
        return remote(
            dots_send.at[k], dots_out.at[me], send_d.at[k], recv_d.at[k], (rep, xor(me, k))
        )

    def start_r(k, carry):
        copy_c(k).start()
        copy_r(k).start()
        return carry

    per = 256 // cap
    groups = sz.slots // 256
    early = list(range(groups // 2, groups - 1)) + list(range(0, groups // 2))
    for g in early:
        lax.fori_loop(max(g * per, 1), (g + 1) * per, start_r, 0)
    for n in range(sz.line // 2):
        for k in range(1, 4):
            copy_f(n, k).start()
    scales[0] = cs_ref[me]
    dots_send[...] = jnp.zeros_like(dots_send)
    for copy in loads:
        copy.wait()

    step = 1024

    def copy_p(j):
        return remote(
            results_ref.at[row_block(group // 2 + j, cap)],
            relay_out.at[lax.div(j, 4), row_block(low_bits, cap)],
            send_p.at[j], recv_p.at[j], (rep, xor(me, lax.rem(j, 4))),
        )

    def own_p(n):
        return pltpu.make_async_copy(
            results_ref.at[pl.ds((group // 2 + 4 * n) * cap, cap)],
            relay_out.at[n, row_block(low_bits, cap)],
            keep_r.at[n],
        )

    def rows_of(g):
        start = g * per

        def arrive(k, carry):
            copy_c(k).wait_recv()
            copy_r(k).wait_recv()
            return carry

        lax.fori_loop(max(start, 1), start + per, arrive, 0)
        for n in range(sz.line // 2):
            if (sz.slots // 2 + 4 * n * cap) // 256 == g:
                later[n].wait()
                for k in range(1, 4):
                    copy_f(n, k).wait_recv()
        span = slice(g * 256, (g + 1) * 256)
        x = arrived[span, :]
        arrived_t[:, span] = x.T
        columns = [column_of(scales[start + i, 0:1, :])[:cap, 0:1] for i in range(per)]
        column = jnp.concatenate(columns, axis=0)
        raw = grads_ref[span, :].astype(f32)
        scaled[span, :] = (raw * column).astype(bf16)
        scaled_t[:, span] = scaled[span, :].T

        def part(j, carry):
            cols = row_block(j, step)
            pre = dot_nn(arrived[span, :], win[:, cols])
            grad_hidden = dot_nn(scaled[span, :], wout[:, cols])
            act, slope = gelu_parts(pre)
            hidden[span, cols] = act.astype(bf16)
            pre_grad[span, cols] = (grad_hidden * slope).astype(bf16)
            return carry

        lax.fori_loop(0, sz.ff // step, part, 0)
        back_send[span, :] = dot_nt(pre_grad[span, :], win[...]).astype(bf16)

        def send_back(k, carry):
            copy_b(k).start()
            return carry

        lax.fori_loop(max(start, 1), start + per, send_back, 0)
        results = dot_nt(hidden[span, :], wout[...])
        results_ref[span, :] = (results * column).astype(bf16)
        if g < groups // 2:

            def send_near(k, carry):
                copy_n(k).start()
                return carry

            lax.fori_loop(max(start, 1), start + per, send_near, 0)
        else:
            for j in range(start - group // 2, start - group // 2 + per):
                if j % 4:
                    copy_p(j).start()
                else:
                    own_p(j // 4).start()
        dots = jnp.sum(results * raw, axis=-1, keepdims=True)
        for i in range(per):
            tall = jnp.broadcast_to(dots[i * cap : (i + 1) * cap], (cap, BLK))
            if cap < BLK:
                tall = jnp.concatenate([tall, jnp.zeros((BLK - cap, BLK), f32)], axis=0)
            dots_send[start + i, 0:1, :] = tall.T[0:1, :]

        def send_dots(k, carry):
            copy_d(k).start()
            return carry

        lax.fori_loop(max(start, 1), start + per, send_dots, 0)

    def start_last():
        def sent(k, carry):
            copy_r(k).wait_send()
            return carry

        for g in early:
            lax.fori_loop(max(g * per, 1), (g + 1) * per, sent, 0)
        lax.fori_loop((groups - 1) * per, groups * per, start_r, 0)

    for g in range(groups):
        if g == 1:
            start_last()
        rows_of(g)
    own_back = pltpu.make_async_copy(
        back_send.at[pl.ds(0, cap)], back_out.at[row_block(me, cap)], load.at[4]
    )
    own_back.start()
    own_near = pltpu.make_async_copy(
        results_ref.at[pl.ds(0, cap)], near_out.at[row_block(me, cap)], load.at[5]
    )
    own_near.start()
    dots_out[me] = dots_send[0]

    size = sz.ff // sz.reps
    cut = 512 if size > 512 else size
    subs = size // cut
    pieces = sz.reps // 2 * subs

    def columns_of(parity, i):
        return pl.ds(pl.multiple_of((2 * (i // subs) + parity) * size + (i % subs) * cut, BLK), cut)

    def copy_w(m, i):
        return remote(
            sums.at[m, i], others.at[m, i], send_w.at[m, i], recv_w.at[m, i], (sibling, me)
        )

    def copy_k(m, i):
        return pltpu.make_async_copy(
            totals.at[m, i], (grad_in_out, grad_out_out)[m].at[:, pl.ds(i * cut, cut)], keep_w.at[m, i]
        )

    for i in range(pieces):
        cols = columns_of(1 - core, i)
        sums[0, i] = dot_nn(arrived_t[...], pre_grad[:, cols]).astype(bf16)
        copy_w(0, i).start()
        sums[1, i] = dot_nn(scaled_t[...], hidden[:, cols]).astype(bf16)
        copy_w(1, i).start()
    for i in range(pieces):
        cols = columns_of(core, i)
        for m, left, right in ((0, arrived_t, pre_grad), (1, scaled_t, hidden)):
            total = dot_nn(left[...], right[:, cols])
            copy_w(m, i).wait_recv()
            totals[m, i] = (total + others[m, i].astype(f32)).astype(bf16)
            copy_k(m, i).start()

    def finish(k, carry):
        copy_c(k).wait_send()
        copy_b(k).wait_send()
        copy_d(k).wait_send()
        from_back = remote(
            back_send.at[row_block(k, cap)], back_out.at[row_block(xor(me, k), cap)],
            send_b.at[k], recv_b.at[k], (rep, xor(me, k)),
        )
        from_back.wait_recv()
        from_dots = remote(
            dots_send.at[k], dots_out.at[xor(me, k)], send_d.at[k], recv_d.at[k], (rep, xor(me, k))
        )
        from_dots.wait_recv()
        return carry

    lax.fori_loop(1, group, finish, 0)

    def sent_last(k, carry):
        copy_r(k).wait_send()
        return carry

    lax.fori_loop((groups - 1) * per, groups * per, sent_last, 0)

    def end_near(k, carry):
        copy_n(k).wait()
        return carry

    lax.fori_loop(1, group // 2, end_near, 0)
    for n in range(sz.line // 2):
        for k in range(1, 4):
            copy_f(n, k).wait_send()
    for j in range(group // 2):
        if j % 4:
            copy_p(j).wait()
        else:
            own_p(j // 4).wait()
    own_back.wait()
    own_near.wait()
    for i in range(pieces):
        for m in range(2):
            copy_w(m, i).wait_send()
            copy_k(m, i).wait()


def expert_call(sz, rows, scales, grads, far, weight_in, weight_out):
    group, width, ff, slots = sz.group, sz.width, sz.ff, sz.slots
    shape = jax.ShapeDtypeStruct
    dma = pltpu.SemaphoreType.DMA
    size = ff // sz.reps
    cut = 512 if size > 512 else size
    pieces = sz.reps // 2 * (size // cut)
    return pl.pallas_call(
        functools.partial(expert_kernel, sz),
        out_shape=[
            shape((sz.experts, 8, BLK), f32),
            shape((sz.line // 2, 4 * sz.cap, width), bf16),
            shape((slots, width), bf16),
            shape((slots, width), bf16),
            shape((width, ff // 2), bf16),
            shape((width, ff // 2), bf16),
        ],
        in_specs=[vmem()] + [anywhere()] * 5,
        out_specs=[vmem()] + [anywhere()] * 5,
        scratch_shapes=[
            pltpu.VMEM((width, ff), bf16),
            pltpu.VMEM((width, ff), bf16),
            pltpu.VMEM((slots, width), bf16),
            pltpu.VMEM((group, 8, BLK), f32),
            pltpu.VMEM((width, slots), bf16),
            pltpu.VMEM((slots, width), bf16),
            pltpu.VMEM((width, slots), bf16),
            pltpu.VMEM((slots, ff), bf16),
            pltpu.VMEM((slots, ff), bf16),
            pltpu.VMEM((slots, width), bf16),
            pltpu.VMEM((group, 8, BLK), f32),
            pltpu.VMEM((2, pieces, width, cut), bf16),
            pltpu.VMEM((2, pieces, width, cut), bf16),
            pltpu.VMEM((2, pieces, width, cut), bf16),
            pltpu.VMEM((slots, width), bf16),
            pltpu.VMEM((slots, width), bf16),
            dma((6,)),
        ]
        + [dma((group,))] * 10
        + [dma((2, pieces))] * 3
        + [dma((sz.line // 2,)), dma((sz.line // 2,)), dma((sz.line // 2, 4)), dma((sz.line // 2, 4))]
        + [dma((group // 2,))] * 2,
        compiler_params=pltpu.CompilerParams(
            collective_id=1, has_side_effects=True, vmem_limit_bytes=VMEM_LIMIT
        ),
    )(scales, rows, grads, far, weight_in, weight_out)


def near_onehot(sz):
    lane = iota((1, 3 * BLK), 1)
    distance = jnp.where(lane <= BLK, BLK + lane, lane - 2 * BLK)
    bucket = jnp.where(distance < 16, distance, 16)
    for cutoff in cutoffs:
        bucket = bucket + (distance >= cutoff).astype(jnp.int32)
    per = sz.buckets // sz.group
    shape = (sz.group, sz.rows, 3 * BLK)
    inner = iota(shape, 1)
    named = jnp.where(inner < per, iota(shape, 0) * per + inner, -1)
    return (named == bucket[None]).astype(f32).reshape(sz.width, 3 * BLK).astype(bf16)


def unit_shapes(sz):
    up = lambda n: -(-n // 16) * 16
    return [(up(sz.rows), sz.half)] + [(up(3 * sz.rows), BLK)] * (sz.half // BLK)


def backward_kernel(
    sz,
    len_ref,
    tok_ref,
    cot_ref,
    routes_ref,
    slots_ref,
    n2_ref,
    gate_ref,
    small_ref,
    dots_ref,
    w_hbm,
    qkv_hbm,
    probs_hbm,
    att_hbm,
    resid_hbm,
    pick_hbm,
    results_hbm,
    near_hbm,
    normed_hbm,
    back_hbm,
    out_hbm,
    gtok_hbm,
    gq_ref,
    gk_ref,
    gv_ref,
    go_ref,
    gsmall_ref,
    *scratch,
):
    units = unit_shapes(sz)
    (
        probs, w_ref, qkv_ref, att_ref, resid_ref, pick_ref, back_ref, returned, total_bf, gres, gatt,
        dqkv, dscore, stacks, normed_t, near_sum, far_sum, sums, wide, packed, packed_rows,
        packed_far, small_mine, small_from, small_final,
        load, load_p, send_r, recv_r, send_x, recv_x, send_m, recv_m,
            out_ref, gtok_ref,
    ) = scratch[:35]
    buffers = scratch[35:]
    mine = buffers[0::6]
    theirs = buffers[1::6]
    from_sib = buffers[2::6]
    from_one = buffers[3::6]
    from_two = buffers[4::6]
    final = buffers[5::6]
    rep, me, core, sibling = peers(sz)
    seq, width, half, line, group = sz.seq, sz.width, sz.half, sz.line, sz.group
    near = jnp.where(core == 0, 1, 2)
    last = jnp.where(core == 0, 2, 1)
    cap = sz.cap
    blocks = seq // BLK

    def fetch(n, src, dst):
        return pltpu.make_async_copy(src, dst, load.at[n])

    same_half = row_block(lax.div(me, group // 2), sz.slots // 2)
    loads = [
        fetch(0, back_hbm, back_ref),
        fetch(1, pick_hbm, pick_ref),
        fetch(2, resid_hbm, resid_ref),
        fetch(3, w_hbm.at[3], w_ref.at[3]),
        fetch(4, att_hbm, att_ref),
        fetch(5, qkv_hbm, qkv_ref),
        fetch(6, w_hbm.at[pl.ds(0, 3)], w_ref.at[pl.ds(0, 3)]),
        fetch(7, near_hbm.at[same_half], returned.at[same_half]),
        fetch(8, normed_hbm, normed_t),
    ]

    def copy_p(pair, i):
        part = (pair, pl.ds(0, (i + 1) * BLK), pl.ds(2 * i * BLK, 2 * BLK))
        return pltpu.make_async_copy(probs_hbm.at[part], probs.at[part], load_p.at[pair, i])

    def start_p(pair, carry):
        for i in range(blocks):
            copy_p(pair, i).start()
        return carry

    greet(sz, rep, me, sibling)
    for copy in loads[:6]:
        copy.start()
    lax.fori_loop(0, sz.pairs, start_p, 0)
    for copy in loads[6:]:
        copy.start()

    far_planes = range(line // 2, line)
    place_a = lax.div(me, 4)

    def copy_r(z):
        return remote(
            results_hbm.at[z - line // 2], returned.at[row_block(place_a, 4 * cap)],
            send_r.at[z], recv_r.at[z], (rep, xor(me, 4 * z)),
        )

    met(sz)
    for z in far_planes:
        copy_r(z).start()

    far_stages = [4, 5] if line == 4 else list(range(4, 3 + line))

    def copy_x(u, stage):
        if stage == 0:
            src, dst, to = theirs[u], from_sib[u], (sibling, me)
        elif stage == 1:
            src, dst, to = mine[u].at[pl.ds(group // 2, group // 2)], from_one[u], (rep, xor(me, last))
        elif stage == 2:
            src, dst, to = mine[u].at[pl.ds(line, line)], from_two[u].at[pl.ds(0, line)], (rep, xor(me, near))
        elif stage == 3:
            src, dst, to = final[u].at[core], final[u].at[core], (sibling, me)
        elif line == 4:
            if stage == 4:
                src, dst = mine[u].at[pl.ds(1, 2)], from_two[u].at[pl.ds(line, 2)]
                to = (rep, xor(me, 4))
            else:
                src, dst, to = mine[u].at[3], from_two[u].at[line + 2], (rep, xor(me, 12))
        else:
            z = stage - 3
            src, dst, to = mine[u].at[z], from_two[u].at[line + z], (rep, xor(me, 4 * z))
        return remote(src, dst, send_x.at[u, stage], recv_x.at[u, stage], to)

    def add_into(ref, start, stop, other, skip=0):
        def add(p, carry):
            ref[p] = (ref[p].astype(f32) + other[p + skip].astype(f32)).astype(bf16)
            return carry

        lax.fori_loop(start, stop, add, 0)

    def step(u, number):
        if number == 0:
            copy_x(u, 0).start()
        elif number == 1:
            copy_x(u, 0).wait_recv()
            add_into(mine[u], group // 2, group, from_sib[u])
            copy_x(u, 1).start()
            add_into(mine[u], 0, group // 2, from_sib[u])
        elif number == 2:
            copy_x(u, 1).wait_recv()
            add_into(mine[u], line, 2 * line, from_one[u])
            copy_x(u, 2).start()
            add_into(mine[u], 0, line, from_one[u])
        elif number == 3:
            copy_x(u, 2).wait_recv()
            add_into(mine[u], 0, line, from_two[u])
            for stage in far_stages[:1] if line == 4 else far_stages:
                copy_x(u, stage).start()
        elif number == 3.5:
            if line == 4:
                copy_x(u, 4).wait_recv()
                across = mine[u][3].astype(f32) + from_two[u][line + 1].astype(f32)
                mine[u][3] = across.astype(bf16)
                copy_x(u, 5).start()
        elif number == 4:
            total = mine[u][0].astype(f32)
            if line == 4:
                copy_x(u, 5).wait_recv()
                total = total + from_two[u][line].astype(f32) + from_two[u][line + 2].astype(f32)
            else:
                for z in range(1, line):
                    copy_x(u, 3 + z).wait_recv()
                    total = total + from_two[u][line + z].astype(f32)
            final[u][core] = total
            copy_x(u, 3).start()
        else:
            remote(
                final[u].at[1 - core], final[u].at[1 - core], send_x.at[u, 3], recv_x.at[u, 3],
                (sibling, me),
            ).wait_recv()
            for stage in list(range(4)) + far_stages:
                copy_x(u, stage).wait_send()

    def owner_of(p, swap):
        one, two = (last, near) if swap else (near, last)
        rel = lax.rem(p, line) * 4 + lax.rem(lax.div(p, line), 2) * one + lax.div(p, 2 * line) * two
        return xor(me, rel)

    def fill(u, read):
        def put(p, carry):
            mine[u][p] = read(core, owner_of(p, False)).astype(bf16)
            theirs[u][p] = read(1 - core, owner_of(p, True)).astype(bf16)
            return carry

        lax.fori_loop(0, group, put, 0)

    def padded(value, u):
        short = units[u][0] - value.shape[0]
        if short:
            value = jnp.concatenate([value, jnp.zeros((short, value.shape[1]), f32)], axis=0)
        return value

    small = small_ref[...].astype(f32)[:, : sz.rows].reshape(width, BLK)
    small_t = small.T
    gain_one = small_t[GAIN_ONE : GAIN_ONE + 1]
    gain_two = small_t[GAIN_TWO : GAIN_TWO + 1]
    router = small.astype(bf16)
    length = len_ref[0]

    places = jnp.concatenate(
        [routes_ref[...], slots_ref[...], jnp.zeros((4, seq), jnp.int32)], axis=0
    )
    places = places.astype(f32).T.astype(jnp.int32)
    route = places[:, 0:2]
    target = target_slots(sz, route, places[:, 2:4])
    first, second = target[:, 0:1], target[:, 1:2]
    dot_one = jnp.zeros((seq, BLK), f32)
    dot_two = jnp.zeros((seq, BLK), f32)
    lanes = iota((1, BLK), 1)
    per = BLK // cap
    for j in range(sz.slots // BLK):
        row = jnp.concatenate([dots_ref[j * per + e, 0:1, 0:cap] for e in range(per)], axis=1)
        lane = lanes + j * BLK
        dot_one = dot_one + jnp.where(first == lane, row, 0.0)
        dot_two = dot_two + jnp.where(second == lane, row, 0.0)
    dot_one = jnp.sum(dot_one, axis=-1, keepdims=True)
    dot_two = jnp.sum(dot_two, axis=-1, keepdims=True)
    share = gate_ref[:, 0:1] * gate_ref[:, 1:2] * (dot_one - dot_two)
    grad_logits = share * (
        (lanes == route[:, 0:1]).astype(f32) - (lanes == route[:, 1:2]).astype(f32)
    )
    grad_logits = grad_logits.astype(bf16)
    packed[...] = dot_tn(n2_ref[...], grad_logits)

    for copy in loads[:3]:
        copy.wait()
    gain_two_grad = jnp.zeros((1, width), f32)
    for i in range(blocks):
        rows = slice(i * BLK, (i + 1) * BLK)
        grad = dot_nn(pick_ref[rows, :], back_ref[...]) + dot_nt(grad_logits[rows], router)
        resid = resid_ref[rows, :]
        scale = lax.rsqrt(jnp.mean(resid * resid, axis=-1, keepdims=True) + norm_eps)
        gain_two_grad = gain_two_grad + jnp.sum(grad * resid * scale, axis=0, keepdims=True)
        valid = (iota((BLK, 1), 0) + i * BLK < length).astype(f32)
        grad_out = cot_ref[rows, :].astype(f32) * valid
        moved = grad * gain_two
        mean = jnp.mean(moved * resid, axis=-1, keepdims=True)
        total = grad_out + scale * moved - resid * (scale * scale * scale * mean)
        gres[rows, :] = total
        total_bf[rows, :] = total.astype(bf16)
    loads[3].wait()
    loads[4].wait()
    gatt[...] = dot_nt(total_bf[...], w_ref[3]).astype(bf16)
    wide[...] = dot_tn(att_ref[...], total_bf[...])

    def read_o(h, s):
        cols = pl.ds(pl.multiple_of(h * half, BLK), half)
        return padded(wide[row_block8(s, sz.rows), cols], 0)

    fill(0, read_o)
    step(0, 0)

    loads[8].wait()
    step(0, 1)

    low = iota((1, BLK), 1) < width // sz.heads
    halves = [jnp.where(low, 1.0, 0.0).astype(bf16), jnp.where(low, 0.0, 1.0).astype(bf16)]

    size = width // sz.heads
    loads[5].wait()

    def back_pair(pair):
        cols = row_block(pair, BLK)
        query = qkv_ref[0, :, cols]
        key = qkv_ref[1, :, cols]
        key_t = key.T
        value = qkv_ref[2, :, cols]
        grads = gatt[:, cols]
        for i in range(blocks):
            copy_p(pair, i).wait()
        for i in range(blocks):
            rows = slice(i * BLK, (i + 1) * BLK)
            keys = (i + 1) * BLK
            at = slice(2 * i * BLK, 2 * (i + 1) * BLK)
            both = jnp.concatenate([grads[rows] * halves[0], grads[rows] * halves[1]], axis=0)
            stacks[0, at, :] = jnp.concatenate(
                [query[rows] * halves[0], query[rows] * halves[1]], axis=0
            )
            stacks[1, at, :] = both
            soft = probs[pair, :keys, at].astype(f32)
            product = soft * dot_nt(value[:keys], both)
            grad_score = product - soft * jnp.sum(product, axis=0, keepdims=True)
            if i == 0:
                near_sum[pair, :BLK] = jnp.zeros((BLK, 2 * BLK), f32)
                near_sum[pair, BLK:] = grad_score
                far_sum[pair] = jnp.zeros((8, 2 * BLK), f32)
            else:
                near_sum[pair] += grad_score[keys - 2 * BLK :]
                if i >= 2:
                    far = grad_score[: keys - 2 * BLK].reshape((keys - 2 * BLK) // 8, 8, 2 * BLK)
                    far_sum[pair] += jnp.sum(far, axis=0)
            low_score = grad_score.astype(bf16)
            dscore[:keys, at] = low_score
            moved = dot_nn(key_t[:, :keys], low_score)
            moved = jnp.concatenate([moved[:size, :BLK], moved[size:, BLK:]], axis=0)
            dqkv[0, rows, cols] = (moved.T * score_scale).astype(bf16)
        for i in range(blocks):
            rows = slice(i * BLK, (i + 1) * BLK)
            below = slice(2 * i * BLK, 2 * seq)
            grad_key = dot_nn(dscore[rows, below], stacks[0, below, :])
            grad_value = dot_nn(probs[pair, rows, below], stacks[1, below, :])
            dqkv[1, rows, cols] = (grad_key * score_scale).astype(bf16)
            dqkv[2, rows, cols] = grad_value.astype(bf16)

    parts = half // BLK
    for j in range(parts):

        def one(h, carry, j=j):
            pair = h * parts + j
            back_pair(pair)
            cols = row_block(pair, BLK)
            grads = jnp.concatenate([dqkv[m, :, cols] for m in range(3)], axis=1)
            sums[h] = dot_nn(normed_t[...], grads)
            return carry

        one(0, 0)
        for u, n in PLAN_H[j]:
            step(u, n)
        one(1, 0)

        def read_j(h, s):
            rows = row_block8(s, sz.rows)
            value = sums[h, rows, :]
            return padded(
                jnp.concatenate([value[:, m * BLK : (m + 1) * BLK] for m in range(3)], axis=0), 1
            )

        fill(1 + j, read_j)
        for u, n in PLAN_J[j]:
            step(u, n)

    loads[6].wait()
    gain_one_grads = []

    def input_grad(i):
        rows = slice(i * BLK, (i + 1) * BLK)
        grad = dot_nt(dqkv[0, rows, :], w_ref[0]) + dot_nt(dqkv[1, rows, :], w_ref[1])
        grad = grad + dot_nt(dqkv[2, rows, :], w_ref[2])
        x = tok_ref[rows, :].astype(f32)
        scale = lax.rsqrt(jnp.mean(x * x, axis=-1, keepdims=True) + norm_eps)
        gain_one_grads.append(jnp.sum(grad * x * scale, axis=0, keepdims=True))
        moved = grad * gain_one
        mean = jnp.mean(moved * x, axis=-1, keepdims=True)
        gtok_ref[rows, :] = gres[rows, :] + scale * moved - x * (scale * scale * scale * mean)

    flip = (iota((2 * BLK, 2 * BLK), 0) + iota((2 * BLK, 2 * BLK), 1) == 2 * BLK - 1)
    flip = flip.astype(f32).astype(bf16)

    def bucket_sums(pair, carry):
        turned = dot_nn(flip, near_sum[pair].astype(bf16))
        far = jnp.sum(far_sum[pair], axis=0, keepdims=True)
        for b in range(2):
            tall = jnp.concatenate(
                [turned[:, b * BLK : (b + 1) * BLK], jnp.zeros((2 * BLK, 2 * BLK), f32)], axis=1
            )
            rolled = pltpu.roll(tall, BLK + 1, 1, stride=1, stride_axis=0)
            packed_rows[pl.ds(2 * pair + b, 1), :] = jnp.sum(rolled, axis=0, keepdims=True)
            packed_far[pl.ds(2 * pair + b, 1), :] = far[:, b * BLK : (b + 1) * BLK]
        return carry

    def table_grad():
        packed_rows[...] = jnp.zeros_like(packed_rows)
        packed_far[...] = jnp.zeros_like(packed_far)
        lax.fori_loop(0, sz.pairs, bucket_sums, 0)
        onehot = near_onehot(sz)
        values = packed_rows[...]
        upper = values.astype(bf16)
        lower = (values - upper.astype(f32)).astype(bf16)
        table = dot_nt(upper, onehot) + dot_nt(lower, onehot)
        far = jnp.sum(packed_far[...], axis=-1, keepdims=True)
        one_far = jnp.broadcast_to((lanes == 0).astype(f32), (8, BLK)).astype(bf16)
        farthest = dot_nt(one_far, onehot[:, :BLK])[0:1]
        return table + far * farthest

    def copy_m(k):
        return remote(
            small_mine.at[xor(me, k)], small_from.at[k], send_m.at[k], recv_m.at[k], (rep, xor(me, k))
        )

    def small_start(table):
        fetch(10, gtok_ref, gtok_hbm).start()
        gain_one_grad = gain_one_grads[0]
        for grad in gain_one_grads[1:]:
            gain_one_grad = gain_one_grad + grad
        tall = jnp.concatenate(
            [
                jnp.zeros((GAIN_ONE, width), f32),
                gain_one_grad,
                gain_two_grad,
                jnp.zeros((TABLE - GAIN_TWO - 1, width), f32),
                table,
                jnp.zeros((BLK - TABLE - 16, width), f32),
            ],
            axis=0,
        )
        whole = (packed[...] + tall.T).reshape(group, sz.rows, BLK)
        if sz.small != sz.rows:
            whole = jnp.concatenate(
                [whole, jnp.zeros((group, sz.small - sz.rows, BLK), f32)], axis=1
            )
        small_mine[...] = whole.astype(bf16)

        def start_m(k, carry):
            copy_m(k).start()
            return carry

        lax.fori_loop(1, group, start_m, 0)

    def copy_f():
        return remote(
            small_final.at[core], small_final.at[core], send_m.at[0], recv_m.at[0], (sibling, me)
        )

    def small_sum():
        small_final[core] = small_mine[me].astype(f32)

        def add(k, carry):
            copy_m(k).wait()
            small_final[core] += small_from[k].astype(f32)
            return carry

        lax.fori_loop(1, group, add, 0)
        copy_f().start()

    def small_end():
        remote(
            small_final.at[1 - core], small_final.at[1 - core], send_m.at[0], recv_m.at[0],
            (sibling, me),
        ).wait_recv()
        gsmall_ref[...] = small_final[0] + small_final[1]
        copy_f().wait_send()

    def results():
        for z in far_planes:
            remote(
                results_hbm.at[z - line // 2], returned.at[row_block(xor(place_a, z), 4 * cap)],
                send_r.at[z], recv_r.at[z], (rep, xor(me, 4 * z)),
            ).wait_recv()
        loads[7].wait()
        for i in range(blocks):
            rows = slice(i * BLK, (i + 1) * BLK)
            valid = (iota((BLK, 1), 0) + i * BLK < length).astype(f32)
            total = resid_ref[rows, :] + dot_nn(pick_ref[rows, :], returned[...])
            out_ref[rows, :] = (total * valid).astype(bf16)
        fetch(9, out_ref, out_hbm).start()

    table = None
    for act in PLAN_T:
        if act == "T":
            table = table_grad()
        elif act == "M":
            small_start(table)
        elif act == "R":
            results()
        elif act == "m":
            small_sum()
        elif act == "e":
            small_end()
        elif isinstance(act, int):
            input_grad(act)
        else:
            step(*act)
    for u in range(1, 1 + parts):
        step(u, 5)
    for h in range(2):
        cols = slice(h * half, (h + 1) * half)
        go_ref[:, cols] = final[0][h, : sz.rows]
        for j in range(parts):
            at = slice(h * half + j * BLK, h * half + (j + 1) * BLK)
            for m, ref in enumerate((gq_ref, gk_ref, gv_ref)):
                ref[:, at] = final[1 + j][h, m * sz.rows : (m + 1) * sz.rows]

    for z in far_planes:
        copy_r(z).wait_send()
    fetch(9, out_ref, out_hbm).wait()
    fetch(10, gtok_ref, gtok_hbm).wait()


def backward_call(sz, lengths, tokens, cotangent, routes, slots, saved, results, near, back, dots):
    seq, width, group, line = sz.seq, sz.width, sz.group, sz.line
    shape = jax.ShapeDtypeStruct
    dma = pltpu.SemaphoreType.DMA
    w, qkv, probs, att, resid, pick, n2, gate, small, normed = saved
    units = unit_shapes(sz)
    buffers = []
    for rows, cols in units:
        buffers += [
            pltpu.VMEM((group, rows, cols), bf16),
            pltpu.VMEM((group, rows, cols), bf16),
            pltpu.VMEM((group, rows, cols), bf16),
            pltpu.VMEM((group // 2, rows, cols), bf16),
            pltpu.VMEM((2 * line, rows, cols), bf16),
            pltpu.VMEM((2, rows, cols), f32),
        ]
    dense = shape((sz.rows, width), f32)
    return pl.pallas_call(
        functools.partial(backward_kernel, sz),
        out_shape=[
            shape((seq, width), bf16),
            shape((seq, width), f32),
            dense,
            dense,
            dense,
            dense,
            shape((sz.small, BLK), f32),
        ],
        in_specs=[pl.BlockSpec(memory_space=pltpu.SMEM)] + [vmem()] * 8 + [anywhere()] * 10,
        out_specs=[anywhere()] * 2 + [vmem()] * 5,
        scratch_shapes=[
            pltpu.VMEM((sz.pairs, seq, 2 * seq), bf16),
            pltpu.VMEM((4, width, width), bf16),
            pltpu.VMEM((3, seq, width), bf16),
            pltpu.VMEM((seq, width), bf16),
            pltpu.VMEM((seq, width), f32),
            pltpu.VMEM((seq, sz.slots), bf16),
            pltpu.VMEM((sz.slots, width), bf16),
            pltpu.VMEM((sz.slots, width), bf16),
            pltpu.VMEM((seq, width), bf16),
            pltpu.VMEM((seq, width), f32),
            pltpu.VMEM((seq, width), bf16),
            pltpu.VMEM((3, seq, width), bf16),
            pltpu.VMEM((seq, 2 * seq), bf16),
            pltpu.VMEM((2, 2 * seq, BLK), bf16),
            pltpu.VMEM((width, seq), bf16),
            pltpu.VMEM((sz.pairs, 2 * BLK, 2 * BLK), f32),
            pltpu.VMEM((sz.pairs, 8, 2 * BLK), f32),
            pltpu.VMEM((2, width, 3 * BLK), f32),
            pltpu.VMEM((width, width), f32),
            pltpu.VMEM((width, BLK), f32),
            pltpu.VMEM((16, 3 * BLK), f32),
            pltpu.VMEM((16, BLK), f32),
            pltpu.VMEM((group, sz.small, BLK), bf16),
            pltpu.VMEM((group, sz.small, BLK), bf16),
            pltpu.VMEM((2, sz.small, BLK), f32),
            dma((11,)),
            dma((sz.pairs, seq // BLK)),
            dma((group,)),
            dma((group,)),
            dma((len(units), 3 + line)),
            dma((len(units), 3 + line)),
            dma((group,)),
            dma((group,)),
            pltpu.VMEM((seq, width), bf16),
            pltpu.VMEM((seq, width), f32),
        ]
        + buffers,
        compiler_params=pltpu.CompilerParams(
            collective_id=2, has_side_effects=True, vmem_limit_bytes=VMEM_LIMIT
        ),
    )(
        lengths, tokens, cotangent, routes, slots, n2, gate, small, dots, w, qkv, probs, att, resid,
        pick, results, near, normed, back,
    )


def finish_kernel(
    sz, cuts, in_ref, out_ref, result_ref, tokens_ref, q_ref, k_ref, v_ref, o_ref, small_ref,
    to_in, to_out, to_result, to_tokens, to_q, to_k, to_v, to_o, to_one, to_two, to_router, to_table,
    *scratch,
):
    held, wide, load, store = scratch[:8], scratch[8:10], scratch[10], scratch[11]
    moves = []

    def move(n, src, dst, parts):
        size = src.shape[0] // parts
        for i in range(parts):
            at = pl.ds(i * size, size)
            moves.append((n, at, src, dst))

    move(2, result_ref, to_result, 1)
    move(3, tokens_ref, to_tokens, 2)
    for n, src, dst in ((4, q_ref, to_q), (5, k_ref, to_k), (6, v_ref, to_v), (7, o_ref, to_o)):
        move(n, src, dst, 1)
    move(0, in_ref, to_in, cuts)
    move(1, out_ref, to_out, cuts)
    ins, outs = [], []
    for i, (n, at, src, dst) in enumerate(moves):
        ins.append(pltpu.make_async_copy(src.at[at], held[n].at[at], load.at[i]))
        kept = wide[n] if n < 2 else held[n]
        outs.append(pltpu.make_async_copy(kept.at[at], dst.at[at], store.at[i]))
    for copy in ins:
        copy.start()
    small = small_ref[...]
    tall = jnp.concatenate([small, jnp.zeros((BLK - sz.small, BLK), f32)], axis=0).T
    to_router[...] = tall[: sz.experts, : sz.rows]
    to_one[...] = tall[GAIN_ONE : GAIN_ONE + 1, : sz.rows]
    to_two[...] = tall[GAIN_TWO : GAIN_TWO + 1, : sz.rows]
    to_table[...] = small[: to_table.shape[0], TABLE : TABLE + sz.heads]
    for (n, at, src, dst), came, goes in zip(moves, ins, outs):
        came.wait()
        if n < 2:
            wide[n][at, :] = held[n][at, :].astype(f32)
        goes.start()
    for copy in outs:
        copy.wait()


def finish_call(sz, grad_in, grad_out, result, tokens, dense, small):
    shape = jax.ShapeDtypeStruct
    cuts = 6
    whole = [grad_in, grad_out, result, tokens, *dense]
    kinds = [f32, f32] + [x.dtype for x in whole[2:]]
    return pl.pallas_call(
        functools.partial(finish_kernel, sz, cuts),
        out_shape=[shape(x.shape, kind) for x, kind in zip(whole, kinds)]
        + [
            shape((1, sz.rows), f32),
            shape((1, sz.rows), f32),
            shape((sz.experts, sz.rows), f32),
            shape((sz.buckets // sz.group, sz.heads), f32),
        ],
        in_specs=[anywhere()] * 8 + [vmem()],
        out_specs=[anywhere()] * 8 + [vmem()] * 4,
        scratch_shapes=[pltpu.VMEM(x.shape, x.dtype) for x in whole]
        + [pltpu.VMEM(x.shape, f32) for x in whole[:2]]
        + [pltpu.SemaphoreType.DMA((2 * cuts + 8,))] * 2,
        compiler_params=pltpu.CompilerParams(vmem_limit_bytes=VMEM_LIMIT),
    )(*whole, small)


def shards(
    tokens, lengths, routes, slots, norm_one, w_query, w_key, w_value, w_output, bias_table, norm_two,
    router, expert_in, expert_out, cotangent, *, reps, group,
):
    seq, width = tokens.shape
    rows = w_query.shape[0]
    heads = bias_table.shape[1]
    experts = router.shape[1]
    sz = Sizes(
        reps, group, seq, width, heads, experts, expert_in.shape[2], rows, bias_table.shape[0] * group
    )
    parameters = (norm_one[None], norm_two[None], router.T, bias_table)
    weights = (w_query, w_key, w_value, w_output)
    routes, slots = routes.T, slots.T
    (w, qkv, probs, att, resid, grads, far, normed, pick, n2, sent, scales, gate, small_all) = forward_call(
        sz, lengths, tokens, routes, slots, parameters, weights, cotangent
    )
    dots, results, near, back, grad_in, grad_out = expert_call(sz, sent, scales, grads, far, expert_in, expert_out)
    saved = (w, qkv, probs, att, resid, pick, n2, gate, small_all, normed)
    output, grad_tokens, gq, gk, gv, go, gsmall = backward_call(
        sz, lengths, tokens, cotangent, routes, slots, saved, results, near, back, dots
    )
    if reps > 2:
        same = [[r for r in range(reps) if r % 2 == c] for c in range(2)]
        grad_in, grad_out = (
            lax.psum_scatter(grad, "rep", scatter_dimension=1, axis_index_groups=same, tiled=True)
            for grad in (grad_in, grad_out)
        )
        gq, gk, gv, go, gsmall = lax.psum((gq, gk, gv, go, gsmall), "rep", axis_index_groups=same)
    (grad_in, grad_out, output, grad_tokens, gq, gk, gv, go, g_one, g_two, g_router, g_table) = (
        finish_call(sz, grad_in, grad_out, output, grad_tokens, (gq, gk, gv, go), gsmall)
    )
    return (
        output,
        grad_tokens,
        g_one[0],
        gq,
        gk,
        gv,
        go,
        g_table,
        g_two[0],
        g_router.T,
        grad_in[None],
        grad_out[None],
    )


def solution(mesh):
    both = ("rep", "shard")
    return jax.shard_map(
        functools.partial(shards, reps=mesh.shape["rep"], group=mesh.shape["shard"]),
        mesh=mesh,
        in_specs=(
            P(both, None),
            P(both),
            P(both, None),
            P(both, None),
            P("shard"),
            P("shard", None),
            P("shard", None),
            P("shard", None),
            P("shard", None),
            P("shard", None),
            P("shard"),
            P("shard", None),
            P("shard", None, None),
            P("shard", None, None),
            P(both, None),
        ),
        out_specs=(
            P(both, None),
            P(both, None),
            P("shard"),
            P("shard", None),
            P("shard", None),
            P("shard", None),
            P("shard", None),
            P("shard", None),
            P("shard"),
            P("shard", None),
            P("shard", None, "rep"),
            P("shard", None, "rep"),
        ),
        check_vma=False,
    )
```
